256 devices in a mesh: space: 32 (over y_hi, z, core), ens: 8 (over y_lo, x).
Axes of the slice: x: 4, y: 4 (y_hi: 2, y_lo: 2; y = y_hi * 2 + y_lo), z: 8, core: 2. Of those that a mesh axis runs over, the one named last changes fastest.
Arguments:
- initial_state: bfloat16 [768, 2304], P('space'), may hold values from -6 to 6
- starting_field_nudges: bfloat16 [8, 768, 2304], P('ens', 'space'), may hold values from -4 to 4
- verifying_analysis: bfloat16 [768, 2304], P('space'), may hold values from -6 to 6
- seam_turns: int32 [32], replicated, may hold values from 0 to 3
- w_in: bfloat16 [864, 256], replicated, may hold values from -0.21875 to 0.21875
- b_in: bfloat16 [256], replicated, may hold values from -3 to 3
- w_depth: bfloat16 [49, 256], replicated, may hold values from -0.875 to 0.875
- b_depth: bfloat16 [256], replicated, may hold values from -3 to 3
- norm_gain: bfloat16 [256], replicated, may hold values from 0.5 to 2
- norm_shift: bfloat16 [256], replicated, may hold values from -3 to 3
- w_up: bfloat16 [256, 1024], replicated, may hold values from -0.375 to 0.375
- b_up: bfloat16 [1024], replicated, may hold values from -3 to 3
- w_down: bfloat16 [1024, 256], replicated, may hold values from -0.1875 to 0.1875
- b_down: bfloat16 [256], replicated, may hold values from -3 to 3
- head_weight: bfloat16 [256, 96], replicated, may hold values from -0.375 to 0.375
- head_bias: bfloat16 [96], replicated, may hold values from -3 to 3
Outputs:
- sampled_predictions: float32 [8, 768, 2304], P('ens', 'space')
- grad_w_in: float32 [864, 256], P(None, 'space')
- grad_b_in: float32 [256], P('space')
- grad_w_depth: float32 [49, 256], P(None, 'space')
- grad_b_depth: float32 [256], P('space')
- grad_norm_gain: float32 [256], P('space')
- grad_norm_shift: float32 [256], P('space')
- grad_w_up: float32 [256, 1024], P(None, 'space')
- grad_b_up: float32 [1024], P('space')
- grad_w_down: float32 [1024, 256], P(None, 'space')
- grad_b_down: float32 [256], P('space')
- grad_w_out: float32 [256, 96], P(None, 'space')
- grad_b_out: float32 [96], P('space')
The draws below stay inside these ranges and needn't reach their ends.
Inputs may be any that keep to these rules, and one draw needn't show every extreme that they name: `seam_turns`: each seam's turn is a whole number of quarter turns.
All inputs are finite; a program needn't handle non-finite values.
Results may differ from the reference program's by a relative error of at most 0.01.
Values may be sent and summed in bfloat16 or wider, within the bound.
No kernel may reach another device: no remote copies, remote signals or barrier semaphores. Data moves between devices by JAX's collectives and lax.ppermute only.
A program may use at most 128 MiB of HBM per device.

```python
import math
import jax
import jax.numpy as jnp
from jax import lax

C = 256
CIN = 96
HID = 1024
COUT = 96
TILE = 24
TILES = 32
TCOLS = 8
MEMBERS = 8


def touch_ends(values, rng, smallest, high):
    place = [jax.random.randint(jax.random.fold_in(rng, axis), (), 0, length) for axis, length in enumerate(values.shape)]
    longest = values.shape.index(max(values.shape))
    beside = place[:longest] + [(place[longest] + 1) % values.shape[longest]] + place[longest + 1:]
    return values.at[tuple(place)].set(smallest).at[tuple(beside)].set(high)


def block_levels(rng, extent, split, low, high):
    def one(axis_at, parts):
        draws = jax.random.uniform(jax.random.fold_in(jax.random.fold_in(rng, 6), axis_at), (parts,), jnp.float32, low / len(split), high / len(split))
        return jnp.repeat(jnp.exp(draws), extent[axis_at] // parts).reshape((-1,) + (1,) * (len(extent) - axis_at - 1))

    factor_of = one(*split[0])
    for cut in split[1:]:
        factor_of = factor_of * one(*cut)
    return factor_of


def bell_draw(stream_key, dims, width, reach, cuts=(), held_as=jnp.bfloat16):
    values = width * jax.random.normal(stream_key, dims, jnp.float32)
    if cuts:
        values = values * block_levels(stream_key, dims, cuts, -0.22, 0.18)
    return jnp.clip(values, -reach, reach).astype(held_as)


def setup_inputs(seed: int = 0) -> dict:
    splits = jax.random.split(jax.random.key(seed), 17)
    return {
        "initial_state": bell_draw(splits[0], (TILES * TILE, TILE * CIN), 1.0, 6.0, ((0, 32),)),
        "starting_field_nudges": bell_draw(splits[1], (MEMBERS, TILES * TILE, TILE * CIN), 0.5, 4.0, ((0, 8), (1, 32))),
        "verifying_analysis": bell_draw(splits[2], (TILES * TILE, TILE * COUT), 1.0, 6.0, ((0, 32),)),
        "seam_turns": touch_ends(jax.random.randint(splits[3], (TILES,), 0, 4), jax.random.fold_in(splits[3], 1), 0, 3).astype(jnp.int32),
        "w_in": bell_draw(splits[4], (9 * CIN, C), (9 * CIN) ** -0.5, 0.21875),
        "b_in": bell_draw(splits[5], (C,), 0.5, 3.0),
        "w_depth": bell_draw(splits[6], (49, C), 49 ** -0.5, 0.875),
        "b_depth": bell_draw(splits[7], (C,), 0.5, 3.0),
        "norm_gain": jnp.clip(jnp.exp(jax.random.uniform(splits[8], (C,), jnp.float32, math.log(0.5), math.log(2.0))), 0.5, 2.0).astype(jnp.bfloat16),
        "norm_shift": bell_draw(splits[9], (C,), 0.5, 3.0),
        "w_up": bell_draw(splits[10], (C, HID), C ** -0.5, 0.375),
        "b_up": bell_draw(splits[11], (HID,), 0.5, 3.0),
        "w_down": bell_draw(splits[12], (HID, C), HID ** -0.5, 0.1875),
        "b_down": bell_draw(splits[13], (C,), 0.5, 3.0),
        "head_weight": bell_draw(splits[14], (C, COUT), C ** -0.5, 0.375),
        "head_bias": bell_draw(splits[15], (COUT,), 0.5, 3.0),
    }


EPS = 1e-06
CUBIC = 0.044715
ROOT = math.sqrt(2.0 / math.pi)
SOFT_SQUARE = 0.01

def rotate(tile_stack, quarter_turns):
    result = tile_stack
    for quarter in range(1, 4):
        result = jnp.where((quarter_turns == quarter)[:, None, None, None], jnp.rot90(tile_stack, quarter, axes=(1, 2)), result)
    return result

def gelu_pair(northward_shift):
    inner_arg = ROOT * (northward_shift + CUBIC * northward_shift * northward_shift * northward_shift)
    tanh_part = jnp.tanh(inner_arg)
    output = 0.5 * northward_shift * (1.0 + tanh_part)
    gelu_slope = 0.5 * (1.0 + tanh_part) + 0.5 * northward_shift * (1.0 - tanh_part * tanh_part) * ROOT * (1.0 + 3.0 * CUBIC * northward_shift * northward_shift)
    return (output, gelu_slope)

def stem(source_pad, w_in, b_in):
    height = source_pad.shape[1] - 2
    breadth = source_pad.shape[2] - 2
    pieces = [source_pad[:, row_off:row_off + height, column_start:column_start + breadth] for row_off in range(3) for column_start in range(3)]
    patch_windows = jnp.concatenate(pieces, axis=-1)
    dims_in = patch_windows.shape
    mixed = jnp.dot(patch_windows.reshape(-1, dims_in[-1]), w_in, preferred_element_type=jnp.float32) + b_in.astype(jnp.float32)
    return (patch_windows, mixed.astype(jnp.bfloat16).reshape(dims_in[:3] + (w_in.shape[1],)))

def stem_back(patch_windows, grad_stem):
    grad_low = grad_stem.astype(jnp.bfloat16)
    flat_patches = patch_windows.reshape(-1, patch_windows.shape[-1])
    grad_weight = jnp.dot(flat_patches.T, grad_low.reshape(-1, grad_low.shape[-1]), preferred_element_type=jnp.float32)
    return (grad_weight, lax.optimization_barrier(jnp.sum(grad_stem, axis=(0, 1, 2))))

def depthwise(padded, w_depth):
    height = padded.shape[1] - 6
    breadth = padded.shape[2] - 6
    running = jnp.zeros((padded.shape[0], height, breadth, padded.shape[3]), jnp.float32)
    for row_off in range(7):
        for column_start in range(7):
            window = padded[:, row_off:row_off + height, column_start:column_start + breadth].astype(jnp.float32)
            running = running + window * w_depth[row_off * 7 + column_start].astype(jnp.float32)
    return running

def depthwise_back(padded, w_depth, grad_deep):
    height = grad_deep.shape[1]
    breadth = grad_deep.shape[2]
    weight_rows = []
    input_grad = jnp.zeros(padded.shape, jnp.float32)
    for row_off in range(7):
        for column_start in range(7):
            window = padded[:, row_off:row_off + height, column_start:column_start + breadth].astype(jnp.float32)
            weight_rows.append(lax.optimization_barrier(jnp.sum(window * grad_deep, axis=(0, 1, 2))))
            spread = grad_deep * w_depth[row_off * 7 + column_start].astype(jnp.float32)
            input_grad = input_grad + jnp.pad(spread, ((0, 0), (row_off, 6 - row_off), (column_start, 6 - column_start), (0, 0)))
    return (jnp.stack(weight_rows), input_grad)

def evaluate_residual_unit(stem_result, stem_padding, model_parameters):
    w_depth, b_depth, norm_gain, norm_shift, w_up, b_up, w_down, b_down, head_weight, head_bias = model_parameters
    deep_sum = depthwise(stem_padding, w_depth) + b_depth.astype(jnp.float32)
    center = deep_sum - lax.optimization_barrier(jnp.mean(deep_sum, axis=-1, keepdims=True))
    inverse = lax.rsqrt(lax.optimization_barrier(jnp.mean(center * center, axis=-1, keepdims=True)) + EPS)
    normed = center * inverse
    scaled = (normed * norm_gain.astype(jnp.float32) + norm_shift.astype(jnp.float32)).astype(jnp.bfloat16)
    channels = stem_result.shape[-1]
    northward_shift = jnp.dot(scaled.reshape(-1, channels), w_up, preferred_element_type=jnp.float32) + b_up.astype(jnp.float32)
    active, gelu_slope = gelu_pair(northward_shift)
    active = active.astype(jnp.bfloat16)
    downward = jnp.dot(active, w_down, preferred_element_type=jnp.float32) + b_down.astype(jnp.float32)
    hidden_result = (stem_result.reshape(-1, channels).astype(jnp.float32) + downward).astype(jnp.bfloat16)
    predicted_field = jnp.dot(hidden_result, head_weight, preferred_element_type=jnp.float32) + head_bias.astype(jnp.float32)
    saved_values = (normed, inverse, scaled, gelu_slope, active, hidden_result)
    return (predicted_field, saved_values)

def block_backward(stem_padding, model_parameters, saved_values, grad_f):
    w_depth, b_depth, norm_gain, norm_shift, w_up, b_up, w_down, b_down, head_weight, head_bias = model_parameters
    normed, inverse, scaled, gelu_slope, active, hidden_result = saved_values
    channels = hidden_result.shape[-1]
    grad_f_low = grad_f.astype(jnp.bfloat16)
    grad_w_out = jnp.dot(hidden_result.T, grad_f_low, preferred_element_type=jnp.float32)
    grad_b_out = lax.optimization_barrier(jnp.sum(grad_f, axis=0))
    grad_hidden = jnp.dot(grad_f_low, head_weight.T, preferred_element_type=jnp.float32)
    hidden_low = grad_hidden.astype(jnp.bfloat16)
    grad_w_down = jnp.dot(active.T, hidden_low, preferred_element_type=jnp.float32)
    grad_b_down = lax.optimization_barrier(jnp.sum(grad_hidden, axis=0))
    grad_up = jnp.dot(hidden_low, w_down.T, preferred_element_type=jnp.float32) * gelu_slope
    up_low = grad_up.astype(jnp.bfloat16)
    grad_w_up = jnp.dot(scaled.reshape(-1, channels).T, up_low, preferred_element_type=jnp.float32)
    grad_b_up = lax.optimization_barrier(jnp.sum(grad_up, axis=0))
    grad_scaled = jnp.dot(up_low, w_up.T, preferred_element_type=jnp.float32).reshape(normed.shape)
    grad_gain = lax.optimization_barrier(jnp.sum(grad_scaled * normed, axis=(0, 1, 2)))
    grad_shift = lax.optimization_barrier(jnp.sum(grad_scaled, axis=(0, 1, 2)))
    grad_norm = grad_scaled * norm_gain.astype(jnp.float32)
    grad_deep = (grad_norm - lax.optimization_barrier(jnp.mean(grad_norm, axis=-1, keepdims=True)) - normed * lax.optimization_barrier(jnp.mean(grad_norm * normed, axis=-1, keepdims=True))) * inverse
    grad_w_depth, grad_pad = depthwise_back(stem_padding, w_depth, grad_deep)
    grad_b_depth = lax.optimization_barrier(jnp.sum(grad_deep, axis=(0, 1, 2)))
    grad_direct = grad_hidden.reshape(normed.shape)
    block_grads = (grad_w_depth, grad_b_depth, grad_gain, grad_shift, grad_w_up, grad_b_up, grad_w_down, grad_b_down, grad_w_out, grad_b_out)
    return (grad_pad, grad_direct, block_grads)

def soft_slope(values):
    return values * lax.rsqrt(values * values + SOFT_SQUARE)

def score_sensitivity(every_member, local_grid_lines, target_rows, loss_coefficient):
    member_count = every_member.shape[0]
    own_wide = local_grid_lines.astype(jnp.float32)
    pair_sum = lax.optimization_barrier(jnp.sum(soft_slope(own_wide[:, None] - every_member.astype(jnp.float32)[None]), axis=1))
    direct = soft_slope(own_wide - target_rows.astype(jnp.float32)) / member_count
    return (direct - pair_sum / (member_count * (member_count - 1))) * loss_coefficient

def cycle_pad(tile_stack, seam_turns, margin):
    west_source = jnp.roll(tile_stack, 1, axis=0)
    west_cols = rotate(west_source, seam_turns)[:, :, -margin:]
    east_source = jnp.roll(tile_stack, -1, axis=0)
    east_turns = (4 - jnp.roll(seam_turns, -1)) % 4
    east_cols = rotate(east_source, east_turns)[:, :, :margin]
    widened = jnp.concatenate([west_cols, tile_stack, east_cols], axis=2)
    north_rows = jnp.roll(widened, TCOLS, axis=0)[:, -margin:]
    south_rows = jnp.roll(widened, -TCOLS, axis=0)[:, :margin]
    return jnp.concatenate([north_rows, widened, south_rows], axis=1)

def cycle_unpad(grad_pad, seam_turns, margin):
    tile_length = grad_pad.shape[2] - 2 * margin
    top_grad = grad_pad[:, :margin]
    bottom_grad = grad_pad[:, -margin:]
    inner_rows = grad_pad[:, margin:-margin]
    inner_rows = inner_rows.at[:, -margin:].add(jnp.roll(top_grad, -TCOLS, axis=0))
    inner_rows = inner_rows.at[:, :margin].add(jnp.roll(bottom_grad, TCOLS, axis=0))
    west_grad = inner_rows[:, :, :margin]
    eastern_gradient = inner_rows[:, :, -margin:]
    middle = inner_rows[:, :, margin:-margin]
    west_back = rotate(jnp.pad(west_grad, ((0, 0), (0, 0), (tile_length - margin, 0), (0, 0))), (4 - seam_turns) % 4)
    east_back = rotate(jnp.pad(eastern_gradient, ((0, 0), (0, 0), (0, tile_length - margin), (0, 0))), jnp.roll(seam_turns, -1))
    return middle + jnp.roll(west_back, -1, axis=0) + jnp.roll(east_back, 1, axis=0)

def reference(initial_state, starting_field_nudges, verifying_analysis, seam_turns, w_in, b_in, w_depth, b_depth, norm_gain, norm_shift, w_up, b_up, w_down, b_down, head_weight, head_bias):
    tile_count = seam_turns.shape[0]
    incoming_feature_count = w_in.shape[0] // 9
    output_channels = head_weight.shape[1]
    model_parameters = (w_depth, b_depth, norm_gain, norm_shift, w_up, b_up, w_down, b_down, head_weight, head_bias)
    loss_coefficient = 1.0 / math.sqrt(tile_count * TILE * TILE * output_channels)

    def model_apply(sample_nudge):
        source = (initial_state.astype(jnp.float32) + sample_nudge.astype(jnp.float32)).astype(jnp.bfloat16)
        source = source.reshape(tile_count, TILE, TILE, incoming_feature_count)
        patch_windows, stem_result = stem(cycle_pad(source, seam_turns, 1), w_in, b_in)
        stem_padding = cycle_pad(stem_result, seam_turns, 3)
        predicted_field, saved_values = evaluate_residual_unit(stem_result, stem_padding, model_parameters)
        return (patch_windows, stem_padding, predicted_field, saved_values)

    def prediction_line_group(sample_nudge):
        return model_apply(sample_nudge)[2].reshape(tile_count * TILE, TILE * output_channels)
    sampled_predictions = lax.map(prediction_line_group, starting_field_nudges)
    sensitivity_nest = lax.map(lambda local_grid_lines: score_sensitivity(sampled_predictions, local_grid_lines[None], verifying_analysis, loss_coefficient)[0], sampled_predictions)

    def member_step(global_totals_combined, member_pair):
        sample_nudge, grad_f = member_pair
        patch_windows, stem_padding, predicted_field, saved_values = model_apply(sample_nudge)
        grad_pad, grad_direct, block_grads = block_backward(stem_padding, model_parameters, saved_values, grad_f.reshape(-1, output_channels))
        grad_stem = grad_direct + cycle_unpad(grad_pad, seam_turns, 3)
        grad_w_in, grad_b_in = stem_back(patch_windows, grad_stem)
        member_terms = (grad_w_in, grad_b_in) + block_grads
        return (jax.tree.map(lambda a, b: a + b, global_totals_combined, member_terms), None)
    zero_sums = (jnp.zeros(w_in.shape, jnp.float32), jnp.zeros(b_in.shape, jnp.float32), jnp.zeros(w_depth.shape, jnp.float32), jnp.zeros(b_depth.shape, jnp.float32), jnp.zeros(norm_gain.shape, jnp.float32), jnp.zeros(norm_shift.shape, jnp.float32), jnp.zeros(w_up.shape, jnp.float32), jnp.zeros(b_up.shape, jnp.float32), jnp.zeros(w_down.shape, jnp.float32), jnp.zeros(b_down.shape, jnp.float32), jnp.zeros(head_weight.shape, jnp.float32), jnp.zeros(head_bias.shape, jnp.float32))
    global_totals_combined, unused = lax.scan(member_step, zero_sums, (starting_field_nudges, sensitivity_nest))
    return (sampled_predictions, global_totals_combined[0], global_totals_combined[1], global_totals_combined[2], global_totals_combined[3], global_totals_combined[4], global_totals_combined[5], global_totals_combined[6], global_totals_combined[7], global_totals_combined[8], global_totals_combined[9], global_totals_combined[10], global_totals_combined[11])
```

```python
import math

import jax
import jax.numpy as jnp
from jax import lax
from jax.sharding import PartitionSpec as P

EPS = 1e-06
CUBIC = 0.044715
ROOT = math.sqrt(2.0 / math.pi)
SOFT_SQUARE = 0.01


def as_sent(value):

    def short(part):
        return part.astype(jnp.bfloat16) if part.dtype == jnp.float32 else part

    return jax.tree.map(short, value)


def shifted(value, axis, by):
    peers = lax.axis_size(axis)
    return lax.ppermute(value, axis, [(i, (i + by) % peers) for i in range(peers)])


def rotate(tile_stack, quarter_turns):
    result = tile_stack
    for quarter in range(1, 4):
        result = jnp.where(
            (quarter_turns == quarter)[:, None, None, None],
            jnp.rot90(tile_stack, quarter, axes=(1, 2)),
            result,
        )
    return result


def gelu_pair(northward_shift):
    inner_arg = ROOT * (
        northward_shift + CUBIC * northward_shift * northward_shift * northward_shift
    )
    tanh_part = jnp.tanh(inner_arg)
    output = 0.5 * northward_shift * (1.0 + tanh_part)
    gelu_slope = 0.5 * (1.0 + tanh_part) + 0.5 * northward_shift * (
        1.0 - tanh_part * tanh_part
    ) * ROOT * (1.0 + 3.0 * CUBIC * northward_shift * northward_shift)
    return (output, gelu_slope)


def stem(source_pad, w_in, b_in):
    height = source_pad.shape[1] - 2
    breadth = source_pad.shape[2] - 2
    pieces = [
        source_pad[:, row_off : row_off + height, column_start : column_start + breadth]
        for row_off in range(3)
        for column_start in range(3)
    ]
    patch_windows = jnp.concatenate(pieces, axis=-1)
    dims_in = patch_windows.shape
    mixed = jnp.dot(
        patch_windows.reshape(-1, dims_in[-1]), w_in, preferred_element_type=jnp.float32
    ) + b_in.astype(jnp.float32)
    return (patch_windows, mixed.astype(jnp.bfloat16).reshape(dims_in[:3] + (w_in.shape[1],)))


def stem_back(patch_windows, grad_stem):
    grad_low = grad_stem.astype(jnp.bfloat16)
    flat_patches = patch_windows.reshape(-1, patch_windows.shape[-1])
    grad_weight = jnp.dot(
        flat_patches.T, grad_low.reshape(-1, grad_low.shape[-1]), preferred_element_type=jnp.float32
    )
    return (grad_weight, jnp.sum(grad_stem, axis=(0, 1, 2)))


def depthwise(padded, w_depth):
    height = padded.shape[1] - 6
    breadth = padded.shape[2] - 6
    running = jnp.zeros((padded.shape[0], height, breadth, padded.shape[3]), jnp.float32)
    for row_off in range(7):
        for column_start in range(7):
            window = padded[
                :, row_off : row_off + height, column_start : column_start + breadth
            ].astype(jnp.float32)
            running = running + window * w_depth[row_off * 7 + column_start].astype(jnp.float32)
    return running


def depthwise_back(padded, w_depth, grad_deep):
    height = grad_deep.shape[1]
    breadth = grad_deep.shape[2]
    weight_rows = []
    input_grad = jnp.zeros(padded.shape, jnp.float32)
    for row_off in range(7):
        for column_start in range(7):
            window = padded[
                :, row_off : row_off + height, column_start : column_start + breadth
            ].astype(jnp.float32)
            weight_rows.append(jnp.sum(window * grad_deep, axis=(0, 1, 2)))
            spread = grad_deep * w_depth[row_off * 7 + column_start].astype(jnp.float32)
            input_grad = input_grad + jnp.pad(
                spread, ((0, 0), (row_off, 6 - row_off), (column_start, 6 - column_start), (0, 0))
            )
    return (jnp.stack(weight_rows), input_grad)


def evaluate_residual_unit(stem_result, stem_padding, model_parameters):
    w_depth, b_depth, norm_gain, norm_shift, w_up, b_up, w_down, b_down, head_weight, head_bias = (
        model_parameters
    )
    deep_sum = depthwise(stem_padding, w_depth) + b_depth.astype(jnp.float32)
    center = deep_sum - jnp.mean(deep_sum, axis=-1, keepdims=True)
    inverse = lax.rsqrt(jnp.mean(center * center, axis=-1, keepdims=True) + EPS)
    normed = center * inverse
    scaled = (normed * norm_gain.astype(jnp.float32) + norm_shift.astype(jnp.float32)).astype(
        jnp.bfloat16
    )
    channels = stem_result.shape[-1]
    northward_shift = jnp.dot(
        scaled.reshape(-1, channels), w_up, preferred_element_type=jnp.float32
    ) + b_up.astype(jnp.float32)
    active, gelu_slope = gelu_pair(northward_shift)
    active = active.astype(jnp.bfloat16)
    downward = jnp.dot(active, w_down, preferred_element_type=jnp.float32) + b_down.astype(
        jnp.float32
    )
    hidden_result = (stem_result.reshape(-1, channels).astype(jnp.float32) + downward).astype(
        jnp.bfloat16
    )
    predicted_field = jnp.dot(
        hidden_result, head_weight, preferred_element_type=jnp.float32
    ) + head_bias.astype(jnp.float32)
    saved_values = (normed, inverse, scaled, gelu_slope, active, hidden_result)
    return (predicted_field, saved_values)


def block_backward(stem_padding, model_parameters, saved_values, grad_f):
    w_depth, b_depth, norm_gain, norm_shift, w_up, b_up, w_down, b_down, head_weight, head_bias = (
        model_parameters
    )
    normed, inverse, scaled, gelu_slope, active, hidden_result = saved_values
    channels = hidden_result.shape[-1]
    grad_f_low = grad_f.astype(jnp.bfloat16)
    grad_w_out = jnp.dot(hidden_result.T, grad_f_low, preferred_element_type=jnp.float32)
    grad_b_out = jnp.sum(grad_f, axis=0)
    grad_hidden = jnp.dot(grad_f_low, head_weight.T, preferred_element_type=jnp.float32)
    hidden_low = grad_hidden.astype(jnp.bfloat16)
    grad_w_down = jnp.dot(active.T, hidden_low, preferred_element_type=jnp.float32)
    grad_b_down = jnp.sum(grad_hidden, axis=0)
    grad_up = jnp.dot(hidden_low, w_down.T, preferred_element_type=jnp.float32) * gelu_slope
    up_low = grad_up.astype(jnp.bfloat16)
    grad_w_up = jnp.dot(scaled.reshape(-1, channels).T, up_low, preferred_element_type=jnp.float32)
    grad_b_up = jnp.sum(grad_up, axis=0)
    grad_scaled = jnp.dot(up_low, w_up.T, preferred_element_type=jnp.float32).reshape(normed.shape)
    grad_gain = jnp.sum(grad_scaled * normed, axis=(0, 1, 2))
    grad_shift = jnp.sum(grad_scaled, axis=(0, 1, 2))
    grad_norm = grad_scaled * norm_gain.astype(jnp.float32)
    grad_deep = (
        grad_norm
        - jnp.mean(grad_norm, axis=-1, keepdims=True)
        - normed * jnp.mean(grad_norm * normed, axis=-1, keepdims=True)
    ) * inverse
    grad_w_depth, grad_pad = depthwise_back(stem_padding, w_depth, grad_deep)
    grad_b_depth = jnp.sum(grad_deep, axis=(0, 1, 2))
    grad_direct = grad_hidden.reshape(normed.shape)
    block_grads = (
        grad_w_depth,
        grad_b_depth,
        grad_gain,
        grad_shift,
        grad_w_up,
        grad_b_up,
        grad_w_down,
        grad_b_down,
        grad_w_out,
        grad_b_out,
    )
    return (grad_pad, grad_direct, block_grads)


def soft_slope(values):
    return values * lax.rsqrt(values * values + SOFT_SQUARE)


def score_sensitivity(every_member, local_grid_lines, target_rows, loss_coefficient):
    member_count = every_member.shape[0]
    pair_sum = jnp.sum(soft_slope(local_grid_lines[:, None] - every_member[None]), axis=1)
    direct = soft_slope(local_grid_lines - target_rows.astype(jnp.float32)) / member_count
    return (direct - pair_sum / (member_count * (member_count - 1))) * loss_coefficient


def pass_strip(strip, offset):
    return shifted(as_sent(strip), "space", offset).astype(strip.dtype)


def pass_rows(strip, offset):
    return shifted(as_sent(strip), "space", offset).astype(strip.dtype)


def pass_grad(strip, offset):
    return shifted(strip, "space", offset)


def pass_row_grad(strip, offset):
    return shifted(strip, "space", offset)


def seam_pad(tile_stack, my_turn, next_turn, margin, row_tiles):
    west_out = rotate(tile_stack, next_turn.reshape(1))[:, :, -margin:]
    came_west = pass_strip(west_out, 1)
    east_out = rotate(tile_stack, ((4 - my_turn) % 4).reshape(1))[:, :, :margin]
    arrived_from_east = pass_strip(east_out, -1)
    widened = jnp.concatenate([came_west, tile_stack, arrived_from_east], axis=2)
    came_north = pass_rows(widened[:, -margin:], row_tiles)
    came_south = pass_rows(widened[:, :margin], -row_tiles)
    return jnp.concatenate([came_north, widened, came_south], axis=1)


def seam_unpad(grad_pad, my_turn, next_turn, margin, row_tiles):
    tile_length = grad_pad.shape[2] - 2 * margin
    top_grad = grad_pad[:, :margin]
    bottom_grad = grad_pad[:, -margin:]
    inner_rows = grad_pad[:, margin:-margin]
    from_south = pass_row_grad(top_grad, -row_tiles)
    from_north = pass_row_grad(bottom_grad, row_tiles)
    inner_rows = inner_rows.at[:, -margin:].add(from_south)
    inner_rows = inner_rows.at[:, :margin].add(from_north)
    west_grad = inner_rows[:, :, :margin]
    eastern_gradient = inner_rows[:, :, -margin:]
    middle = inner_rows[:, :, margin:-margin]
    arriving_eastside = pass_grad(west_grad, -1)
    from_west = pass_grad(eastern_gradient, 1)
    placed_east = jnp.pad(arriving_eastside, ((0, 0), (0, 0), (tile_length - margin, 0), (0, 0)))
    placed_west = jnp.pad(from_west, ((0, 0), (0, 0), (0, tile_length - margin), (0, 0)))
    return (
        middle
        + rotate(placed_east, ((4 - next_turn) % 4).reshape(1))
        + rotate(placed_west, my_turn.reshape(1))
    )


def reduce_gradients(gradients):
    spaces = lax.axis_size("space")
    members = lax.axis_size("ens")
    shapes = [g.shape for g in gradients]
    flat = [g.T.reshape(spaces, -1) for g in gradients]
    sizes = [f.shape[1] for f in flat]
    packed = jnp.concatenate(flat, axis=1)
    unit = members * 128
    width = -(-packed.shape[1] // unit) * unit
    packed = jnp.pad(packed, ((0, 0), (0, width - packed.shape[1]))).astype(jnp.bfloat16)
    parts = packed.reshape(spaces, members, width // members).transpose(1, 0, 2)
    over_members = lax.all_to_all(parts, "ens", 0, 0, tiled=True)
    partial = jnp.sum(over_members.astype(jnp.float32), axis=0)
    over_tiles = lax.all_to_all(partial, "space", 0, 0, tiled=True)
    mine = jnp.sum(over_tiles, axis=0)
    whole = lax.all_to_all(
        jnp.broadcast_to(mine, (members, width // members)), "ens", 0, 0, tiled=True
    ).reshape(-1)
    shares = []
    start = 0
    for shape, size in zip(shapes, sizes):
        share = whole[start : start + size].reshape(shape[1] // spaces, shape[0]).T
        shares.append(share)
        start += size
    return shares


def body(
    initial_state,
    starting_field_nudges,
    verifying_analysis,
    seam_turns,
    w_in,
    b_in,
    w_depth,
    b_depth,
    norm_gain,
    norm_shift,
    w_up,
    b_up,
    w_down,
    b_down,
    head_weight,
    head_bias,
):
    spaces = lax.axis_size("space")
    row_tiles = spaces // 4
    tile_index = lax.axis_index("space")
    my_turn = lax.dynamic_index_in_dim(seam_turns, tile_index, keepdims=False)
    next_turn = lax.dynamic_index_in_dim(seam_turns, (tile_index + 1) % spaces, keepdims=False)
    tile_length = initial_state.shape[0]
    incoming_feature_count = w_in.shape[0] // 9
    output_channels = head_weight.shape[1]
    model_parameters = (
        w_depth,
        b_depth,
        norm_gain,
        norm_shift,
        w_up,
        b_up,
        w_down,
        b_down,
        head_weight,
        head_bias,
    )
    source = (
        initial_state.astype(jnp.float32) + starting_field_nudges[0].astype(jnp.float32)
    ).astype(jnp.bfloat16)
    source = source.reshape(1, tile_length, tile_length, incoming_feature_count)
    patch_windows, stem_result = stem(
        seam_pad(source, my_turn, next_turn, 1, row_tiles), w_in, b_in
    )
    stem_padding = seam_pad(stem_result, my_turn, next_turn, 3, row_tiles)
    predicted_field, saved_values = evaluate_residual_unit(
        stem_result, stem_padding, model_parameters
    )
    predicted_rows = predicted_field.reshape(1, tile_length, tile_length * output_channels)
    loss_coefficient = 1.0 / math.sqrt(spaces * tile_length * tile_length * output_channels)
    members = lax.axis_size("ens")
    every_member = lax.all_to_all(
        jnp.broadcast_to(predicted_rows, (members,) + predicted_rows.shape[1:]), "ens", 0, 0, tiled=True
    )
    gradient_rows = score_sensitivity(
        every_member, predicted_rows, verifying_analysis, loss_coefficient
    )
    grad_f = gradient_rows.reshape(-1, output_channels)
    grad_pad, grad_direct, block_grads = block_backward(
        stem_padding, model_parameters, saved_values, grad_f
    )
    grad_stem = grad_direct + seam_unpad(grad_pad, my_turn, next_turn, 3, row_tiles)
    grad_w_in, grad_b_in = stem_back(patch_windows, grad_stem)
    (
        grad_w_depth,
        grad_b_depth,
        grad_gain,
        grad_shift,
        grad_w_up,
        grad_b_up,
        grad_w_down,
        grad_b_down,
        grad_w_out,
        grad_b_out,
    ) = block_grads
    gradients = (
        grad_w_in,
        grad_b_in[None],
        grad_w_depth,
        grad_b_depth[None],
        grad_gain[None],
        grad_shift[None],
        grad_w_up,
        grad_b_up[None],
        grad_w_down,
        grad_b_down[None],
        grad_w_out,
        grad_b_out[None],
    )
    shares = reduce_gradients(gradients)
    return (
        predicted_rows,
        shares[0],
        shares[1][0],
        shares[2],
        shares[3][0],
        shares[4][0],
        shares[5][0],
        shares[6],
        shares[7][0],
        shares[8],
        shares[9][0],
        shares[10],
        shares[11][0],
    )


def solution(mesh):
    return jax.shard_map(
        body,
        mesh=mesh,
        in_specs=(
            P("space", None),
            P("ens", "space", None),
            P("space", None),
            P(),
            P(),
            P(),
            P(),
            P(),
            P(),
            P(),
            P(),
            P(),
            P(),
            P(),
            P(),
            P(),
        ),
        out_specs=(
            P("ens", "space", None),
            P(None, "space"),
            P("space"),
            P(None, "space"),
            P("space"),
            P("space"),
            P("space"),
            P(None, "space"),
            P("space"),
            P(None, "space"),
            P("space"),
            P(None, "space"),
            P("space"),
        ),
        check_vma=False,
    )
```

```python
import functools
import math

import jax
import jax.numpy as jnp
from jax import lax
from jax.experimental import pallas as pl
from jax.experimental.pallas import tpu as pltpu
from jax.sharding import PartitionSpec as P

EPS = 1e-06
CUBIC = 0.044715
ROOT = math.sqrt(2.0 / math.pi)
SOFT_SQUARE = 0.01
F32 = jnp.float32
BF16 = jnp.bfloat16
SIDE = 24
CELLS = SIDE * SIDE
LANE = 128
SMALL = 64
VMEM_BYTES = 56 * 1024 * 1024


def dot(left, right, left_dim=1, right_dim=0):
    return lax.dot_general(
        left, right, (((left_dim,), (right_dim,)), ((), ())), preferred_element_type=F32
    )


def soft_slope(values):
    return values * lax.rsqrt(values * values + SOFT_SQUARE)


def turned_offset(quarter, row_off, col_off):
    return (
        (row_off, col_off),
        (2 - col_off, row_off),
        (2 - row_off, 2 - col_off),
        (col_off, 2 - row_off),
    )[quarter]


def gather_patches(turns_ref, wide_ref, stage_ref, patches_ref):
    bands = ((0, 0, 3), (3, 5, SIDE), (27, 31, 3))
    turn_of = {(1, 0): 0, (1, 2): 1, (0, 0): 2, (0, 2): 3, (2, 0): 4, (2, 2): 5}
    stage_ref[...] = jnp.zeros_like(stage_ref)
    for row_off in range(3):
        for col_off in range(3):
            for row_band, (row_to, row_from, row_len) in enumerate(bands):
                for col_band, (col_to, col_from, col_len) in enumerate(bands):

                    def read(quarter):
                        row, col = turned_offset(quarter, row_off, col_off)
                        return wide_ref[
                            row_from + row : row_from + row + row_len,
                            col_from + col : col_from + col + col_len,
                            :,
                        ]

                    piece = read(0)
                    if (row_band, col_band) in turn_of:
                        turn = turns_ref[turn_of[row_band, col_band]]
                        for quarter in range(1, 4):
                            piece = jnp.where(turn == quarter, read(quarter), piece)
                    stage_ref[row_to : row_to + row_len, col_to : col_to + col_len, :] = piece
            at = (3 * row_off + col_off) * LANE
            patches_ref[:, at : at + LANE] = stage_ref[...].reshape(960, LANE).astype(BF16)


def forward_kernel(
    turns_ref,
    source_ref,
    w_in_ref,
    b_in_ref,
    w_depth_ref,
    b_depth_ref,
    gain_ref,
    shift_ref,
    w_up_ref,
    b_up_ref,
    w_down_ref,
    b_down_ref,
    head_ref,
    head_bias_ref,
    patches_ref,
    stem_ref,
    normed_ref,
    inverse_ref,
    scaled_ref,
    slope_ref,
    active_ref,
    hidden_ref,
    field_ref,
    tight_ref,
    sent_ref,
    wide_ref,
    stage_ref,
):
    wide_ref[...] = source_ref[...].astype(F32)
    gather_patches(turns_ref, wide_ref, stage_ref, patches_ref)
    for part in range(5):
        rows = slice(part * 192, (part + 1) * 192)
        stem = dot(patches_ref[rows, :], w_in_ref[...]) + b_in_ref[...]
        stem = stem.astype(BF16).astype(F32)
        for half in range(2):
            stem_ref[half, part * 6 : (part + 1) * 6] = stem[
                :, half * LANE : (half + 1) * LANE
            ].reshape(6, 32, LANE)

    def normalise(block, carry):
        row = block * 4
        halves = []
        for half in range(2):
            lanes = slice(half * LANE, (half + 1) * LANE)
            total = jnp.zeros((4, SIDE, LANE), F32)
            for col_off in range(7):
                slab = stem_ref[half, pl.ds(row, 10), col_off : col_off + SIDE, :]
                for row_off in range(7):
                    tap = 7 * row_off + col_off
                    total = total + slab[row_off : row_off + 4] * w_depth_ref[tap : tap + 1, lanes][None]
            halves.append(total.reshape(4 * SIDE, LANE) + b_depth_ref[:, lanes])
        mean = (
            jnp.sum(halves[0], axis=-1, keepdims=True) + jnp.sum(halves[1], axis=-1, keepdims=True)
        ) / 256.0
        centers = [h - mean for h in halves]
        spread = (
            jnp.sum(centers[0] * centers[0], axis=-1, keepdims=True)
            + jnp.sum(centers[1] * centers[1], axis=-1, keepdims=True)
        ) / 256.0
        inverse = lax.rsqrt(spread + EPS)
        at = pl.ds(pl.multiple_of(block * 96, 96), 96)
        inverse_ref[at, :] = jnp.broadcast_to(inverse, (96, LANE))
        for half in range(2):
            lanes = slice(half * LANE, (half + 1) * LANE)
            normed = centers[half] * inverse
            normed_ref[at, lanes] = normed
            scaled_ref[at, lanes] = (normed * gain_ref[:, lanes] + shift_ref[:, lanes]).astype(BF16)
        return carry

    lax.fori_loop(0, 6, normalise, 0)

    def mix(part, carry):
        at = pl.ds(pl.multiple_of(part * 96, 96), 96)
        upward = dot(scaled_ref[at, :], w_up_ref[...]) + b_up_ref[...]
        square = upward * upward
        tanh_part = jnp.tanh(ROOT * (upward + CUBIC * square * upward))
        plus = 0.5 * (1.0 + tanh_part)
        slope_ref[at, :] = plus + 0.5 * upward * (1.0 - tanh_part * tanh_part) * (
            ROOT + (3.0 * CUBIC * ROOT) * square
        )
        active = (upward * plus).astype(BF16)
        active_ref[at, :] = active
        own = [
            stem_ref[half, pl.ds(3 + 4 * part, 4), 3 : 3 + SIDE, :].reshape(96, LANE)
            for half in range(2)
        ]
        own = jnp.concatenate(own, axis=1)
        hidden = (own + dot(active, w_down_ref[...]) + b_down_ref[...]).astype(BF16)
        hidden_ref[at, :] = hidden
        field_ref[at, :] = dot(hidden, head_ref[...]) + head_bias_ref[...]
        return carry

    lax.fori_loop(0, 6, mix, 0)
    for quarter in range(4):
        tight_ref[:, 96 * quarter : 96 * (quarter + 1)] = field_ref[
            144 * quarter : 144 * (quarter + 1), 0:96
        ]
    sent = tight_ref[...].astype(BF16)
    for member in range(sent_ref.shape[0]):
        sent_ref[member] = sent


def mixer_backward_kernel(
    coefficient,
    every_ref,
    own_ref,
    target_ref,
    hidden_ref,
    head_ref,
    pick_ref,
    active_ref,
    slope_ref,
    scaled_ref,
    w_down_ref,
    w_up_ref,
    early_ref,
    out_part_ref,
    hidden_grad_ref,
    scaled_grad_ref,
    small_ref,
    tight_ref,
    field_ref,
    low_ref,
    up_low_ref,
    up_sum_ref,
    down_ref,
):
    members = every_ref.shape[0]
    own = own_ref[...]
    own_sent = own.astype(BF16).astype(F32)
    pair_sum = soft_slope(own_sent - every_ref[0].astype(F32))
    for member in range(1, members):
        pair_sum = pair_sum + soft_slope(own_sent - every_ref[member].astype(F32))
    direct = soft_slope(own - target_ref[...].astype(F32))
    tight_ref[...] = (
        direct * (coefficient / members) - pair_sum * (coefficient / (members * (members - 1)))
    )
    field_ref[...] = jnp.zeros_like(field_ref)
    for quarter in range(4):
        field_ref[144 * quarter : 144 * (quarter + 1), 0:96] = tight_ref[
            :, 96 * quarter : 96 * (quarter + 1)
        ]
    grad_f = field_ref[...]
    grad_b_out = jnp.sum(grad_f, axis=0, keepdims=True)
    grad_f_low = grad_f.astype(BF16)
    picked = dot(grad_f_low, pick_ref[...]).astype(BF16)
    out_part_ref[...] = dot(picked, hidden_ref[...], 0, 0).astype(BF16)
    grad_hidden = dot(grad_f_low, head_ref[...], 1, 1)
    hidden_grad_ref[...] = grad_hidden
    low_ref[...] = grad_hidden.astype(BF16)
    grad_b_down = jnp.sum(grad_hidden, axis=0, keepdims=True)
    down_ref[...] = dot(low_ref[...], active_ref[...], 0, 0)
    up_sum_ref[...] = jnp.zeros_like(up_sum_ref)

    def widen(part, carry):
        at = pl.ds(pl.multiple_of(part * 96, 96), 96)
        grad_up = dot(low_ref[at, :], w_down_ref[...], 1, 1) * slope_ref[at, :]
        up_sum_ref[...] += jnp.sum(grad_up.reshape(12, 8, 1024), axis=0)
        up_low = grad_up.astype(BF16)
        up_low_ref[at, :] = up_low
        scaled_grad_ref[at, :] = dot(up_low, w_up_ref[...], 1, 1)
        return carry

    lax.fori_loop(0, 6, widen, 0)
    for chunk in range(4):
        up = dot(up_low_ref[:, chunk * 256 : (chunk + 1) * 256], scaled_ref[...], 0, 0)
        up = up.reshape(8, 4, 8, 256)
        for row_tile in range(4):
            for lane_tile in range(2):
                part = 2 * row_tile + lane_tile
                upper = down_ref[
                    chunk * 64 : (chunk + 1) * 64, part * LANE : (part + 1) * LANE
                ].reshape(8, 8, LANE)
                lower = up[:, row_tile, :, lane_tile * LANE : (lane_tile + 1) * LANE]
                early_ref[part, chunk * 8 : (chunk + 1) * 8] = jnp.concatenate(
                    [upper, lower], axis=1
                ).astype(BF16)
    up_sum = jnp.sum(up_sum_ref[...], axis=0, keepdims=True)
    unit = lax.broadcasted_iota(jnp.int32, (8, 1024), 1)
    row = lax.broadcasted_iota(jnp.int32, (8, 1024), 0)
    spread = jnp.where((unit & 3) == row, jnp.broadcast_to(up_sum, (8, 1024)), 0.0)
    fold = (
        lax.broadcasted_iota(jnp.int32, (1024, 256), 0) >> 2
        == lax.broadcasted_iota(jnp.int32, (1024, 256), 1)
    ).astype(F32).astype(BF16)
    column = lax.broadcasted_iota(jnp.int32, (LANE, 256), 1)
    place = (
        (lax.broadcasted_iota(jnp.int32, (LANE, 256), 0) == 3 * (column >> 3) + (column & 7))
        & ((column & 7) < 3)
    ).astype(F32).astype(BF16)
    b_out = jnp.broadcast_to(grad_b_out, (8, LANE))

    def two_part(values, matrix):
        high = values.astype(BF16)
        rest = (values - high.astype(F32)).astype(BF16)
        return dot(high, matrix) + dot(rest, matrix)

    small_ref[...] = jnp.zeros_like(small_ref)
    small_ref[0:1, :] = grad_b_down
    small_ref[1:5, :] = two_part(spread, fold)[0:4]
    small_ref[5:6, :] = two_part(b_out, place)[0:1]


def depth_backward_kernel(
    scaled_grad_ref,
    normed_ref,
    inverse_ref,
    gain_ref,
    hidden_grad_ref,
    stem_ref,
    w_depth_ref,
    patches_ref,
    order_ref,
    early_small_ref,
    out_part_ref,
    late_ref,
    deep_ref,
    stem_grad_ref,
    small_ref,
    sums_ref,
    low_ref,
    tight_ref,
):
    deep_ref[...] = jnp.zeros_like(deep_ref)
    small_ref[...] = jnp.zeros_like(small_ref)
    sums_ref[...] = jnp.zeros_like(sums_ref)

    def unnormalise(block, carry):
        at = pl.ds(pl.multiple_of(block * 96, 96), 96)
        halves = []
        first = jnp.zeros((96, 1), F32)
        second = jnp.zeros((96, 1), F32)
        for half in range(2):
            lanes = slice(half * LANE, (half + 1) * LANE)
            grad = scaled_grad_ref[at, lanes]
            normed = normed_ref[at, lanes]
            sums_ref[0, :, lanes] += jnp.sum((grad * normed).reshape(12, 8, LANE), axis=0)
            sums_ref[1, :, lanes] += jnp.sum(grad.reshape(12, 8, LANE), axis=0)
            grad = grad * gain_ref[:, lanes]
            first = first + jnp.sum(grad, axis=-1, keepdims=True)
            second = second + jnp.sum(grad * normed, axis=-1, keepdims=True)
            halves.append((grad, normed))
        first = first / 256.0
        second = second / 256.0
        inverse = inverse_ref[at, :]
        for half, (grad, normed) in enumerate(halves):
            lanes = slice(half * LANE, (half + 1) * LANE)
            deep = (grad - first - normed * second) * inverse
            sums_ref[2, :, lanes] += jnp.sum(deep.reshape(12, 8, LANE), axis=0)
            deep_ref[half, pl.ds(6 + block * 4, 4), 8 : 8 + SIDE, :] = deep.reshape(4, SIDE, LANE)
        return carry

    lax.fori_loop(0, 6, unnormalise, 0)
    for half in range(2):
        lanes = slice(half * LANE, (half + 1) * LANE)

        def spread(block, carry):
            row = block * 3
            total = jnp.zeros((3, 32, LANE), F32)
            for col_off in range(7):
                slab = deep_ref[half, pl.ds(row, 9), 8 - col_off : 40 - col_off, :]
                for row_off in range(7):
                    tap = 7 * row_off + col_off
                    total = total + slab[6 - row_off : 9 - row_off] * w_depth_ref[tap : tap + 1, lanes][None]
            stem_grad_ref[half, pl.ds(row, 3)] = total
            return carry

        lax.fori_loop(0, 10, spread, 0)
        for col_off in range(7):

            def weigh(block, totals):
                row = block * 4
                deep = deep_ref[half, pl.ds(6 + row, 4), 8 : 8 + SIDE, :]
                slab = stem_ref[half, pl.ds(row, 10), col_off : col_off + SIDE, :]
                return tuple(
                    totals[row_off]
                    + jnp.sum((slab[row_off : row_off + 4] * deep).reshape(12, 8, LANE), axis=0)
                    for row_off in range(7)
                )

            totals = lax.fori_loop(0, 6, weigh, tuple(jnp.zeros((8, LANE), F32) for _ in range(7)))
            for row_off in range(7):
                tap = 7 * row_off + col_off
                small_ref[tap : tap + 1, lanes] = jnp.sum(totals[row_off], axis=0, keepdims=True)

        def add_direct(block, carry):
            at = pl.ds(pl.multiple_of(block * 96, 96), 96)
            stem_grad_ref[half, pl.ds(3 + block * 4, 4), 3 : 3 + SIDE, :] += hidden_grad_ref[
                at, lanes
            ].reshape(4, SIDE, LANE)
            return carry

        lax.fori_loop(0, 6, add_direct, 0)
        grad_stem = stem_grad_ref[half].reshape(960, LANE)
        small_ref[52:53, lanes] = jnp.sum(grad_stem, axis=0, keepdims=True)
        low_ref[:, lanes] = grad_stem.astype(BF16)
    small_ref[49:50, :] = jnp.sum(sums_ref[2], axis=0, keepdims=True)
    small_ref[50:51, :] = jnp.sum(sums_ref[0], axis=0, keepdims=True)
    small_ref[51:52, :] = jnp.sum(sums_ref[1], axis=0, keepdims=True)
    small_ref[53:59, :] = early_small_ref[0:6, :]
    order = order_ref[...]
    ordered = dot(low_ref[...], order).astype(BF16)
    wide = dot(ordered, patches_ref[...], 0, 0)
    tight_ref[...] = jnp.zeros_like(tight_ref)
    for offset in range(9):
        tight_ref[:, 96 * offset : 96 * (offset + 1)] = wide[:, LANE * offset : LANE * offset + 96]
    late_ref[:, 0:896] = tight_ref[...].astype(BF16)
    small = small_ref[...]
    high = small.astype(BF16)
    rest = (small - high.astype(F32)).astype(BF16)
    both = jnp.concatenate([high, rest], axis=0)
    late_ref[:, 896:1024] = dot(order, both, 0, 1).astype(BF16)
    late_ref[:, 1024:1280] = out_part_ref[...]


def call(kernel, shapes, scratch, *operands, smem=0, flops=0):
    space = [pl.BlockSpec(memory_space=pltpu.SMEM)] * smem
    space += [pl.BlockSpec(memory_space=pltpu.VMEM)] * (len(operands) - smem)
    return pl.pallas_call(
        kernel,
        out_shape=[jax.ShapeDtypeStruct(s, d) for s, d in shapes],
        in_specs=space,
        out_specs=[pl.BlockSpec(memory_space=pltpu.VMEM)] * len(shapes),
        scratch_shapes=[pltpu.VMEM(s, d) for s, d in scratch],
        compiler_params=pltpu.CompilerParams(vmem_limit_bytes=VMEM_BYTES),
        cost_estimate=pl.CostEstimate(flops=flops, bytes_accessed=8_000_000, transcendentals=0),
    )(*operands)


def row_of(values):
    return values.astype(F32).reshape(1, -1)


def run_forward(turns, wide_source, weights, members):
    w_in, b_in, w_depth, b_depth, gain, shift, w_up, b_up, w_down, b_down, head, head_bias = weights
    w_in_wide = jnp.pad(w_in.reshape(9, 96, 256), ((0, 0), (0, 32), (0, 0))).reshape(1152, 256)
    source = jnp.pad(wide_source, ((0, 0), (0, 4), (0, 32)))
    head_wide = jnp.pad(head, ((0, 0), (0, 32)))
    bias_wide = jnp.pad(row_of(head_bias), ((0, 0), (0, 32)))
    w_depth_wide = jnp.pad(w_depth.astype(F32), ((0, 7), (0, 0)))
    outs = call(
        forward_kernel,
        [
            ((960, 1152), BF16),
            ((2, 30, 32, LANE), F32),
            ((CELLS, 256), F32),
            ((CELLS, LANE), F32),
            ((CELLS, 256), BF16),
            ((CELLS, 1024), F32),
            ((CELLS, 1024), BF16),
            ((CELLS, 256), BF16),
            ((CELLS, LANE), F32),
            ((144, 384), F32),
            ((members, 144, 384), BF16),
        ],
        [((36, 40, LANE), F32), ((30, 32, LANE), F32)],
        turns,
        source,
        w_in_wide,
        row_of(b_in),
        w_depth_wide,
        row_of(b_depth),
        row_of(gain),
        row_of(shift),
        w_up,
        row_of(b_up),
        w_down,
        row_of(b_down),
        head_wide,
        bias_wide,
        smem=1,
        flops=2_000_000_000,
    )
    return outs, head_wide, w_depth_wide


def run_mixer_backward(every, tight, target, saved, head_wide, w_down, w_up, coefficient):
    hidden, active, slope, scaled = saved
    column = jnp.arange(256)
    owner = 3 * (column % 32) + column // 32
    pick = ((jnp.arange(LANE)[:, None] == owner[None, :]) & (column[None, :] < 96)).astype(BF16)
    return call(
        functools.partial(mixer_backward_kernel, coefficient),
        [
            ((8, 32, 16, LANE), BF16),
            ((256, 256), BF16),
            ((CELLS, 256), F32),
            ((CELLS, 256), F32),
            ((8, 256), F32),
        ],
        [
            ((144, 384), F32),
            ((CELLS, LANE), F32),
            ((CELLS, 256), BF16),
            ((CELLS, 1024), BF16),
            ((8, 1024), F32),
            ((256, 1024), F32),
        ],
        every,
        tight,
        target,
        hidden,
        head_wide,
        pick,
        active,
        slope,
        scaled,
        w_down,
        w_up,
        flops=3_000_000_000,
    )


def run_depth_backward(
    scaled_grad, normed, inverse, gain, hidden_grad, stem, w_depth_wide, patches, early_small, out_part
):
    column = jnp.arange(256)
    order = (column[:, None] == (8 * (column % 32) + column // 32)[None, :]).astype(BF16)
    return call(
        depth_backward_kernel,
        [((256, 1280), BF16)],
        [
            ((2, 36, 40, LANE), F32),
            ((2, 30, 32, LANE), F32),
            ((SMALL, 256), F32),
            ((3, 8, 256), F32),
            ((960, 256), BF16),
            ((256, 896), F32),
        ],
        scaled_grad,
        normed,
        inverse,
        row_of(gain),
        hidden_grad,
        stem,
        w_depth_wide,
        patches,
        order,
        early_small,
        out_part,
        flops=3_000_000_000,
    )[0]


def shifted(value, axis, by):
    peers = lax.axis_size(axis)
    return lax.ppermute(value, axis, [(i, (i + by) % peers) for i in range(peers)])


def turned_edge(tile, turns, width, east):
    size = tile.shape[0]

    def columns(x):
        return x[:, size - width :] if east else x[:, :width]

    sides = (
        columns(tile),
        columns(jnp.rot90(tile, 1)),
        columns(jnp.rot90(tile, 2)),
        columns(jnp.rot90(tile, 3)),
    )
    result = sides[0]
    for quarter in range(1, 4):
        result = jnp.where(turns == quarter, sides[quarter], result)
    return result


def seam_pad(tile, my_turn, next_turn, margin, row_tiles):
    came_west = shifted(turned_edge(tile, next_turn, margin, True), "space", 1)
    came_east = shifted(turned_edge(tile, (4 - my_turn) % 4, margin, False), "space", -1)
    widened = jnp.concatenate([came_west, tile, came_east], axis=1)
    came_north = shifted(widened[-margin:], "space", row_tiles)
    came_south = shifted(widened[:margin], "space", -row_tiles)
    return jnp.concatenate([came_north, widened, came_south], axis=0)


def swap(value, axis):
    return lax.all_to_all(value, axis, 0, 0, tiled=True)


def body(
    initial_state,
    starting_field_nudges,
    verifying_analysis,
    seam_turns,
    w_in,
    b_in,
    w_depth,
    b_depth,
    norm_gain,
    norm_shift,
    w_up,
    b_up,
    w_down,
    b_down,
    head_weight,
    head_bias,
):
    spaces = lax.axis_size("space")
    members = lax.axis_size("ens")
    row_tiles = spaces // 4
    tile_index = lax.axis_index("space")

    def turn_at(offset):
        return lax.dynamic_index_in_dim(seam_turns, (tile_index + offset) % spaces, keepdims=False)

    my_turn = turn_at(0)
    next_turn = turn_at(1)
    turns = jnp.stack(
        [
            my_turn,
            (4 - next_turn) % 4,
            turn_at(spaces - row_tiles),
            (4 - turn_at(spaces - row_tiles + 1)) % 4,
            turn_at(row_tiles),
            (4 - turn_at(row_tiles + 1)) % 4,
        ]
    )
    source = (
        initial_state.astype(F32) + starting_field_nudges[0].astype(F32)
    ).astype(BF16).reshape(SIDE, SIDE, 96)
    near = seam_pad(source, my_turn, next_turn, 1, row_tiles)
    wide_source = seam_pad(near, my_turn, next_turn, 5, row_tiles)
    weights = (
        w_in, b_in, w_depth, b_depth, norm_gain, norm_shift, w_up, b_up, w_down, b_down, head_weight, head_bias
    )
    saved, head_wide, w_depth_wide = run_forward(turns, wide_source, weights, members)
    patches, stem, normed, inverse, scaled, slope, active, hidden, field, tight, sent = saved
    every = swap(sent, "ens")
    predicted = field[:, :96].reshape(1, SIDE, SIDE * 96)
    target = verifying_analysis.reshape(4, 144, 96).transpose(1, 0, 2).reshape(144, 384)
    coefficient = 1.0 / math.sqrt(spaces * CELLS * 96)
    early, out_part, hidden_grad, scaled_grad, early_small = run_mixer_backward(
        every, tight, target, (hidden, active, slope, scaled), head_wide, w_down, w_up, coefficient
    )
    early_sum = jnp.sum(swap(early, "ens").astype(F32), axis=0).astype(BF16)
    late = run_depth_backward(
        scaled_grad, normed, inverse, norm_gain, hidden_grad, stem, w_depth_wide, patches, early_small, out_part
    )
    late_sum = jnp.sum(swap(late.reshape(8, 32, 1280), "ens").astype(F32), axis=0)
    early_mine = jnp.sum(swap(early_sum, "space").astype(F32), axis=0)
    late_mine = jnp.sum(swap(late_sum, "space"), axis=0)
    mine = jnp.concatenate([early_mine.reshape(2048), late_mine])
    whole = swap(jnp.broadcast_to(mine, (members, 3328)), "ens")
    early_whole = whole[:, :2048].reshape(8, 16, LANE)
    late_whole = whole[:, 2048:]
    small = late_whole[:, 896:960] + late_whole[:, 960:1024]
    return (
        predicted,
        late_whole[:, :864].T,
        small[:, 52],
        small[:, :49].T,
        small[:, 49],
        small[:, 50],
        small[:, 51],
        early_whole[:, 8:].reshape(4, 2, 8, LANE).transpose(1, 3, 0, 2).reshape(256, 32),
        small[:, 54:58].reshape(32),
        early_whole[:, :8].transpose(0, 2, 1).reshape(1024, 8),
        small[:, 53],
        late_whole[:3, 1024:].T,
        small[:3, 58],
    )


def solution(mesh):
    return jax.shard_map(
        body,
        mesh=mesh,
        in_specs=(
            P("space", None),
            P("ens", "space", None),
            P("space", None),
            P(),
            P(),
            P(),
            P(),
            P(),
            P(),
            P(),
            P(),
            P(),
            P(),
            P(),
            P(),
            P(),
        ),
        out_specs=(
            P("ens", "space", None),
            P(None, "space"),
            P("space"),
            P(None, "space"),
            P("space"),
            P("space"),
            P("space"),
            P(None, "space"),
            P("space"),
            P(None, "space"),
            P("space"),
            P(None, "space"),
            P("space"),
        ),
        check_vma=False,
    )
```

```python
import functools
import math

import jax
import jax.numpy as jnp
from jax import lax
from jax.experimental import pallas as pl
from jax.experimental.pallas import tpu as pltpu
from jax.sharding import PartitionSpec as P

EPS = 1e-06
CUBIC = 0.044715
ROOT = math.sqrt(2.0 / math.pi)
SOFT_SQUARE = 0.01
F32 = jnp.float32
BF16 = jnp.bfloat16
SIDE = 24
CELLS = SIDE * SIDE
LANE = 128
SMALL = 64
VMEM_BYTES = 24 * 1024 * 1024


def dot(left, right, left_dim=1, right_dim=0):
    return lax.dot_general(
        left, right, (((left_dim,), (right_dim,)), ((), ())), preferred_element_type=F32
    )


def soft_slope(values):
    return values * lax.rsqrt(values * values + SOFT_SQUARE)


def turned_offset(quarter, row_off, col_off):
    return (
        (row_off, col_off),
        (2 - col_off, row_off),
        (2 - row_off, 2 - col_off),
        (col_off, 2 - row_off),
    )[quarter]


def gather_patches(turns, wide_ref, stage_ref, patches_ref):
    bands = ((0, 0, 3), (3, 5, SIDE), (27, 31, 3))
    turn_of = {(1, 0): 0, (1, 2): 1, (0, 0): 2, (0, 2): 3, (2, 0): 4, (2, 2): 5}
    stage_ref[...] = jnp.zeros_like(stage_ref)
    for row_off in range(3):
        for col_off in range(3):
            for row_band, (row_to, row_from, row_len) in enumerate(bands):
                for col_band, (col_to, col_from, col_len) in enumerate(bands):

                    def read(quarter):
                        row, col = turned_offset(quarter, row_off, col_off)
                        return wide_ref[
                            row_from + row : row_from + row + row_len,
                            col_from + col : col_from + col + col_len,
                            :,
                        ]

                    piece = read(0)
                    if (row_band, col_band) in turn_of:
                        turn = turns[turn_of[row_band, col_band]]
                        for quarter in range(1, 4):
                            piece = jnp.where(turn == quarter, read(quarter), piece)
                    stage_ref[row_to : row_to + row_len, col_to : col_to + col_len, :] = piece
            at = (3 * row_off + col_off) * LANE
            patches_ref[:, at : at + LANE] = stage_ref[...].reshape(960, LANE).astype(BF16)


def forward_kernel(
    seam_turns_ref,
    source_ref,
    w_in_ref,
    w_depth_low_ref,
    vectors_ref,
    w_up_ref,
    w_down_ref,
    head_ref,
    patches_ref,
    stem_ref,
    normed_ref,
    inverse_ref,
    scaled_ref,
    slope_ref,
    active_ref,
    hidden_ref,
    field_ref,
    tight_ref,
    sent_ref,
    w_depth_ref,
    wide_ref,
    stage_ref,
    w_in_wide_ref,
):
    tile = lax.axis_index("space")
    tiles = seam_turns_ref.shape[0]
    across = tiles // 4

    def turn_at(offset):
        return seam_turns_ref[lax.rem(tile + (tiles + offset), tiles)]

    turns = (
        turn_at(0),
        (4 - turn_at(1)) & 3,
        turn_at(-across),
        (4 - turn_at(1 - across)) & 3,
        turn_at(across),
        (4 - turn_at(across + 1)) & 3,
    )
    b_in, b_depth, gain, shift, b_down = (vectors_ref[k : k + 1, :] for k in range(5))
    head_bias = vectors_ref[5:6, 0:96]
    b_up = jnp.concatenate([vectors_ref[6 + k : 7 + k, :] for k in range(4)], axis=1)
    w_depth_ref[...] = w_depth_low_ref[...].astype(F32)
    for offset in range(9):
        w_in_wide_ref[offset * LANE : offset * LANE + 96, :] = w_in_ref[offset * 96 : (offset + 1) * 96, :]
        w_in_wide_ref[offset * LANE + 96 : (offset + 1) * LANE, :] = jnp.zeros((32, 256), BF16)
    wide_ref[...] = jnp.zeros_like(wide_ref)
    wide_ref[:, 0:36, 0:96] = source_ref[...].astype(F32)
    gather_patches(turns, wide_ref, stage_ref, patches_ref)
    for part in range(5):
        rows = slice(part * 192, (part + 1) * 192)
        stem = dot(patches_ref[rows, :], w_in_wide_ref[...]) + b_in
        stem = stem.astype(BF16).astype(F32)
        for half in range(2):
            stem_ref[half, part * 6 : (part + 1) * 6] = stem[
                :, half * LANE : (half + 1) * LANE
            ].reshape(6, 32, LANE)

    def normalise(block, carry):
        row = block * 4
        halves = []
        for half in range(2):
            lanes = slice(half * LANE, (half + 1) * LANE)
            total = jnp.zeros((4, SIDE, LANE), F32)
            for col_off in range(7):
                slab = stem_ref[half, pl.ds(row, 10), col_off : col_off + SIDE, :]
                for row_off in range(7):
                    tap = 7 * row_off + col_off
                    total = total + slab[row_off : row_off + 4] * w_depth_ref[tap : tap + 1, lanes][None]
            halves.append(total.reshape(4 * SIDE, LANE) + b_depth[:, lanes])
        mean = (
            jnp.sum(halves[0], axis=-1, keepdims=True) + jnp.sum(halves[1], axis=-1, keepdims=True)
        ) / 256.0
        centers = [h - mean for h in halves]
        spread = (
            jnp.sum(centers[0] * centers[0], axis=-1, keepdims=True)
            + jnp.sum(centers[1] * centers[1], axis=-1, keepdims=True)
        ) / 256.0
        inverse = lax.rsqrt(spread + EPS)
        at = pl.ds(pl.multiple_of(block * 96, 96), 96)
        inverse_ref[at, :] = jnp.broadcast_to(inverse, (96, LANE))
        for half in range(2):
            lanes = slice(half * LANE, (half + 1) * LANE)
            normed = centers[half] * inverse
            normed_ref[at, lanes] = normed
            scaled_ref[at, lanes] = (normed * gain[:, lanes] + shift[:, lanes]).astype(BF16)
        return carry

    lax.fori_loop(0, 6, normalise, 0)

    def mix(part, carry):
        at = pl.ds(pl.multiple_of(part * 96, 96), 96)
        upward = dot(scaled_ref[at, :], w_up_ref[...]) + b_up
        square = upward * upward
        tanh_part = jnp.tanh(ROOT * (upward + CUBIC * square * upward))
        plus = 0.5 * (1.0 + tanh_part)
        slope_ref[at, :] = plus + 0.5 * upward * (1.0 - tanh_part * tanh_part) * (
            ROOT + (3.0 * CUBIC * ROOT) * square
        )
        active = (upward * plus).astype(BF16)
        active_ref[at, :] = active
        own = [
            stem_ref[half, pl.ds(3 + 4 * part, 4), 3 : 3 + SIDE, :].reshape(96, LANE)
            for half in range(2)
        ]
        own = jnp.concatenate(own, axis=1)
        hidden = (own + dot(active, w_down_ref[...]) + b_down).astype(BF16)
        hidden_ref[at, :] = hidden
        field_ref[at, :] = dot(hidden, head_ref[...], 1, 1) + head_bias
        return carry

    lax.fori_loop(0, 6, mix, 0)
    for quarter in range(4):
        tight_ref[:, 96 * quarter : 96 * (quarter + 1)] = field_ref[
            144 * quarter : 144 * (quarter + 1), :
        ]
    sent = tight_ref[...].astype(BF16)
    for member in range(sent_ref.shape[0]):
        sent_ref[member] = sent


def mixer_backward_kernel(
    coefficient,
    every_ref,
    own_ref,
    target_ref,
    hidden_ref,
    head_ref,
    pick_ref,
    active_ref,
    slope_ref,
    scaled_ref,
    w_down_ref,
    w_up_ref,
    early_ref,
    out_part_ref,
    hidden_grad_ref,
    scaled_grad_ref,
    small_ref,
    tight_ref,
    field_ref,
    low_ref,
    up_low_ref,
    up_sum_ref,
    down_ref,
):
    members = every_ref.shape[0]
    own = own_ref[...]
    own_sent = own.astype(BF16).astype(F32)
    pair_sum = soft_slope(own_sent - every_ref[0].astype(F32))
    for member in range(1, members):
        pair_sum = pair_sum + soft_slope(own_sent - every_ref[member].astype(F32))
    direct = soft_slope(own - target_ref[...].astype(F32))
    tight_ref[...] = (
        direct * (coefficient / members) - pair_sum * (coefficient / (members * (members - 1)))
    )
    field_ref[...] = jnp.zeros_like(field_ref)
    for quarter in range(4):
        field_ref[144 * quarter : 144 * (quarter + 1), 0:96] = tight_ref[
            :, 96 * quarter : 96 * (quarter + 1)
        ]
    grad_f = field_ref[...]
    grad_b_out = jnp.sum(grad_f, axis=0, keepdims=True)
    grad_f_low = grad_f.astype(BF16)
    picked = dot(grad_f_low, pick_ref[...]).astype(BF16)
    out_part_ref[...] = dot(picked, hidden_ref[...], 0, 0).astype(BF16)
    grad_hidden = dot(grad_f_low[:, 0:96], head_ref[...])
    hidden_grad_ref[...] = grad_hidden
    low_ref[...] = grad_hidden.astype(BF16)
    grad_b_down = jnp.sum(grad_hidden, axis=0, keepdims=True)
    down_ref[...] = dot(low_ref[...], active_ref[...], 0, 0)
    up_sum_ref[...] = jnp.zeros_like(up_sum_ref)

    def widen(part, carry):
        at = pl.ds(pl.multiple_of(part * 96, 96), 96)
        grad_up = dot(low_ref[at, :], w_down_ref[...], 1, 1) * slope_ref[at, :]
        up_sum_ref[...] += jnp.sum(grad_up.reshape(12, 8, 1024), axis=0)
        up_low = grad_up.astype(BF16)
        up_low_ref[at, :] = up_low
        scaled_grad_ref[at, :] = dot(up_low, w_up_ref[...], 1, 1)
        return carry

    lax.fori_loop(0, 6, widen, 0)
    for chunk in range(4):
        up = dot(up_low_ref[:, chunk * 256 : (chunk + 1) * 256], scaled_ref[...], 0, 0)
        up = up.reshape(8, 4, 8, 256)
        for row_tile in range(4):
            for lane_tile in range(2):
                part = 2 * row_tile + lane_tile
                upper = down_ref[
                    chunk * 64 : (chunk + 1) * 64, part * LANE : (part + 1) * LANE
                ].reshape(8, 8, LANE)
                lower = up[:, row_tile, :, lane_tile * LANE : (lane_tile + 1) * LANE]
                early_ref[part, chunk * 8 : (chunk + 1) * 8] = jnp.concatenate(
                    [upper, lower], axis=1
                ).astype(BF16)
    up_sum = jnp.sum(up_sum_ref[...], axis=0, keepdims=True)
    unit = lax.broadcasted_iota(jnp.int32, (8, 1024), 1)
    row = lax.broadcasted_iota(jnp.int32, (8, 1024), 0)
    spread = jnp.where((unit & 3) == row, jnp.broadcast_to(up_sum, (8, 1024)), 0.0)
    fold = (
        lax.broadcasted_iota(jnp.int32, (1024, 256), 0) >> 2
        == lax.broadcasted_iota(jnp.int32, (1024, 256), 1)
    ).astype(F32).astype(BF16)
    column = lax.broadcasted_iota(jnp.int32, (LANE, 256), 1)
    place = (
        (lax.broadcasted_iota(jnp.int32, (LANE, 256), 0) == 3 * (column >> 3) + (column & 7))
        & ((column & 7) < 3)
    ).astype(F32).astype(BF16)
    b_out = jnp.broadcast_to(grad_b_out, (8, LANE))

    def two_part(values, matrix):
        high = values.astype(BF16)
        rest = (values - high.astype(F32)).astype(BF16)
        return dot(high, matrix) + dot(rest, matrix)

    small_ref[...] = jnp.zeros_like(small_ref)
    small_ref[0:1, :] = grad_b_down
    small_ref[1:5, :] = two_part(spread, fold)[0:4]
    small_ref[5:6, :] = two_part(b_out, place)[0:1]


def depth_backward_kernel(
    scaled_grad_ref,
    normed_ref,
    inverse_ref,
    vectors_ref,
    hidden_grad_ref,
    stem_ref,
    w_depth_ref,
    patches_ref,
    order_ref,
    early_small_ref,
    out_part_ref,
    late_ref,
    deep_ref,
    stem_grad_ref,
    small_ref,
    sums_ref,
    low_ref,
    tight_ref,
):
    deep_ref[...] = jnp.zeros_like(deep_ref)
    small_ref[...] = jnp.zeros_like(small_ref)
    sums_ref[...] = jnp.zeros_like(sums_ref)

    def unnormalise(block, carry):
        at = pl.ds(pl.multiple_of(block * 96, 96), 96)
        halves = []
        first = jnp.zeros((96, 1), F32)
        second = jnp.zeros((96, 1), F32)
        for half in range(2):
            lanes = slice(half * LANE, (half + 1) * LANE)
            grad = scaled_grad_ref[at, lanes]
            normed = normed_ref[at, lanes]
            sums_ref[0, :, lanes] += jnp.sum((grad * normed).reshape(12, 8, LANE), axis=0)
            sums_ref[1, :, lanes] += jnp.sum(grad.reshape(12, 8, LANE), axis=0)
            grad = grad * vectors_ref[2:3, lanes]
            first = first + jnp.sum(grad, axis=-1, keepdims=True)
            second = second + jnp.sum(grad * normed, axis=-1, keepdims=True)
            halves.append((grad, normed))
        first = first / 256.0
        second = second / 256.0
        inverse = inverse_ref[at, :]
        for half, (grad, normed) in enumerate(halves):
            lanes = slice(half * LANE, (half + 1) * LANE)
            deep = (grad - first - normed * second) * inverse
            sums_ref[2, :, lanes] += jnp.sum(deep.reshape(12, 8, LANE), axis=0)
            deep_ref[half, pl.ds(6 + block * 4, 4), 8 : 8 + SIDE, :] = deep.reshape(4, SIDE, LANE)
        return carry

    lax.fori_loop(0, 6, unnormalise, 0)
    for half in range(2):
        lanes = slice(half * LANE, (half + 1) * LANE)

        def spread(block, carry):
            row = block * 3
            total = jnp.zeros((3, 32, LANE), F32)
            for col_off in range(7):
                slab = deep_ref[half, pl.ds(row, 9), 8 - col_off : 40 - col_off, :]
                for row_off in range(7):
                    tap = 7 * row_off + col_off
                    total = total + slab[6 - row_off : 9 - row_off] * w_depth_ref[tap : tap + 1, lanes][None]
            stem_grad_ref[half, pl.ds(row, 3)] = total
            return carry

        lax.fori_loop(0, 10, spread, 0)
        for col_off in range(7):

            def weigh(block, totals):
                row = block * 4
                deep = deep_ref[half, pl.ds(6 + row, 4), 8 : 8 + SIDE, :]
                slab = stem_ref[half, pl.ds(row, 10), col_off : col_off + SIDE, :]
                return tuple(
                    totals[row_off]
                    + jnp.sum((slab[row_off : row_off + 4] * deep).reshape(12, 8, LANE), axis=0)
                    for row_off in range(7)
                )

            totals = lax.fori_loop(0, 6, weigh, tuple(jnp.zeros((8, LANE), F32) for _ in range(7)))
            for row_off in range(7):
                tap = 7 * row_off + col_off
                small_ref[tap : tap + 1, lanes] = jnp.sum(totals[row_off], axis=0, keepdims=True)

        def add_direct(block, carry):
            at = pl.ds(pl.multiple_of(block * 96, 96), 96)
            stem_grad_ref[half, pl.ds(3 + block * 4, 4), 3 : 3 + SIDE, :] += hidden_grad_ref[
                at, lanes
            ].reshape(4, SIDE, LANE)
            return carry

        lax.fori_loop(0, 6, add_direct, 0)
        grad_stem = stem_grad_ref[half].reshape(960, LANE)
        small_ref[52:53, lanes] = jnp.sum(grad_stem, axis=0, keepdims=True)
        low_ref[:, lanes] = grad_stem.astype(BF16)
    small_ref[49:50, :] = jnp.sum(sums_ref[2], axis=0, keepdims=True)
    small_ref[50:51, :] = jnp.sum(sums_ref[0], axis=0, keepdims=True)
    small_ref[51:52, :] = jnp.sum(sums_ref[1], axis=0, keepdims=True)
    small_ref[53:59, :] = early_small_ref[0:6, :]
    order = order_ref[...]
    ordered = dot(low_ref[...], order).astype(BF16)
    wide = dot(ordered, patches_ref[...], 0, 0)
    tight_ref[...] = jnp.zeros_like(tight_ref)
    for offset in range(9):
        tight_ref[:, 96 * offset : 96 * (offset + 1)] = wide[:, LANE * offset : LANE * offset + 96]
    late_ref[:, 0:896] = tight_ref[...].astype(BF16)
    small = small_ref[...]
    high = small.astype(BF16)
    rest = (small - high.astype(F32)).astype(BF16)
    both = jnp.concatenate([high, rest], axis=0)
    late_ref[:, 896:1024] = dot(order, both, 0, 1).astype(BF16)
    late_ref[:, 1024:1280] = out_part_ref[...]


def combine_kernel(early_ref, late_ref, share_ref, rows_ref):
    members = early_ref.shape[0]
    early = early_ref[0].astype(F32)
    late = late_ref[0].astype(F32)
    for member in range(1, members):
        early = early + early_ref[member].astype(F32)
        late = late + late_ref[member].astype(F32)
    rows_ref[:, 0:16, :] = early
    rows_ref[:, 26:32, :] = jnp.zeros_like(rows_ref[:, 26:32, :])
    for row in range(10):
        piece = late[:, row * LANE : (row + 1) * LANE]
        if row == 7:
            piece = piece + jnp.concatenate([piece[:, SMALL:], jnp.zeros_like(piece[:, SMALL:])], axis=1)
        rows_ref[:, 16 + row : 17 + row, :] = piece[:, None, :]
    share_ref[...] = rows_ref[...].astype(BF16)


def total_kernel(share_ref, copies_ref):
    total = share_ref[0].astype(F32)
    for tile in range(1, share_ref.shape[0]):
        total = total + share_ref[tile].astype(F32)
    for member in range(copies_ref.shape[0]):
        copies_ref[member] = total


def unpack_kernel(
    whole_ref, w_in_ref, w_depth_ref, w_up_ref, w_down_ref, w_out_ref, small_ref, b_up_ref
):
    parts = whole_ref.shape[0]
    for part in range(parts):
        for row in range(7):
            lanes = slice(row * LANE, min((row + 1) * LANE, 864))
            w_in_ref[part : part + 1, lanes] = whole_ref[part, 16 + row : 17 + row, 0 : lanes.stop - lanes.start]
        w_down_ref[:, part * LANE : (part + 1) * LANE] = whole_ref[part, 0:8, :]
        row_tile, lane_tile = divmod(part, 2)
        w_up_ref[8 * row_tile : 8 * row_tile + 8, lane_tile * LANE : (lane_tile + 1) * LANE] = whole_ref[
            part, 8:16, :
        ]
        w_depth_ref[part : part + 1, :] = whole_ref[part, 23:24, 0:49]
        b_up_ref[0:1, 4 * part : 4 * part + 4] = whole_ref[part, 23:24, 54:58]
    for part in range(3):
        for half in range(2):
            w_out_ref[part : part + 1, half * LANE : (half + 1) * LANE] = whole_ref[
                part, 24 + half : 25 + half, :
            ]
    small = jnp.concatenate([whole_ref[part, 23:24, :] for part in range(parts)], axis=0)
    small_ref[...] = small.T[48:64, :]


def call(kernel, shapes, scratch, *operands, smem=0, flops=0):
    space = [pl.BlockSpec(memory_space=pltpu.SMEM)] * smem
    space += [pl.BlockSpec(memory_space=pltpu.VMEM)] * (len(operands) - smem)
    return pl.pallas_call(
        kernel,
        out_shape=[jax.ShapeDtypeStruct(s, d) for s, d in shapes],
        in_specs=space,
        out_specs=[pl.BlockSpec(memory_space=pltpu.VMEM)] * len(shapes),
        scratch_shapes=[pltpu.VMEM(s, d) for s, d in scratch],
        compiler_params=pltpu.CompilerParams(vmem_limit_bytes=VMEM_BYTES),
        cost_estimate=pl.CostEstimate(flops=flops, bytes_accessed=8_000_000, transcendentals=0),
    )(*operands)


def stack_vectors(b_in, b_depth, gain, shift, b_down, head_bias, b_up):
    rows = [b_in, b_depth, gain, shift, b_down, jnp.pad(head_bias, (0, 160)), b_up]
    return jnp.concatenate(rows).astype(F32).reshape(10, 256)


def run_forward(seam_turns, source, w_in, w_depth, vectors, w_up, w_down, head, members):
    return call(
        forward_kernel,
        [
            ((960, 1152), BF16),
            ((2, 30, 32, LANE), F32),
            ((CELLS, 256), F32),
            ((CELLS, LANE), F32),
            ((CELLS, 256), BF16),
            ((CELLS, 1024), F32),
            ((CELLS, 1024), BF16),
            ((CELLS, 256), BF16),
            ((CELLS, 96), F32),
            ((144, 384), F32),
            ((members, 144, 384), BF16),
            ((49, 256), F32),
        ],
        [((36, 40, LANE), F32), ((30, 32, LANE), F32), ((1152, 256), BF16)],
        seam_turns,
        source,
        w_in,
        w_depth,
        vectors,
        w_up,
        w_down,
        head,
        smem=1,
        flops=10_000_000_000,
    )


def run_mixer_backward(every, tight, target, saved, head, w_down, w_up, coefficient):
    hidden, active, slope, scaled = saved
    column = jnp.arange(256)
    owner = 3 * (column % 32) + column // 32
    pick = ((jnp.arange(LANE)[:, None] == owner[None, :]) & (column[None, :] < 96)).astype(BF16)
    return call(
        functools.partial(mixer_backward_kernel, coefficient),
        [
            ((8, 32, 16, LANE), BF16),
            ((256, 256), BF16),
            ((CELLS, 256), F32),
            ((CELLS, 256), F32),
            ((8, 256), F32),
        ],
        [
            ((144, 384), F32),
            ((CELLS, LANE), F32),
            ((CELLS, 256), BF16),
            ((CELLS, 1024), BF16),
            ((8, 1024), F32),
            ((256, 1024), F32),
        ],
        every,
        tight,
        target,
        hidden,
        head,
        pick,
        active,
        slope,
        scaled,
        w_down,
        w_up,
        flops=12_000_000_000,
    )


def run_depth_backward(
    scaled_grad, normed, inverse, vectors, hidden_grad, stem, w_depth, patches, early_small, out_part
):
    column = jnp.arange(256)
    order = (column[:, None] == (8 * (column % 32) + column // 32)[None, :]).astype(BF16)
    return call(
        depth_backward_kernel,
        [((256, 1280), BF16)],
        [
            ((2, 36, 40, LANE), F32),
            ((2, 30, 32, LANE), F32),
            ((SMALL, 256), F32),
            ((3, 8, 256), F32),
            ((960, 256), BF16),
            ((256, 896), F32),
        ],
        scaled_grad,
        normed,
        inverse,
        vectors,
        hidden_grad,
        stem,
        w_depth,
        patches,
        order,
        early_small,
        out_part,
        flops=12_000_000_000,
    )[0]


def run_combine(early, late):
    return call(combine_kernel, [((32, 32, LANE), BF16)], [((32, 32, LANE), F32)], early, late)[0]


def run_total(share, members):
    return call(total_kernel, [((members, 32, LANE), F32)], [], share)[0]


def run_unpack(whole):
    shapes = ((8, 864), (8, 49), (32, 256), (8, 1024), (3, 256), (16, 8), (1, 32))
    return call(unpack_kernel, [(shape, F32) for shape in shapes], [], whole)


def shifted(value, axis, by):
    peers = lax.axis_size(axis)
    return lax.ppermute(value, axis, [(i, (i + by) % peers) for i in range(peers)])


def turned_edge(tile, turns, width, east):
    size = tile.shape[0]

    def columns(x):
        return x[:, size - width :] if east else x[:, :width]

    sides = (
        columns(tile),
        columns(jnp.rot90(tile, 1)),
        columns(jnp.rot90(tile, 2)),
        columns(jnp.rot90(tile, 3)),
    )
    result = sides[0]
    for quarter in range(1, 4):
        result = jnp.where(turns == quarter, sides[quarter], result)
    return result


def seam_pad(tile, my_turn, next_turn, margin, row_tiles):
    came_west = shifted(turned_edge(tile, next_turn, margin, True), "space", 1)
    came_east = shifted(turned_edge(tile, (4 - my_turn) % 4, margin, False), "space", -1)
    widened = jnp.concatenate([came_west, tile, came_east], axis=1)
    came_north = shifted(widened[-margin:], "space", row_tiles)
    came_south = shifted(widened[:margin], "space", -row_tiles)
    return jnp.concatenate([came_north, widened, came_south], axis=0)


def swap(value, axis):
    return lax.all_to_all(value, axis, 0, 0, tiled=True)


def body(
    initial_state,
    starting_field_nudges,
    verifying_analysis,
    seam_turns,
    w_in,
    b_in,
    w_depth,
    b_depth,
    norm_gain,
    norm_shift,
    w_up,
    b_up,
    w_down,
    b_down,
    head_weight,
    head_bias,
):
    spaces = lax.axis_size("space")
    members = lax.axis_size("ens")
    row_tiles = spaces // 4
    tile_index = lax.axis_index("space")

    def turn_at(offset):
        return lax.dynamic_index_in_dim(seam_turns, (tile_index + offset) % spaces, keepdims=False)

    my_turn = turn_at(0)
    next_turn = turn_at(1)
    source = (
        initial_state.astype(F32) + starting_field_nudges[0].astype(F32)
    ).astype(BF16).reshape(SIDE, SIDE, 96)
    near = seam_pad(source, my_turn, next_turn, 1, row_tiles)
    wide_source = seam_pad(near, my_turn, next_turn, 5, row_tiles)
    vectors = stack_vectors(b_in, b_depth, norm_gain, norm_shift, b_down, head_bias, b_up)
    head = head_weight.T
    saved = run_forward(seam_turns, wide_source, w_in, w_depth, vectors, w_up, w_down, head, members)
    patches, stem, normed, inverse, scaled, slope, active, hidden, field, tight, sent, w_depth_wide = saved
    sent, verifying_analysis, field_again = lax.optimization_barrier((sent, verifying_analysis, field))
    every = swap(sent, "ens")
    predicted = field_again.reshape(1, SIDE, SIDE * 96)
    target = verifying_analysis.reshape(4, 144, 96).transpose(1, 0, 2).reshape(144, 384)
    coefficient = 1.0 / math.sqrt(spaces * CELLS * 96)
    early, out_part, hidden_grad, scaled_grad, early_small = run_mixer_backward(
        every, tight, target, (hidden, active, slope, scaled), head, w_down, w_up, coefficient
    )
    late = run_depth_backward(
        scaled_grad, normed, inverse, vectors, hidden_grad, stem, w_depth_wide, patches, early_small, out_part
    )
    early_parts, late = lax.optimization_barrier((swap(early, "ens"), late))
    late_parts = swap(late.reshape(8, 32, 1280), "ens")
    shares = swap(run_combine(early_parts, late_parts), "space")
    whole = swap(run_total(shares, members), "ens")
    grad_w_in, grad_w_depth, grad_w_up, grad_w_down, grad_w_out, small, grad_b_up = run_unpack(whole)
    return (
        predicted,
        grad_w_in.T,
        small[4],
        grad_w_depth.T,
        small[1],
        small[2],
        small[3],
        grad_w_up.T,
        grad_b_up[0],
        grad_w_down.T,
        small[5],
        grad_w_out.T,
        small[10, :3],
    )


def solution(mesh):
    return jax.shard_map(
        body,
        mesh=mesh,
        in_specs=(
            P("space", None),
            P("ens", "space", None),
            P("space", None),
            P(),
            P(),
            P(),
            P(),
            P(),
            P(),
            P(),
            P(),
            P(),
            P(),
            P(),
            P(),
            P(),
        ),
        out_specs=(
            P("ens", "space", None),
            P(None, "space"),
            P("space"),
            P(None, "space"),
            P("space"),
            P("space"),
            P("space"),
            P(None, "space"),
            P("space"),
            P(None, "space"),
            P("space"),
            P(None, "space"),
            P("space"),
        ),
        check_vma=False,
    )
```

```python
import functools
import math

import jax
import jax.numpy as jnp
from jax import lax
from jax.experimental import pallas as pl
from jax.experimental.pallas import tpu as pltpu
from jax.sharding import PartitionSpec as P

EPS = 1e-06
CUBIC = 0.044715
ROOT = math.sqrt(2.0 / math.pi)
SOFT_SQUARE = 0.01
F32 = jnp.float32
BF16 = jnp.bfloat16
SIDE = 24
CELLS = SIDE * SIDE
LANE = 128
SMALL = 64
VMEM_BYTES = 56 * 1024 * 1024
SMALL_VMEM_BYTES = 16 * 1024 * 1024


def dot(left, right, left_dim=1, right_dim=0):
    return lax.dot_general(
        left, right, (((left_dim,), (right_dim,)), ((), ())), preferred_element_type=F32
    )


def soft_slope(values):
    return values * lax.rsqrt(values * values + SOFT_SQUARE)


def turned_offset(quarter, row_off, col_off):
    return (
        (row_off, col_off),
        (2 - col_off, row_off),
        (2 - row_off, 2 - col_off),
        (col_off, 2 - row_off),
    )[quarter]


def gather_patches(turns, wide_ref, stage_ref, patches_ref):
    bands = ((0, 0, 3), (3, 5, SIDE), (27, 31, 3))
    turn_of = {(1, 0): 0, (1, 2): 1, (0, 0): 2, (0, 2): 3, (2, 0): 4, (2, 2): 5}
    stage_ref[...] = jnp.zeros_like(stage_ref)
    for row_off in range(3):
        for col_off in range(3):
            for row_band, (row_to, row_from, row_len) in enumerate(bands):
                for col_band, (col_to, col_from, col_len) in enumerate(bands):

                    def read(quarter):
                        row, col = turned_offset(quarter, row_off, col_off)
                        return wide_ref[
                            row_from + row : row_from + row + row_len,
                            col_from + col : col_from + col + col_len,
                            :,
                        ]

                    piece = read(0)
                    if (row_band, col_band) in turn_of:
                        turn = turns[turn_of[row_band, col_band]]
                        for quarter in range(1, 4):
                            piece = jnp.where(turn == quarter, read(quarter), piece)
                    stage_ref[row_to : row_to + row_len, col_to : col_to + col_len, :] = piece
            at = (3 * row_off + col_off) * LANE
            patches_ref[:, at : at + LANE] = stage_ref[...].reshape(960, LANE).astype(BF16)


def forward_kernel(
    seam_turns_ref,
    source_ref,
    w_in_ref,
    w_depth_low_ref,
    vectors_ref,
    w_up_ref,
    w_down_ref,
    head_ref,
    patches_out,
    stem_out,
    normed_ref,
    inverse_ref,
    scaled_ref,
    slope_out,
    active_out,
    hidden_ref,
    field_ref,
    tight_ref,
    sent_ref,
    w_depth_ref,
    patches_ref,
    stem_ref,
    slope_ref,
    active_ref,
    wide_ref,
    stage_ref,
    w_in_wide_ref,
    whole_sem,
    part_sem,
):
    def send_part(part, row):
        at = pl.ds(row, 96)
        return (
            pltpu.make_async_copy(slope_ref.at[at], slope_out.at[at], part_sem.at[0, part]),
            pltpu.make_async_copy(active_ref.at[at], active_out.at[at], part_sem.at[1, part]),
        )

    send_patches = pltpu.make_async_copy(patches_ref, patches_out, whole_sem.at[0])
    send_stem = pltpu.make_async_copy(stem_ref, stem_out, whole_sem.at[1])
    tile = lax.axis_index("space")
    tiles = seam_turns_ref.shape[0]
    across = tiles // 4

    def turn_at(offset):
        return seam_turns_ref[lax.rem(tile + (tiles + offset), tiles)]

    turns = (
        turn_at(0),
        (4 - turn_at(1)) & 3,
        turn_at(-across),
        (4 - turn_at(1 - across)) & 3,
        turn_at(across),
        (4 - turn_at(across + 1)) & 3,
    )
    b_in, b_depth, gain, shift, b_down = (vectors_ref[k : k + 1, :] for k in range(5))
    head_bias = vectors_ref[5:6, 0:96]
    b_up = jnp.concatenate([vectors_ref[6 + k : 7 + k, :] for k in range(4)], axis=1)
    w_depth_ref[...] = w_depth_low_ref[...].astype(F32)
    for offset in range(9):
        w_in_wide_ref[offset * LANE : offset * LANE + 96, :] = w_in_ref[offset * 96 : (offset + 1) * 96, :]
        w_in_wide_ref[offset * LANE + 96 : (offset + 1) * LANE, :] = jnp.zeros((32, 256), BF16)
    wide_ref[...] = jnp.zeros_like(wide_ref)
    wide_ref[:, 0:36, 0:96] = source_ref[...].astype(F32)
    gather_patches(turns, wide_ref, stage_ref, patches_ref)
    send_patches.start()
    for part in range(5):
        rows = slice(part * 192, (part + 1) * 192)
        stem = dot(patches_ref[rows, :], w_in_wide_ref[...]) + b_in
        stem = stem.astype(BF16).astype(F32)
        for half in range(2):
            stem_ref[half, part * 6 : (part + 1) * 6] = stem[
                :, half * LANE : (half + 1) * LANE
            ].reshape(6, 32, LANE)

    send_stem.start()

    def normalise(block, carry):
        row = block * 4
        halves = []
        for half in range(2):
            lanes = slice(half * LANE, (half + 1) * LANE)
            total = jnp.zeros((4, SIDE, LANE), F32)
            for col_off in range(7):
                slab = stem_ref[half, pl.ds(row, 10), col_off : col_off + SIDE, :]
                for row_off in range(7):
                    tap = 7 * row_off + col_off
                    total = total + slab[row_off : row_off + 4] * w_depth_ref[tap : tap + 1, lanes][None]
            halves.append(total.reshape(4 * SIDE, LANE) + b_depth[:, lanes])
        mean = (
            jnp.sum(halves[0], axis=-1, keepdims=True) + jnp.sum(halves[1], axis=-1, keepdims=True)
        ) / 256.0
        centers = [h - mean for h in halves]
        spread = (
            jnp.sum(centers[0] * centers[0], axis=-1, keepdims=True)
            + jnp.sum(centers[1] * centers[1], axis=-1, keepdims=True)
        ) / 256.0
        inverse = lax.rsqrt(spread + EPS)
        at = pl.ds(pl.multiple_of(block * 96, 96), 96)
        inverse_ref[at, :] = jnp.broadcast_to(inverse, (96, LANE))
        for half in range(2):
            lanes = slice(half * LANE, (half + 1) * LANE)
            normed = centers[half] * inverse
            normed_ref[at, lanes] = normed
            scaled_ref[at, lanes] = (normed * gain[:, lanes] + shift[:, lanes]).astype(BF16)
        return carry

    lax.fori_loop(0, 6, normalise, 0)

    def mix(part, carry):
        row = pl.multiple_of(part * 96, 96)
        at = pl.ds(row, 96)
        upward = dot(scaled_ref[at, :], w_up_ref[...]) + b_up
        square = upward * upward
        tanh_part = jnp.tanh(ROOT * (upward + CUBIC * square * upward))
        plus = 0.5 * (1.0 + tanh_part)
        slope = plus + 0.5 * upward * (1.0 - tanh_part * tanh_part) * (
            ROOT + (3.0 * CUBIC * ROOT) * square
        )
        slope_ref[at, :] = slope.astype(BF16)
        active = (upward * plus).astype(BF16)
        active_ref[at, :] = active
        for send in send_part(part, row):
            send.start()
        own = [
            stem_ref[half, pl.ds(3 + 4 * part, 4), 3 : 3 + SIDE, :].reshape(96, LANE)
            for half in range(2)
        ]
        own = jnp.concatenate(own, axis=1)
        hidden = (own + dot(active, w_down_ref[...]) + b_down).astype(BF16)
        hidden_ref[at, :] = hidden
        field_ref[at, :] = dot(hidden, head_ref[...], 1, 1) + head_bias
        return carry

    lax.fori_loop(0, 6, mix, 0)
    for quarter in range(4):
        tight_ref[:, 96 * quarter : 96 * (quarter + 1)] = field_ref[
            144 * quarter : 144 * (quarter + 1), :
        ]
    sent = tight_ref[...].astype(BF16)
    for member in range(sent_ref.shape[0]):
        sent_ref[member] = sent
    send_patches.wait()
    send_stem.wait()
    for part in range(6):
        for send in send_part(part, 96 * part):
            send.wait()


def mixer_backward_kernel(
    coefficient,
    every_ref,
    own_ref,
    target_ref,
    hidden_ref,
    head_ref,
    pick_ref,
    active_in,
    slope_in,
    scaled_ref,
    w_down_in,
    w_up_in,
    early_ref,
    out_part_ref,
    hidden_grad_out,
    scaled_grad_out,
    small_ref,
    tight_ref,
    field_ref,
    low_ref,
    up_low_ref,
    up_sum_ref,
    down_ref,
    active_ref,
    slope_ref,
    w_down_ref,
    w_up_ref,
    hidden_grad_ref,
    scaled_grad_ref,
    in_sem,
    out_sem,
):
    fetch_active = pltpu.make_async_copy(active_in, active_ref, in_sem.at[0])
    fetch_slope = pltpu.make_async_copy(slope_in, slope_ref, in_sem.at[1])
    fetch_down = pltpu.make_async_copy(w_down_in, w_down_ref, in_sem.at[2])
    fetch_up = pltpu.make_async_copy(w_up_in, w_up_ref, in_sem.at[3])
    for fetch in (fetch_active, fetch_down, fetch_slope, fetch_up):
        fetch.start()
    send_hidden = pltpu.make_async_copy(hidden_grad_ref, hidden_grad_out, out_sem.at[0])
    send_scaled = pltpu.make_async_copy(scaled_grad_ref, scaled_grad_out, out_sem.at[1])
    members = every_ref.shape[0]
    own = own_ref[...]
    own_sent = own.astype(BF16).astype(F32)
    pair_sum = soft_slope(own_sent - every_ref[0].astype(F32))
    for member in range(1, members):
        pair_sum = pair_sum + soft_slope(own_sent - every_ref[member].astype(F32))
    direct = soft_slope(own - target_ref[...].astype(F32))
    tight_ref[...] = (
        direct * (coefficient / members) - pair_sum * (coefficient / (members * (members - 1)))
    )
    field_ref[...] = jnp.zeros_like(field_ref)
    for quarter in range(4):
        field_ref[144 * quarter : 144 * (quarter + 1), 0:96] = tight_ref[
            :, 96 * quarter : 96 * (quarter + 1)
        ]
    grad_f = field_ref[...]
    grad_b_out = jnp.sum(grad_f, axis=0, keepdims=True)
    grad_f_low = grad_f.astype(BF16)
    picked = dot(grad_f_low, pick_ref[...]).astype(BF16)
    out_part_ref[...] = dot(picked, hidden_ref[...], 0, 0)
    grad_hidden = dot(grad_f_low[:, 0:96], head_ref[...])
    hidden_grad_ref[...] = grad_hidden
    send_hidden.start()
    low_ref[...] = grad_hidden.astype(BF16)
    grad_b_down = jnp.sum(grad_hidden, axis=0, keepdims=True)
    fetch_active.wait()
    down_ref[...] = dot(low_ref[...], active_ref[...], 0, 0)
    up_sum_ref[...] = jnp.zeros_like(up_sum_ref)
    fetch_down.wait()
    fetch_slope.wait()
    fetch_up.wait()

    def widen(part, carry):
        at = pl.ds(pl.multiple_of(part * 96, 96), 96)
        grad_up = dot(low_ref[at, :], w_down_ref[...], 1, 1) * slope_ref[at, :].astype(F32)
        up_sum_ref[...] += jnp.sum(grad_up.reshape(12, 8, 1024), axis=0)
        up_low = grad_up.astype(BF16)
        up_low_ref[at, :] = up_low
        scaled_grad_ref[at, :] = dot(up_low, w_up_ref[...], 1, 1)
        return carry

    lax.fori_loop(0, 6, widen, 0)
    send_scaled.start()
    for chunk in range(4):
        up = dot(up_low_ref[:, chunk * 256 : (chunk + 1) * 256], scaled_ref[...], 0, 0)
        up = up.reshape(8, 4, 8, 256)
        for row_tile in range(4):
            for lane_tile in range(2):
                part = 2 * row_tile + lane_tile
                upper = down_ref[
                    chunk * 64 : (chunk + 1) * 64, part * LANE : (part + 1) * LANE
                ].reshape(8, 8, LANE)
                lower = up[:, row_tile, :, lane_tile * LANE : (lane_tile + 1) * LANE]
                early_ref[part, chunk * 8 : (chunk + 1) * 8] = jnp.concatenate(
                    [upper, lower], axis=1
                ).astype(BF16)
    up_sum = jnp.sum(up_sum_ref[...], axis=0, keepdims=True)
    unit = lax.broadcasted_iota(jnp.int32, (8, 1024), 1)
    row = lax.broadcasted_iota(jnp.int32, (8, 1024), 0)
    spread = jnp.where((unit & 3) == row, jnp.broadcast_to(up_sum, (8, 1024)), 0.0)
    fold = (
        lax.broadcasted_iota(jnp.int32, (1024, 256), 0) >> 2
        == lax.broadcasted_iota(jnp.int32, (1024, 256), 1)
    ).astype(F32).astype(BF16)
    column = lax.broadcasted_iota(jnp.int32, (LANE, 256), 1)
    place = (
        (lax.broadcasted_iota(jnp.int32, (LANE, 256), 0) == 3 * (column >> 3) + (column & 7))
        & ((column & 7) < 3)
    ).astype(F32).astype(BF16)
    b_out = jnp.broadcast_to(grad_b_out, (8, LANE))

    def two_part(values, matrix):
        high = values.astype(BF16)
        rest = (values - high.astype(F32)).astype(BF16)
        return dot(high, matrix) + dot(rest, matrix)

    small_ref[...] = jnp.zeros_like(small_ref)
    small_ref[0:1, :] = grad_b_down
    small_ref[1:5, :] = two_part(spread, fold)[0:4]
    small_ref[5:6, :] = two_part(b_out, place)[0:1]
    send_hidden.wait()
    send_scaled.wait()


def depth_backward_kernel(
    scaled_grad_ref,
    normed_ref,
    inverse_ref,
    vectors_ref,
    hidden_grad_in,
    stem_in,
    w_depth_ref,
    patches_in,
    order_ref,
    early_small_ref,
    out_part_ref,
    late_ref,
    deep_ref,
    stem_grad_ref,
    small_ref,
    sums_ref,
    low_ref,
    tight_ref,
    hidden_grad_ref,
    stem_ref,
    patches_ref,
    in_sem,
):
    fetch_stem = pltpu.make_async_copy(stem_in, stem_ref, in_sem.at[0])
    fetch_hidden = pltpu.make_async_copy(hidden_grad_in, hidden_grad_ref, in_sem.at[1])
    fetch_patches = pltpu.make_async_copy(patches_in, patches_ref, in_sem.at[2])
    for fetch in (fetch_stem, fetch_hidden, fetch_patches):
        fetch.start()
    deep_ref[...] = jnp.zeros_like(deep_ref)
    small_ref[...] = jnp.zeros_like(small_ref)
    sums_ref[...] = jnp.zeros_like(sums_ref)

    def unnormalise(block, carry):
        at = pl.ds(pl.multiple_of(block * 96, 96), 96)
        halves = []
        first = jnp.zeros((96, 1), F32)
        second = jnp.zeros((96, 1), F32)
        for half in range(2):
            lanes = slice(half * LANE, (half + 1) * LANE)
            grad = scaled_grad_ref[at, lanes]
            normed = normed_ref[at, lanes]
            sums_ref[0, :, lanes] += jnp.sum((grad * normed).reshape(12, 8, LANE), axis=0)
            sums_ref[1, :, lanes] += jnp.sum(grad.reshape(12, 8, LANE), axis=0)
            grad = grad * vectors_ref[2:3, lanes]
            first = first + jnp.sum(grad, axis=-1, keepdims=True)
            second = second + jnp.sum(grad * normed, axis=-1, keepdims=True)
            halves.append((grad, normed))
        first = first / 256.0
        second = second / 256.0
        inverse = inverse_ref[at, :]
        for half, (grad, normed) in enumerate(halves):
            lanes = slice(half * LANE, (half + 1) * LANE)
            deep = (grad - first - normed * second) * inverse
            sums_ref[2, :, lanes] += jnp.sum(deep.reshape(12, 8, LANE), axis=0)
            deep_ref[half, pl.ds(6 + block * 4, 4), 8 : 8 + SIDE, :] = deep.reshape(4, SIDE, LANE)
        return carry

    lax.fori_loop(0, 6, unnormalise, 0)
    fetch_stem.wait()
    fetch_hidden.wait()
    for half in range(2):
        lanes = slice(half * LANE, (half + 1) * LANE)

        def spread(block, carry):
            row = block * 3
            total = jnp.zeros((3, 32, LANE), F32)
            for col_off in range(7):
                slab = deep_ref[half, pl.ds(row, 9), 8 - col_off : 40 - col_off, :]
                for row_off in range(7):
                    tap = 7 * row_off + col_off
                    total = total + slab[6 - row_off : 9 - row_off] * w_depth_ref[tap : tap + 1, lanes][None]
            stem_grad_ref[half, pl.ds(row, 3)] = total
            return carry

        lax.fori_loop(0, 10, spread, 0)
        for col_off in range(7):

            def weigh(block, totals):
                row = block * 4
                deep = deep_ref[half, pl.ds(6 + row, 4), 8 : 8 + SIDE, :]
                slab = stem_ref[half, pl.ds(row, 10), col_off : col_off + SIDE, :]
                return tuple(
                    totals[row_off]
                    + jnp.sum((slab[row_off : row_off + 4] * deep).reshape(12, 8, LANE), axis=0)
                    for row_off in range(7)
                )

            totals = lax.fori_loop(0, 6, weigh, tuple(jnp.zeros((8, LANE), F32) for _ in range(7)))
            for row_off in range(7):
                tap = 7 * row_off + col_off
                small_ref[tap : tap + 1, lanes] = jnp.sum(totals[row_off], axis=0, keepdims=True)

        def add_direct(block, carry):
            at = pl.ds(pl.multiple_of(block * 96, 96), 96)
            stem_grad_ref[half, pl.ds(3 + block * 4, 4), 3 : 3 + SIDE, :] += hidden_grad_ref[
                at, lanes
            ].reshape(4, SIDE, LANE)
            return carry

        lax.fori_loop(0, 6, add_direct, 0)
        grad_stem = stem_grad_ref[half].reshape(960, LANE)
        small_ref[52:53, lanes] = jnp.sum(grad_stem, axis=0, keepdims=True)
        low_ref[:, lanes] = grad_stem.astype(BF16)
    small_ref[49:50, :] = jnp.sum(sums_ref[2], axis=0, keepdims=True)
    small_ref[50:51, :] = jnp.sum(sums_ref[0], axis=0, keepdims=True)
    small_ref[51:52, :] = jnp.sum(sums_ref[1], axis=0, keepdims=True)
    small_ref[53:59, :] = early_small_ref[0:6, :]
    fetch_patches.wait()
    order = order_ref[...]
    ordered = dot(low_ref[...], order).astype(BF16)
    wide = dot(ordered, patches_ref[...], 0, 0)
    tight_ref[...] = jnp.zeros_like(tight_ref)
    for offset in range(9):
        tight_ref[:, 96 * offset : 96 * (offset + 1)] = wide[:, LANE * offset : LANE * offset + 96]
    for part in range(8):
        rows = slice(32 * part, 32 * (part + 1))
        for row, at in enumerate((864, 1024, 1056)):
            tight_ref[rows, at : at + 32] = out_part_ref[32 * row : 32 * (row + 1), rows]
    small = small_ref[...]
    high = small.astype(BF16)
    rest = (small - high.astype(F32)).astype(BF16)
    both = jnp.concatenate([high, rest], axis=0)
    tight_ref[:, 896:1024] = dot(order, both, 0, 1)
    late_ref[...] = tight_ref[...].astype(BF16)


def combine_kernel(early_ref, late_ref, share_ref, rows_ref):
    members = early_ref.shape[0]
    early = early_ref[0].astype(F32)
    late = late_ref[0].astype(F32)
    for member in range(1, members):
        early = early + early_ref[member].astype(F32)
        late = late + late_ref[member].astype(F32)
    rows_ref[:, 0:16, :] = early
    for row in range(7):
        rows_ref[:, 16 + row : 17 + row, :] = late[:, row * LANE : (row + 1) * LANE][:, None, :]
    small = late[:, 896 : 896 + SMALL] + late[:, 960 : 960 + SMALL]
    last = jnp.concatenate([small, late[:, 1024:1088]], axis=1)
    rows_ref[:, 23:24, :] = last[:, None, :]
    share_ref[...] = rows_ref[...].astype(BF16)


def total_kernel(share_ref, copies_ref):
    total = share_ref[0].astype(F32)
    for tile in range(1, share_ref.shape[0]):
        total = total + share_ref[tile].astype(F32)
    for member in range(copies_ref.shape[0]):
        copies_ref[member] = total


def unpack_kernel(
    whole_ref, w_in_ref, w_depth_ref, w_up_ref, w_down_ref, w_out_ref, small_ref, b_up_ref
):
    parts = whole_ref.shape[0]
    for part in range(parts):
        for row in range(7):
            lanes = slice(row * LANE, min((row + 1) * LANE, 864))
            w_in_ref[part : part + 1, lanes] = whole_ref[part, 16 + row : 17 + row, 0 : lanes.stop - lanes.start]
        w_down_ref[:, part * LANE : (part + 1) * LANE] = whole_ref[part, 0:8, :]
        row_tile, lane_tile = divmod(part, 2)
        w_up_ref[8 * row_tile : 8 * row_tile + 8, lane_tile * LANE : (lane_tile + 1) * LANE] = whole_ref[
            part, 8:16, :
        ]
        w_depth_ref[part : part + 1, :] = whole_ref[part, 23:24, 0:49]
        lanes = slice(32 * part, 32 * (part + 1))
        w_out_ref[0:1, lanes] = whole_ref[part, 22:23, 96:128]
        w_out_ref[1:2, lanes] = whole_ref[part, 23:24, 64:96]
        w_out_ref[2:3, lanes] = whole_ref[part, 23:24, 96:128]
        b_up_ref[0:1, 4 * part : 4 * part + 4] = whole_ref[part, 23:24, 54:58]
    small = jnp.concatenate([whole_ref[part, 23:24, :] for part in range(parts)], axis=0)
    small_ref[...] = small.T[48:64, :]


def call(kernel, outs, scratch, *operands, spaces=None, vmem=VMEM_BYTES, flops=0):
    kinds = {"v": pltpu.VMEM, "s": pltpu.SMEM, "a": pl.ANY}
    spaces = spaces or "v" * len(operands)
    return pl.pallas_call(
        kernel,
        out_shape=[jax.ShapeDtypeStruct(shape, kind) for shape, kind, _ in outs],
        in_specs=[pl.BlockSpec(memory_space=kinds[letter]) for letter in spaces],
        out_specs=[pl.BlockSpec(memory_space=kinds[letter]) for _, _, letter in outs],
        scratch_shapes=[x if not isinstance(x, tuple) else pltpu.VMEM(*x) for x in scratch],
        compiler_params=pltpu.CompilerParams(vmem_limit_bytes=vmem),
        cost_estimate=pl.CostEstimate(flops=flops, bytes_accessed=8_000_000, transcendentals=0),
    )(*operands)


def stack_vectors(b_in, b_depth, gain, shift, b_down, head_bias, b_up):
    rows = [b_in, b_depth, gain, shift, b_down, jnp.pad(head_bias, (0, 160)), b_up]
    return jnp.concatenate(rows).astype(F32).reshape(10, 256)


def run_forward(seam_turns, source, w_in, w_depth, vectors, w_up, w_down, head, members):
    return call(
        forward_kernel,
        [
            ((960, 1152), BF16, "a"),
            ((2, 30, 32, LANE), F32, "a"),
            ((CELLS, 256), F32, "v"),
            ((CELLS, LANE), F32, "v"),
            ((CELLS, 256), BF16, "v"),
            ((CELLS, 1024), BF16, "a"),
            ((CELLS, 1024), BF16, "a"),
            ((CELLS, 256), BF16, "v"),
            ((CELLS, 96), F32, "v"),
            ((144, 384), F32, "v"),
            ((members, 144, 384), BF16, "v"),
            ((49, 256), F32, "v"),
        ],
        [
            ((960, 1152), BF16),
            ((2, 30, 32, LANE), F32),
            ((CELLS, 1024), BF16),
            ((CELLS, 1024), BF16),
            ((36, 40, LANE), F32),
            ((30, 32, LANE), F32),
            ((1152, 256), BF16),
            pltpu.SemaphoreType.DMA((2,)),
            pltpu.SemaphoreType.DMA((2, 6)),
        ],
        seam_turns,
        source,
        w_in,
        w_depth,
        vectors,
        w_up,
        w_down,
        head,
        spaces="svvvvvvv",
        flops=10_000_000_000,
    )


def run_mixer_backward(every, tight, target, saved, head, w_down, w_up, coefficient):
    hidden, active, slope, scaled = saved
    column = jnp.arange(96)
    owner = 3 * (column % 32) + column // 32
    pick = (jnp.arange(LANE)[:, None] == owner[None, :]).astype(BF16)
    return call(
        functools.partial(mixer_backward_kernel, coefficient),
        [
            ((8, 32, 16, LANE), BF16, "v"),
            ((96, 256), F32, "v"),
            ((CELLS, 256), F32, "a"),
            ((CELLS, 256), F32, "a"),
            ((8, 256), F32, "v"),
        ],
        [
            ((144, 384), F32),
            ((CELLS, LANE), F32),
            ((CELLS, 256), BF16),
            ((CELLS, 1024), BF16),
            ((8, 1024), F32),
            ((256, 1024), F32),
            ((CELLS, 1024), BF16),
            ((CELLS, 1024), BF16),
            ((1024, 256), BF16),
            ((256, 1024), BF16),
            ((CELLS, 256), F32),
            ((CELLS, 256), F32),
            pltpu.SemaphoreType.DMA((4,)),
            pltpu.SemaphoreType.DMA((2,)),
        ],
        every,
        tight,
        target,
        hidden,
        head,
        pick,
        active,
        slope,
        scaled,
        w_down,
        w_up,
        spaces="vvvvvvaavaa",
        flops=12_000_000_000,
    )


def run_depth_backward(
    scaled_grad, normed, inverse, vectors, hidden_grad, stem, w_depth, patches, early_small, out_part
):
    column = jnp.arange(256)
    order = (column[:, None] == (8 * (column % 32) + column // 32)[None, :]).astype(BF16)
    return call(
        depth_backward_kernel,
        [((256, 1152), BF16, "v")],
        [
            ((2, 36, 40, LANE), F32),
            ((2, 30, 32, LANE), F32),
            ((SMALL, 256), F32),
            ((3, 8, 256), F32),
            ((960, 256), BF16),
            ((256, 1152), F32),
            ((CELLS, 256), F32),
            ((2, 30, 32, LANE), F32),
            ((960, 1152), BF16),
            pltpu.SemaphoreType.DMA((3,)),
        ],
        scaled_grad,
        normed,
        inverse,
        vectors,
        hidden_grad,
        stem,
        w_depth,
        patches,
        order,
        early_small,
        out_part,
        spaces="vvvvaavavvv",
        flops=12_000_000_000,
    )[0]


def run_combine(early, late):
    return call(
        combine_kernel,
        [((32, 24, LANE), BF16, "v")],
        [((32, 24, LANE), F32)],
        early,
        late,
        vmem=SMALL_VMEM_BYTES,
    )[0]


def run_total(share, members):
    return call(total_kernel, [((members, 24, LANE), F32, "v")], [], share, vmem=SMALL_VMEM_BYTES)[0]


def run_unpack(whole):
    shapes = ((8, 864), (8, 49), (32, 256), (8, 1024), (3, 256), (16, 8), (1, 32))
    return call(
        unpack_kernel, [(shape, F32, "v") for shape in shapes], [], whole, vmem=SMALL_VMEM_BYTES
    )


def shifted(value, axis, by):
    peers = lax.axis_size(axis)
    return lax.ppermute(value, axis, [(i, (i + by) % peers) for i in range(peers)])


def turned_edge(tile, turns, width, east):
    size = tile.shape[0]

    def columns(x):
        return x[:, size - width :] if east else x[:, :width]

    sides = (
        columns(tile),
        columns(jnp.rot90(tile, 1)),
        columns(jnp.rot90(tile, 2)),
        columns(jnp.rot90(tile, 3)),
    )
    result = sides[0]
    for quarter in range(1, 4):
        result = jnp.where(turns == quarter, sides[quarter], result)
    return result


def seam_pad(tile, my_turn, next_turn, margin, row_tiles):
    came_west = shifted(turned_edge(tile, next_turn, margin, True), "space", 1)
    came_east = shifted(turned_edge(tile, (4 - my_turn) % 4, margin, False), "space", -1)
    widened = jnp.concatenate([came_west, tile, came_east], axis=1)
    came_north = shifted(widened[-margin:], "space", row_tiles)
    came_south = shifted(widened[:margin], "space", -row_tiles)
    return jnp.concatenate([came_north, widened, came_south], axis=0)


def swap(value, axis):
    return lax.all_to_all(value, axis, 0, 0, tiled=True)


def body(
    initial_state,
    starting_field_nudges,
    verifying_analysis,
    seam_turns,
    w_in,
    b_in,
    w_depth,
    b_depth,
    norm_gain,
    norm_shift,
    w_up,
    b_up,
    w_down,
    b_down,
    head_weight,
    head_bias,
):
    spaces = lax.axis_size("space")
    members = lax.axis_size("ens")
    row_tiles = spaces // 4
    tile_index = lax.axis_index("space")

    def turn_at(offset):
        return lax.dynamic_index_in_dim(seam_turns, (tile_index + offset) % spaces, keepdims=False)

    my_turn = turn_at(0)
    next_turn = turn_at(1)
    source = (
        initial_state.astype(F32) + starting_field_nudges[0].astype(F32)
    ).astype(BF16).reshape(SIDE, SIDE, 96)
    near = seam_pad(source, my_turn, next_turn, 1, row_tiles)
    wide_source = seam_pad(near, my_turn, next_turn, 5, row_tiles)
    vectors = stack_vectors(b_in, b_depth, norm_gain, norm_shift, b_down, head_bias, b_up)
    head = head_weight.T
    saved = run_forward(seam_turns, wide_source, w_in, w_depth, vectors, w_up, w_down, head, members)
    patches, stem, normed, inverse, scaled, slope, active, hidden, field, tight, sent, w_depth_wide = saved
    sent, verifying_analysis, field_again = lax.optimization_barrier((sent, verifying_analysis, field))
    every = swap(sent, "ens")
    predicted = field_again.reshape(1, SIDE, SIDE * 96)
    target = verifying_analysis.reshape(4, 144, 96).transpose(1, 0, 2).reshape(144, 384)
    coefficient = 1.0 / math.sqrt(spaces * CELLS * 96)
    early, out_part, hidden_grad, scaled_grad, early_small = run_mixer_backward(
        every, tight, target, (hidden, active, slope, scaled), head, w_down, w_up, coefficient
    )
    late = run_depth_backward(
        scaled_grad, normed, inverse, vectors, hidden_grad, stem, w_depth_wide, patches, early_small, out_part
    )
    early_parts, late = lax.optimization_barrier((swap(early, "ens"), late))
    late_parts = swap(late.reshape(8, 32, 1152), "ens")
    shares = swap(run_combine(early_parts, late_parts), "space")
    whole = swap(run_total(shares, members), "ens")
    grad_w_in, grad_w_depth, grad_w_up, grad_w_down, grad_w_out, small, grad_b_up = run_unpack(whole)
    return (
        predicted,
        grad_w_in.T,
        small[4],
        grad_w_depth.T,
        small[1],
        small[2],
        small[3],
        grad_w_up.T,
        grad_b_up[0],
        grad_w_down.T,
        small[5],
        grad_w_out.T,
        small[10, :3],
    )


def solution(mesh):
    return jax.shard_map(
        body,
        mesh=mesh,
        in_specs=(
            P("space", None),
            P("ens", "space", None),
            P("space", None),
            P(),
            P(),
            P(),
            P(),
            P(),
            P(),
            P(),
            P(),
            P(),
            P(),
            P(),
            P(),
            P(),
        ),
        out_specs=(
            P("ens", "space", None),
            P(None, "space"),
            P("space"),
            P(None, "space"),
            P("space"),
            P("space"),
            P("space"),
            P(None, "space"),
            P("space"),
            P(None, "space"),
            P("space"),
            P(None, "space"),
            P("space"),
        ),
        check_vma=False,
    )
```

```python
import functools
import math

import jax
import jax.numpy as jnp
from jax import lax
from jax.experimental import pallas as pl
from jax.experimental.pallas import tpu as pltpu
from jax.sharding import PartitionSpec as P

EPS = 1e-06
CUBIC = 0.044715
ROOT = math.sqrt(2.0 / math.pi)
SOFT_SQUARE = 0.01
F32 = jnp.float32
BF16 = jnp.bfloat16
SIDE = 24
CELLS = SIDE * SIDE
LANE = 128
SMALL = 64
VMEM_BYTES = 56 * 1024 * 1024
SMALL_VMEM_BYTES = 16 * 1024 * 1024


def dot(left, right, left_dim=1, right_dim=0):
    return lax.dot_general(
        left, right, (((left_dim,), (right_dim,)), ((), ())), preferred_element_type=F32
    )


def soft_slope(values):
    return values * lax.rsqrt(values * values + SOFT_SQUARE)


def turned_offset(quarter, row_off, col_off):
    return (
        (row_off, col_off),
        (2 - col_off, row_off),
        (2 - row_off, 2 - col_off),
        (col_off, 2 - row_off),
    )[quarter]


BANDS = ((0, 0, 3), (3, 5, SIDE), (27, 31, 3))


def gather_patches(pieces, wide_ref, stage_ref, patches_ref):
    stage_ref[...] = jnp.zeros_like(stage_ref)
    cells = patches_ref.shape[0]
    for row_off in range(3):
        for col_off in range(3):
            for turn, row_to, row_from, row_len, col_to, col_from, col_len in pieces:

                def read(quarter):
                    row, col = turned_offset(quarter, row_off, col_off)
                    return wide_ref[
                        row_from + row : row_from + row + row_len,
                        col_from + col : col_from + col + col_len,
                        :,
                    ]

                piece = read(0)
                if turn is not None:
                    for quarter in range(1, 4):
                        piece = jnp.where(turn == quarter, read(quarter), piece)
                stage_ref[row_to : row_to + row_len, col_to : col_to + col_len, :] = piece
            at = (3 * row_off + col_off) * LANE
            patches_ref[:, at : at + LANE] = stage_ref[...].reshape(cells, LANE).astype(BF16)


def turn_reader(seam_turns_ref):
    tile = lax.axis_index("space")
    tiles = seam_turns_ref.shape[0]
    return lambda offset: seam_turns_ref[lax.rem(tile + (tiles + offset), tiles)], tiles // 4


def widen_stem_weight(w_in_ref, w_in_wide_ref):
    for offset in range(9):
        w_in_wide_ref[offset * LANE : offset * LANE + 96, :] = w_in_ref[offset * 96 : (offset + 1) * 96, :]
        w_in_wide_ref[offset * LANE + 96 : (offset + 1) * LANE, :] = jnp.zeros((32, 256), BF16)


def normalise_block(slab_row, row, stem_ref, w_depth_ref, vectors_ref, normed_ref, inverse_ref, scaled_ref):
    halves = []
    for half in range(2):
        lanes = slice(half * LANE, (half + 1) * LANE)
        total = jnp.zeros((4, SIDE, LANE), F32)
        for col_off in range(7):
            slab = stem_ref[half, pl.ds(slab_row, 10), col_off : col_off + SIDE, :]
            for row_off in range(7):
                tap = 7 * row_off + col_off
                total = total + slab[row_off : row_off + 4] * w_depth_ref[tap : tap + 1, lanes][None]
        halves.append(total.reshape(4 * SIDE, LANE) + vectors_ref[1:2, lanes])
    mean = (
        jnp.sum(halves[0], axis=-1, keepdims=True) + jnp.sum(halves[1], axis=-1, keepdims=True)
    ) / 256.0
    centers = [h - mean for h in halves]
    spread = (
        jnp.sum(centers[0] * centers[0], axis=-1, keepdims=True)
        + jnp.sum(centers[1] * centers[1], axis=-1, keepdims=True)
    ) / 256.0
    inverse = lax.rsqrt(spread + EPS)
    at = pl.ds(row, 96)
    inverse_ref[at, :] = jnp.broadcast_to(inverse, (96, LANE))
    for half in range(2):
        lanes = slice(half * LANE, (half + 1) * LANE)
        normed = centers[half] * inverse
        normed_ref[at, lanes] = normed
        scaled_ref[at, lanes] = (normed * vectors_ref[2:3, lanes] + vectors_ref[3:4, lanes]).astype(BF16)


def mix_block(
    own_row, row, stem_ref, vectors_ref, w_up_ref, w_down_ref, head_ref,
    scaled_ref, slope_ref, active_ref, hidden_ref,
):
    b_up = jnp.concatenate([vectors_ref[6 + k : 7 + k, :] for k in range(4)], axis=1)
    at = pl.ds(row, 96)
    upward = dot(scaled_ref[at, :], w_up_ref[...]) + b_up
    square = upward * upward
    tanh_part = jnp.tanh(ROOT * (upward + CUBIC * square * upward))
    plus = 0.5 * (1.0 + tanh_part)
    slope = plus + 0.5 * upward * (1.0 - tanh_part * tanh_part) * (ROOT + (3.0 * CUBIC * ROOT) * square)
    slope_ref[at, :] = slope.astype(BF16)
    active = (upward * plus).astype(BF16)
    active_ref[at, :] = active
    own = [
        stem_ref[half, pl.ds(own_row, 4), 3 : 3 + SIDE, :].reshape(96, LANE) for half in range(2)
    ]
    own = jnp.concatenate(own, axis=1)
    hidden = (own + dot(active, w_down_ref[...]) + vectors_ref[4:5, :]).astype(BF16)
    hidden_ref[at, :] = hidden
    return dot(hidden, head_ref[...], 1, 1) + vectors_ref[5:6, 0:96]


def middle_forward_kernel(
    seam_turns_ref, band_ref, w_in_ref, w_depth_low_ref, vectors_ref, w_up_ref, w_down_ref, head_ref,
    patches_out, stem_out, normed_out, inverse_out, scaled_out, slope_out, active_out, hidden_out,
    field_ref, w_depth_ref,
    patches_ref, stem_ref, normed_ref, inverse_ref, scaled_ref, slope_ref, active_ref, hidden_ref,
    wide_ref, stage_ref, w_in_wide_ref, sem,
):
    pairs = ((normed_ref, normed_out), (inverse_ref, inverse_out), (scaled_ref, scaled_out),
             (slope_ref, slope_out), (active_ref, active_out), (hidden_ref, hidden_out))
    sends = [pltpu.make_async_copy(a, b.at[96:480], sem.at[2 + k]) for k, (a, b) in enumerate(pairs)]
    send_patches = pltpu.make_async_copy(patches_ref, patches_out.at[96:864], sem.at[0])
    send_stem = pltpu.make_async_copy(stem_ref, stem_out.at[:, 3:27], sem.at[1])
    turn_at, _ = turn_reader(seam_turns_ref)
    w_depth_ref[...] = w_depth_low_ref[...].astype(F32)
    widen_stem_weight(w_in_ref, w_in_wide_ref)
    wide_ref[...] = jnp.zeros_like(wide_ref)
    wide_ref[:, 0:36, 0:96] = band_ref[...].astype(F32)
    turns = (turn_at(0), None, (4 - turn_at(1)) & 3)
    pieces = [(turn, 0, 0, SIDE) + columns for turn, columns in zip(turns, BANDS)]
    gather_patches(pieces, wide_ref, stage_ref, patches_ref)
    send_patches.start()
    for part in range(4):
        stem = dot(patches_ref[part * 192 : (part + 1) * 192, :], w_in_wide_ref[...]) + vectors_ref[0:1, :]
        stem = stem.astype(BF16).astype(F32)
        for half in range(2):
            stem_ref[half, part * 6 : (part + 1) * 6] = stem[
                :, half * LANE : (half + 1) * LANE
            ].reshape(6, 32, LANE)
    send_stem.start()

    def normalise(block, carry):
        normalise_block(
            1 + 4 * block, pl.multiple_of(block * 96, 96), stem_ref, w_depth_ref, vectors_ref,
            normed_ref, inverse_ref, scaled_ref,
        )
        return carry

    lax.fori_loop(0, 4, normalise, 0)

    def mix(block, carry):
        row = pl.multiple_of(block * 96, 96)
        field_ref[pl.ds(row, 96), :] = mix_block(
            4 + 4 * block, row, stem_ref, vectors_ref, w_up_ref, w_down_ref, head_ref,
            scaled_ref, slope_ref, active_ref, hidden_ref,
        )
        return carry

    lax.fori_loop(0, 4, mix, 0)
    for send in sends:
        send.start()
    for send in sends + [send_patches, send_stem]:
        send.wait()


def rim_forward_kernel(
    seam_turns_ref, north_ref, south_ref, w_in_ref, w_depth_ref, vectors_ref, w_up_ref, w_down_ref,
    head_ref, middle_field_ref,
    patches_in, stem_in, normed_in, inverse_in, scaled_in, slope_in, active_in, hidden_in,
    patches_out, stem_out, normed_out, inverse_out, scaled_out, slope_out, active_out, hidden_out,
    field_ref, tight_ref, sent_ref,
    patches_ref, stem_ref, normed_ref, inverse_ref, scaled_ref, slope_ref, active_ref, hidden_ref,
    wide_ref, stage_ref, w_in_wide_ref, sem,
):
    fetches = [
        pltpu.make_async_copy(stem_in.at[:, 3:10], stem_ref.at[:, 3:10], sem.at[0, 0]),
        pltpu.make_async_copy(stem_in.at[:, 20:27], stem_ref.at[:, 10:17], sem.at[0, 1]),
    ]
    for fetch in fetches:
        fetch.start()
    pairs = ((normed_ref, normed_out), (inverse_ref, inverse_out), (scaled_ref, scaled_out),
             (slope_ref, slope_out), (active_ref, active_out), (hidden_ref, hidden_out))
    sends = []
    for k, (here, there) in enumerate(pairs):
        sends.append(pltpu.make_async_copy(here.at[0:96], there.at[0:96], sem.at[1, 2 + k]))
        sends.append(pltpu.make_async_copy(here.at[96:192], there.at[480:576], sem.at[2, 2 + k]))
    early_sends = [
        pltpu.make_async_copy(patches_ref.at[0:96], patches_out.at[0:96], sem.at[1, 0]),
        pltpu.make_async_copy(patches_ref.at[96:192], patches_out.at[864:960], sem.at[2, 0]),
        pltpu.make_async_copy(stem_ref.at[:, 0:3], stem_out.at[:, 0:3], sem.at[1, 1]),
        pltpu.make_async_copy(stem_ref.at[:, 17:20], stem_out.at[:, 27:30], sem.at[2, 1]),
    ]
    turn_at, across = turn_reader(seam_turns_ref)
    widen_stem_weight(w_in_ref, w_in_wide_ref)
    wide_ref[...] = jnp.zeros_like(wide_ref)
    wide_ref[0:5, 0:36, 0:96] = north_ref[...].astype(F32)
    wide_ref[5:10, 0:36, 0:96] = south_ref[...].astype(F32)
    north = (turn_at(-across), None, (4 - turn_at(1 - across)) & 3)
    south = (turn_at(across), None, (4 - turn_at(across + 1)) & 3)
    pieces = [(turn, 0, 0, 3) + columns for turn, columns in zip(north, BANDS)]
    pieces += [(turn, 3, 5, 3) + columns for turn, columns in zip(south, BANDS)]
    gather_patches(pieces, wide_ref, stage_ref, patches_ref)
    stem = dot(patches_ref[...], w_in_wide_ref[...]) + vectors_ref[0:1, :]
    stem = stem.astype(BF16).astype(F32)
    for half in range(2):
        lanes = slice(half * LANE, (half + 1) * LANE)
        stem_ref[half, 0:3] = stem[0:96, lanes].reshape(3, 32, LANE)
        stem_ref[half, 17:20] = stem[96:192, lanes].reshape(3, 32, LANE)
    for send in early_sends:
        send.start()
    for fetch in fetches:
        fetch.wait()

    def normalise(block, carry):
        normalise_block(
            10 * block, pl.multiple_of(block * 96, 96), stem_ref, w_depth_ref, vectors_ref,
            normed_ref, inverse_ref, scaled_ref,
        )
        return carry

    lax.fori_loop(0, 2, normalise, 0)
    field_ref[96:480, :] = middle_field_ref[...]

    def mix(block, carry):
        row = pl.multiple_of(block * 96, 96)
        field_ref[pl.ds(pl.multiple_of(block * 480, 96), 96), :] = mix_block(
            10 * block + 3, row, stem_ref, vectors_ref, w_up_ref, w_down_ref, head_ref,
            scaled_ref, slope_ref, active_ref, hidden_ref,
        )
        return carry

    lax.fori_loop(0, 2, mix, 0)
    for send in sends:
        send.start()
    for quarter in range(4):
        tight_ref[:, 96 * quarter : 96 * (quarter + 1)] = field_ref[
            144 * quarter : 144 * (quarter + 1), :
        ]
    sent = tight_ref[...].astype(BF16)
    for member in range(sent_ref.shape[0]):
        sent_ref[member] = sent
    for send in sends + early_sends:
        send.wait()


def mixer_backward_kernel(
    coefficient,
    every_ref,
    own_ref,
    target_ref,
    hidden_ref,
    head_ref,
    pick_ref,
    active_in,
    slope_in,
    scaled_ref,
    w_down_in,
    w_up_in,
    early_ref,
    out_part_ref,
    hidden_grad_out,
    scaled_grad_out,
    small_ref,
    tight_ref,
    field_ref,
    low_ref,
    up_low_ref,
    up_sum_ref,
    down_ref,
    active_ref,
    slope_ref,
    w_down_ref,
    w_up_ref,
    hidden_grad_ref,
    scaled_grad_ref,
    in_sem,
    out_sem,
):
    fetch_active = pltpu.make_async_copy(active_in, active_ref, in_sem.at[0])
    fetch_slope = pltpu.make_async_copy(slope_in, slope_ref, in_sem.at[1])
    fetch_down = pltpu.make_async_copy(w_down_in, w_down_ref, in_sem.at[2])
    fetch_up = pltpu.make_async_copy(w_up_in, w_up_ref, in_sem.at[3])
    for fetch in (fetch_active, fetch_down, fetch_slope, fetch_up):
        fetch.start()
    send_hidden = pltpu.make_async_copy(hidden_grad_ref, hidden_grad_out, out_sem.at[0])
    send_scaled = pltpu.make_async_copy(scaled_grad_ref, scaled_grad_out, out_sem.at[1])
    members = every_ref.shape[0]
    own = own_ref[...]
    own_sent = own.astype(BF16).astype(F32)
    pair_sum = soft_slope(own_sent - every_ref[0].astype(F32))
    for member in range(1, members):
        pair_sum = pair_sum + soft_slope(own_sent - every_ref[member].astype(F32))
    direct = soft_slope(own - target_ref[...].astype(F32))
    tight_ref[...] = (
        direct * (coefficient / members) - pair_sum * (coefficient / (members * (members - 1)))
    )
    field_ref[...] = jnp.zeros_like(field_ref)
    for quarter in range(4):
        field_ref[144 * quarter : 144 * (quarter + 1), 0:96] = tight_ref[
            :, 96 * quarter : 96 * (quarter + 1)
        ]
    grad_f = field_ref[...]
    grad_b_out = jnp.sum(grad_f, axis=0, keepdims=True)
    grad_f_low = grad_f.astype(BF16)
    picked = dot(grad_f_low, pick_ref[...]).astype(BF16)
    out_part_ref[...] = dot(picked, hidden_ref[...], 0, 0)
    grad_hidden = dot(grad_f_low[:, 0:96], head_ref[...])
    hidden_grad_ref[...] = grad_hidden
    send_hidden.start()
    low_ref[...] = grad_hidden.astype(BF16)
    grad_b_down = jnp.sum(grad_hidden, axis=0, keepdims=True)
    fetch_active.wait()
    down_ref[...] = dot(low_ref[...], active_ref[...], 0, 0)
    up_sum_ref[...] = jnp.zeros_like(up_sum_ref)
    fetch_down.wait()
    fetch_slope.wait()
    fetch_up.wait()

    def widen(part, carry):
        at = pl.ds(pl.multiple_of(part * 96, 96), 96)
        grad_up = dot(low_ref[at, :], w_down_ref[...], 1, 1) * slope_ref[at, :].astype(F32)
        up_sum_ref[...] += jnp.sum(grad_up.reshape(12, 8, 1024), axis=0)
        up_low = grad_up.astype(BF16)
        up_low_ref[at, :] = up_low
        scaled_grad_ref[at, :] = dot(up_low, w_up_ref[...], 1, 1)
        return carry

    lax.fori_loop(0, 6, widen, 0)
    send_scaled.start()
    for chunk in range(4):
        up = dot(up_low_ref[:, chunk * 256 : (chunk + 1) * 256], scaled_ref[...], 0, 0)
        up = up.reshape(8, 4, 8, 256)
        for row_tile in range(4):
            for lane_tile in range(2):
                part = 2 * row_tile + lane_tile
                upper = down_ref[
                    chunk * 64 : (chunk + 1) * 64, part * LANE : (part + 1) * LANE
                ].reshape(8, 8, LANE)
                lower = up[:, row_tile, :, lane_tile * LANE : (lane_tile + 1) * LANE]
                early_ref[part, chunk * 8 : (chunk + 1) * 8] = jnp.concatenate(
                    [upper, lower], axis=1
                ).astype(BF16)
    up_sum = jnp.sum(up_sum_ref[...], axis=0, keepdims=True)
    unit = lax.broadcasted_iota(jnp.int32, (8, 1024), 1)
    row = lax.broadcasted_iota(jnp.int32, (8, 1024), 0)
    spread = jnp.where((unit & 3) == row, jnp.broadcast_to(up_sum, (8, 1024)), 0.0)
    fold = (
        lax.broadcasted_iota(jnp.int32, (1024, 256), 0) >> 2
        == lax.broadcasted_iota(jnp.int32, (1024, 256), 1)
    ).astype(F32).astype(BF16)
    column = lax.broadcasted_iota(jnp.int32, (LANE, 256), 1)
    place = (
        (lax.broadcasted_iota(jnp.int32, (LANE, 256), 0) == 3 * (column >> 3) + (column & 7))
        & ((column & 7) < 3)
    ).astype(F32).astype(BF16)
    b_out = jnp.broadcast_to(grad_b_out, (8, LANE))

    def two_part(values, matrix):
        high = values.astype(BF16)
        rest = (values - high.astype(F32)).astype(BF16)
        return dot(high, matrix) + dot(rest, matrix)

    small_ref[...] = jnp.zeros_like(small_ref)
    small_ref[0:1, :] = grad_b_down
    small_ref[1:5, :] = two_part(spread, fold)[0:4]
    small_ref[5:6, :] = two_part(b_out, place)[0:1]
    send_hidden.wait()
    send_scaled.wait()


def depth_backward_kernel(
    scaled_grad_ref,
    normed_ref,
    inverse_ref,
    vectors_ref,
    hidden_grad_in,
    stem_in,
    w_depth_ref,
    patches_in,
    order_ref,
    early_small_ref,
    out_part_ref,
    late_ref,
    deep_ref,
    stem_grad_ref,
    small_ref,
    sums_ref,
    low_ref,
    tight_ref,
    hidden_grad_ref,
    stem_ref,
    patches_ref,
    in_sem,
):
    fetch_stem = pltpu.make_async_copy(stem_in, stem_ref, in_sem.at[0])
    fetch_hidden = pltpu.make_async_copy(hidden_grad_in, hidden_grad_ref, in_sem.at[1])
    fetch_patches = pltpu.make_async_copy(patches_in, patches_ref, in_sem.at[2])
    for fetch in (fetch_stem, fetch_hidden, fetch_patches):
        fetch.start()
    deep_ref[...] = jnp.zeros_like(deep_ref)
    small_ref[...] = jnp.zeros_like(small_ref)
    sums_ref[...] = jnp.zeros_like(sums_ref)

    def unnormalise(block, carry):
        at = pl.ds(pl.multiple_of(block * 96, 96), 96)
        halves = []
        first = jnp.zeros((96, 1), F32)
        second = jnp.zeros((96, 1), F32)
        for half in range(2):
            lanes = slice(half * LANE, (half + 1) * LANE)
            grad = scaled_grad_ref[at, lanes]
            normed = normed_ref[at, lanes]
            sums_ref[0, :, lanes] += jnp.sum((grad * normed).reshape(12, 8, LANE), axis=0)
            sums_ref[1, :, lanes] += jnp.sum(grad.reshape(12, 8, LANE), axis=0)
            grad = grad * vectors_ref[2:3, lanes]
            first = first + jnp.sum(grad, axis=-1, keepdims=True)
            second = second + jnp.sum(grad * normed, axis=-1, keepdims=True)
            halves.append((grad, normed))
        first = first / 256.0
        second = second / 256.0
        inverse = inverse_ref[at, :]
        for half, (grad, normed) in enumerate(halves):
            lanes = slice(half * LANE, (half + 1) * LANE)
            deep = (grad - first - normed * second) * inverse
            sums_ref[2, :, lanes] += jnp.sum(deep.reshape(12, 8, LANE), axis=0)
            deep_ref[half, pl.ds(6 + block * 4, 4), 8 : 8 + SIDE, :] = deep.reshape(4, SIDE, LANE)
        return carry

    lax.fori_loop(0, 6, unnormalise, 0)
    fetch_stem.wait()
    fetch_hidden.wait()
    for half in range(2):
        lanes = slice(half * LANE, (half + 1) * LANE)

        def spread(block, carry):
            row = block * 3
            total = jnp.zeros((3, 32, LANE), F32)
            for col_off in range(7):
                slab = deep_ref[half, pl.ds(row, 9), 8 - col_off : 40 - col_off, :]
                for row_off in range(7):
                    tap = 7 * row_off + col_off
                    total = total + slab[6 - row_off : 9 - row_off] * w_depth_ref[tap : tap + 1, lanes][None]
            stem_grad_ref[half, pl.ds(row, 3)] = total
            return carry

        lax.fori_loop(0, 10, spread, 0)
        for col_off in range(7):

            def weigh(block, totals):
                row = block * 4
                deep = deep_ref[half, pl.ds(6 + row, 4), 8 : 8 + SIDE, :]
                slab = stem_ref[half, pl.ds(row, 10), col_off : col_off + SIDE, :]
                return tuple(
                    totals[row_off]
                    + jnp.sum((slab[row_off : row_off + 4] * deep).reshape(12, 8, LANE), axis=0)
                    for row_off in range(7)
                )

            totals = lax.fori_loop(0, 6, weigh, tuple(jnp.zeros((8, LANE), F32) for _ in range(7)))
            for row_off in range(7):
                tap = 7 * row_off + col_off
                small_ref[tap : tap + 1, lanes] = jnp.sum(totals[row_off], axis=0, keepdims=True)

        def add_direct(block, carry):
            at = pl.ds(pl.multiple_of(block * 96, 96), 96)
            stem_grad_ref[half, pl.ds(3 + block * 4, 4), 3 : 3 + SIDE, :] += hidden_grad_ref[
                at, lanes
            ].reshape(4, SIDE, LANE)
            return carry

        lax.fori_loop(0, 6, add_direct, 0)
        grad_stem = stem_grad_ref[half].reshape(960, LANE)
        small_ref[52:53, lanes] = jnp.sum(grad_stem, axis=0, keepdims=True)
        low_ref[:, lanes] = grad_stem.astype(BF16)
    small_ref[49:50, :] = jnp.sum(sums_ref[2], axis=0, keepdims=True)
    small_ref[50:51, :] = jnp.sum(sums_ref[0], axis=0, keepdims=True)
    small_ref[51:52, :] = jnp.sum(sums_ref[1], axis=0, keepdims=True)
    small_ref[53:59, :] = early_small_ref[0:6, :]
    fetch_patches.wait()
    order = order_ref[...]
    ordered = dot(low_ref[...], order).astype(BF16)
    wide = dot(ordered, patches_ref[...], 0, 0)
    tight_ref[...] = jnp.zeros_like(tight_ref)
    for offset in range(9):
        tight_ref[:, 96 * offset : 96 * (offset + 1)] = wide[:, LANE * offset : LANE * offset + 96]
    for part in range(8):
        rows = slice(32 * part, 32 * (part + 1))
        for row, at in enumerate((864, 1024, 1056)):
            tight_ref[rows, at : at + 32] = out_part_ref[32 * row : 32 * (row + 1), rows]
    small = small_ref[...]
    high = small.astype(BF16)
    rest = (small - high.astype(F32)).astype(BF16)
    both = jnp.concatenate([high, rest], axis=0)
    tight_ref[:, 896:1024] = dot(order, both, 0, 1)
    late_ref[...] = tight_ref[...].astype(BF16)


def combine_kernel(early_ref, late_ref, share_ref, rows_ref):
    members = early_ref.shape[0]
    early = early_ref[0].astype(F32)
    late = late_ref[0].astype(F32)
    for member in range(1, members):
        early = early + early_ref[member].astype(F32)
        late = late + late_ref[member].astype(F32)
    rows_ref[:, 0:16, :] = early
    for row in range(7):
        rows_ref[:, 16 + row : 17 + row, :] = late[:, row * LANE : (row + 1) * LANE][:, None, :]
    small = late[:, 896 : 896 + SMALL] + late[:, 960 : 960 + SMALL]
    last = jnp.concatenate([small, late[:, 1024:1088]], axis=1)
    rows_ref[:, 23:24, :] = last[:, None, :]
    share_ref[...] = rows_ref[...].astype(BF16)


def total_kernel(share_ref, copies_ref):
    total = share_ref[0].astype(F32)
    for tile in range(1, share_ref.shape[0]):
        total = total + share_ref[tile].astype(F32)
    for member in range(copies_ref.shape[0]):
        copies_ref[member] = total


def unpack_kernel(
    whole_ref, w_in_ref, w_depth_ref, w_up_ref, w_down_ref, w_out_ref, small_ref, b_up_ref
):
    parts = whole_ref.shape[0]
    for part in range(parts):
        for row in range(7):
            lanes = slice(row * LANE, min((row + 1) * LANE, 864))
            w_in_ref[part : part + 1, lanes] = whole_ref[part, 16 + row : 17 + row, 0 : lanes.stop - lanes.start]
        w_down_ref[:, part * LANE : (part + 1) * LANE] = whole_ref[part, 0:8, :]
        row_tile, lane_tile = divmod(part, 2)
        w_up_ref[8 * row_tile : 8 * row_tile + 8, lane_tile * LANE : (lane_tile + 1) * LANE] = whole_ref[
            part, 8:16, :
        ]
        w_depth_ref[part : part + 1, :] = whole_ref[part, 23:24, 0:49]
        lanes = slice(32 * part, 32 * (part + 1))
        w_out_ref[0:1, lanes] = whole_ref[part, 22:23, 96:128]
        w_out_ref[1:2, lanes] = whole_ref[part, 23:24, 64:96]
        w_out_ref[2:3, lanes] = whole_ref[part, 23:24, 96:128]
        b_up_ref[0:1, 4 * part : 4 * part + 4] = whole_ref[part, 23:24, 54:58]
    small = jnp.concatenate([whole_ref[part, 23:24, :] for part in range(parts)], axis=0)
    small_ref[...] = small.T[48:64, :]


def call(kernel, outs, scratch, *operands, spaces=None, vmem=VMEM_BYTES, flops=0, aliases=None):
    kinds = {"v": pltpu.VMEM, "s": pltpu.SMEM, "a": pl.ANY}
    spaces = spaces or "v" * len(operands)
    return pl.pallas_call(
        kernel,
        out_shape=[jax.ShapeDtypeStruct(shape, kind) for shape, kind, _ in outs],
        in_specs=[pl.BlockSpec(memory_space=kinds[letter]) for letter in spaces],
        out_specs=[pl.BlockSpec(memory_space=kinds[letter]) for _, _, letter in outs],
        scratch_shapes=[x if not isinstance(x, tuple) else pltpu.VMEM(*x) for x in scratch],
        input_output_aliases=aliases or {},
        compiler_params=pltpu.CompilerParams(vmem_limit_bytes=vmem),
        cost_estimate=pl.CostEstimate(flops=flops, bytes_accessed=8_000_000, transcendentals=0),
    )(*operands)


def stack_vectors(b_in, b_depth, gain, shift, b_down, head_bias, b_up):
    rows = [b_in, b_depth, gain, shift, b_down, jnp.pad(head_bias, (0, 160)), b_up]
    return jnp.concatenate(rows).astype(F32).reshape(10, 256)


KEPT = (
    ((960, 1152), BF16),
    ((2, 30, 32, LANE), F32),
    ((CELLS, 256), F32),
    ((CELLS, LANE), F32),
    ((CELLS, 256), BF16),
    ((CELLS, 1024), BF16),
    ((CELLS, 1024), BF16),
    ((CELLS, 256), BF16),
)


def forward_scratch(patch_rows, stem_rows, cells, wide_rows, semaphores):
    return [
        ((patch_rows, 1152), BF16),
        ((2, stem_rows, 32, LANE), F32),
        ((cells, 256), F32),
        ((cells, LANE), F32),
        ((cells, 256), BF16),
        ((cells, 1024), BF16),
        ((cells, 1024), BF16),
        ((cells, 256), BF16),
        ((wide_rows, 40, LANE), F32),
        ((patch_rows // 32, 32, LANE), F32),
        ((1152, 256), BF16),
        pltpu.SemaphoreType.DMA(semaphores),
    ]


def run_middle_forward(seam_turns, band, w_in, w_depth, vectors, w_up, w_down, head):
    outs = call(
        middle_forward_kernel,
        [(shape, kind, "a") for shape, kind in KEPT]
        + [((384, 96), F32, "v"), ((49, 256), F32, "v")],
        forward_scratch(768, SIDE, 384, 26, (8,)),
        seam_turns, band, w_in, w_depth, vectors, w_up, w_down, head,
        spaces="svvvvvvv",
        flops=10_000_000_000,
    )
    return outs[:8], outs[8], outs[9]


def run_rim_forward(
    seam_turns, north, south, w_in, w_depth, vectors, w_up, w_down, head, middle_field, kept, members
):
    outs = call(
        rim_forward_kernel,
        [(shape, kind, "a") for shape, kind in KEPT]
        + [((CELLS, 96), F32, "v"), ((144, 384), F32, "v"), ((members, 144, 384), BF16, "v")],
        forward_scratch(192, 20, 192, 10, (3, 8)),
        seam_turns, north, south, w_in, w_depth, vectors, w_up, w_down, head, middle_field, *kept,
        spaces="svvvvvvvvvaaaaaaaa",
        aliases={10 + k: k for k in range(8)},
        flops=5_000_000_000,
    )
    return outs[:8], outs[8], outs[9], outs[10]


def run_mixer_backward(every, tight, target, saved, head, w_down, w_up, coefficient):
    hidden, active, slope, scaled = saved
    column = jnp.arange(96)
    owner = 3 * (column % 32) + column // 32
    pick = (jnp.arange(LANE)[:, None] == owner[None, :]).astype(BF16)
    return call(
        functools.partial(mixer_backward_kernel, coefficient),
        [
            ((8, 32, 16, LANE), BF16, "v"),
            ((96, 256), F32, "v"),
            ((CELLS, 256), F32, "a"),
            ((CELLS, 256), F32, "a"),
            ((8, 256), F32, "v"),
        ],
        [
            ((144, 384), F32),
            ((CELLS, LANE), F32),
            ((CELLS, 256), BF16),
            ((CELLS, 1024), BF16),
            ((8, 1024), F32),
            ((256, 1024), F32),
            ((CELLS, 1024), BF16),
            ((CELLS, 1024), BF16),
            ((1024, 256), BF16),
            ((256, 1024), BF16),
            ((CELLS, 256), F32),
            ((CELLS, 256), F32),
            pltpu.SemaphoreType.DMA((4,)),
            pltpu.SemaphoreType.DMA((2,)),
        ],
        every,
        tight,
        target,
        hidden,
        head,
        pick,
        active,
        slope,
        scaled,
        w_down,
        w_up,
        spaces="vvvvvvaavaa",
        flops=12_000_000_000,
    )


def run_depth_backward(
    scaled_grad, normed, inverse, vectors, hidden_grad, stem, w_depth, patches, early_small, out_part
):
    column = jnp.arange(256)
    order = (column[:, None] == (8 * (column % 32) + column // 32)[None, :]).astype(BF16)
    return call(
        depth_backward_kernel,
        [((256, 1152), BF16, "v")],
        [
            ((2, 36, 40, LANE), F32),
            ((2, 30, 32, LANE), F32),
            ((SMALL, 256), F32),
            ((3, 8, 256), F32),
            ((960, 256), BF16),
            ((256, 1152), F32),
            ((CELLS, 256), F32),
            ((2, 30, 32, LANE), F32),
            ((960, 1152), BF16),
            pltpu.SemaphoreType.DMA((3,)),
        ],
        scaled_grad,
        normed,
        inverse,
        vectors,
        hidden_grad,
        stem,
        w_depth,
        patches,
        order,
        early_small,
        out_part,
        spaces="vvvvaavavvv",
        flops=12_000_000_000,
    )[0]


def run_combine(early, late):
    return call(
        combine_kernel,
        [((32, 24, LANE), BF16, "v")],
        [((32, 24, LANE), F32)],
        early,
        late,
        vmem=SMALL_VMEM_BYTES,
    )[0]


def run_total(share, members):
    return call(total_kernel, [((members, 24, LANE), F32, "v")], [], share, vmem=SMALL_VMEM_BYTES)[0]


def run_unpack(whole):
    shapes = ((8, 864), (8, 49), (32, 256), (8, 1024), (3, 256), (16, 8), (1, 32))
    return call(
        unpack_kernel, [(shape, F32, "v") for shape in shapes], [], whole, vmem=SMALL_VMEM_BYTES
    )


def shifted(value, axis, by):
    peers = lax.axis_size(axis)
    return lax.ppermute(value, axis, [(i, (i + by) % peers) for i in range(peers)])


def turned_edge(tile, turns, width, east):
    size = tile.shape[0]

    def columns(x):
        return x[:, size - width :] if east else x[:, :width]

    sides = (
        columns(tile),
        columns(jnp.rot90(tile, 1)),
        columns(jnp.rot90(tile, 2)),
        columns(jnp.rot90(tile, 3)),
    )
    result = sides[0]
    for quarter in range(1, 4):
        result = jnp.where(turns == quarter, sides[quarter], result)
    return result


def seam_strips(tile, my_turn, next_turn, margin, row_tiles):
    came_west = shifted(turned_edge(tile, next_turn, margin, True), "space", 1)
    came_east = shifted(turned_edge(tile, (4 - my_turn) % 4, margin, False), "space", -1)
    widened = jnp.concatenate([came_west, tile, came_east], axis=1)
    came_north = shifted(widened[-margin:], "space", row_tiles)
    came_south = shifted(widened[:margin], "space", -row_tiles)
    return came_north, widened, came_south


def swap(value, axis):
    return lax.all_to_all(value, axis, 0, 0, tiled=True)


def body(
    initial_state,
    starting_field_nudges,
    verifying_analysis,
    seam_turns,
    w_in,
    b_in,
    w_depth,
    b_depth,
    norm_gain,
    norm_shift,
    w_up,
    b_up,
    w_down,
    b_down,
    head_weight,
    head_bias,
):
    spaces = lax.axis_size("space")
    members = lax.axis_size("ens")
    row_tiles = spaces // 4
    tile_index = lax.axis_index("space")

    def turn_at(offset):
        return lax.dynamic_index_in_dim(seam_turns, (tile_index + offset) % spaces, keepdims=False)

    my_turn = turn_at(0)
    next_turn = turn_at(1)
    source = (
        initial_state.astype(F32) + starting_field_nudges[0].astype(F32)
    ).astype(BF16).reshape(SIDE, SIDE, 96)
    near = jnp.concatenate(seam_strips(source, my_turn, next_turn, 1, row_tiles), axis=0)
    north, band, south = seam_strips(near, my_turn, next_turn, 5, row_tiles)
    vectors = stack_vectors(b_in, b_depth, norm_gain, norm_shift, b_down, head_bias, b_up)
    head = head_weight.T
    kept, middle_field, w_depth_wide = run_middle_forward(
        seam_turns, band, w_in, w_depth, vectors, w_up, w_down, head
    )
    kept, field, tight, sent = run_rim_forward(
        seam_turns, north, south, w_in, w_depth_wide, vectors, w_up, w_down, head, middle_field, kept, members
    )
    patches, stem, normed, inverse, scaled, slope, active, hidden = kept
    sent, verifying_analysis, field_again = lax.optimization_barrier((sent, verifying_analysis, field))
    every = swap(sent, "ens")
    predicted = field_again.reshape(1, SIDE, SIDE * 96)
    target = verifying_analysis.reshape(4, 144, 96).transpose(1, 0, 2).reshape(144, 384)
    coefficient = 1.0 / math.sqrt(spaces * CELLS * 96)
    early, out_part, hidden_grad, scaled_grad, early_small = run_mixer_backward(
        every, tight, target, (hidden, active, slope, scaled), head, w_down, w_up, coefficient
    )
    late = run_depth_backward(
        scaled_grad, normed, inverse, vectors, hidden_grad, stem, w_depth_wide, patches, early_small, out_part
    )
    early_parts, late = lax.optimization_barrier((swap(early, "ens"), late))
    late_parts = swap(late.reshape(8, 32, 1152), "ens")
    shares = swap(run_combine(early_parts, late_parts), "space")
    whole = swap(run_total(shares, members), "ens")
    grad_w_in, grad_w_depth, grad_w_up, grad_w_down, grad_w_out, small, grad_b_up = run_unpack(whole)
    return (
        predicted,
        grad_w_in.T,
        small[4],
        grad_w_depth.T,
        small[1],
        small[2],
        small[3],
        grad_w_up.T,
        grad_b_up[0],
        grad_w_down.T,
        small[5],
        grad_w_out.T,
        small[10, :3],
    )


def solution(mesh):
    return jax.shard_map(
        body,
        mesh=mesh,
        in_specs=(
            P("space", None),
            P("ens", "space", None),
            P("space", None),
            P(),
            P(),
            P(),
            P(),
            P(),
            P(),
            P(),
            P(),
            P(),
            P(),
            P(),
            P(),
            P(),
        ),
        out_specs=(
            P("ens", "space", None),
            P(None, "space"),
            P("space"),
            P(None, "space"),
            P("space"),
            P("space"),
            P("space"),
            P(None, "space"),
            P("space"),
            P(None, "space"),
            P("space"),
            P(None, "space"),
            P("space"),
        ),
        check_vma=False,
    )
```

```python
import functools
import math

import jax
import jax.numpy as jnp
from jax import lax
from jax.experimental import pallas as pl
from jax.experimental.pallas import tpu as pltpu
from jax.sharding import PartitionSpec as P

EPS = 1e-06
CUBIC = 0.044715
ROOT = math.sqrt(2.0 / math.pi)
SOFT_SQUARE = 0.01
F32 = jnp.float32
BF16 = jnp.bfloat16
SIDE = 24
CELLS = SIDE * SIDE
LANE = 128
SMALL = 64
VMEM_BYTES = 56 * 1024 * 1024
SMALL_VMEM_BYTES = 16 * 1024 * 1024


def dot(left, right, left_dim=1, right_dim=0):
    return lax.dot_general(
        left, right, (((left_dim,), (right_dim,)), ((), ())), preferred_element_type=F32
    )


def soft_slope(values):
    return values * lax.rsqrt(values * values + SOFT_SQUARE)


def turned_offset(quarter, row_off, col_off):
    return (
        (row_off, col_off),
        (2 - col_off, row_off),
        (2 - row_off, 2 - col_off),
        (col_off, 2 - row_off),
    )[quarter]


BANDS = ((0, 0, 3), (3, 5, SIDE), (27, 31, 3))


def gather_patches(pieces, wide_ref, stage_ref, patches_ref):
    stage_ref[...] = jnp.zeros_like(stage_ref)
    cells = patches_ref.shape[0]
    for row_off in range(3):
        for col_off in range(3):
            for turn, row_to, row_from, row_len, col_to, col_from, col_len in pieces:

                def read(quarter):
                    row, col = turned_offset(quarter, row_off, col_off)
                    return wide_ref[
                        row_from + row : row_from + row + row_len,
                        col_from + col : col_from + col + col_len,
                        :,
                    ]

                piece = read(0)
                if turn is not None:
                    for quarter in range(1, 4):
                        piece = jnp.where(turn == quarter, read(quarter), piece)
                stage_ref[row_to : row_to + row_len, col_to : col_to + col_len, :] = piece
            at = (3 * row_off + col_off) * LANE
            patches_ref[:, at : at + LANE] = stage_ref[...].reshape(cells, LANE).astype(BF16)


def turn_reader(seam_turns_ref):
    tile = lax.axis_index("space")
    tiles = seam_turns_ref.shape[0]
    return lambda offset: seam_turns_ref[lax.rem(tile + (tiles + offset), tiles)], tiles // 4


def widen_stem_weight(w_in_ref, w_in_wide_ref):
    for offset in range(9):
        w_in_wide_ref[offset * LANE : offset * LANE + 96, :] = w_in_ref[offset * 96 : (offset + 1) * 96, :]
        w_in_wide_ref[offset * LANE + 96 : (offset + 1) * LANE, :] = jnp.zeros((32, 256), BF16)


def normalise_block(slab_row, row, stem_ref, w_depth_ref, vectors_ref, normed_ref, inverse_ref, scaled_ref):
    halves = []
    for half in range(2):
        lanes = slice(half * LANE, (half + 1) * LANE)
        total = jnp.zeros((4, SIDE, LANE), F32)
        for col_off in range(7):
            slab = stem_ref[half, pl.ds(slab_row, 10), col_off : col_off + SIDE, :]
            for row_off in range(7):
                tap = 7 * row_off + col_off
                total = total + slab[row_off : row_off + 4] * w_depth_ref[tap : tap + 1, lanes][None]
        halves.append(total.reshape(4 * SIDE, LANE) + vectors_ref[1:2, lanes])
    mean = (
        jnp.sum(halves[0], axis=-1, keepdims=True) + jnp.sum(halves[1], axis=-1, keepdims=True)
    ) / 256.0
    centers = [h - mean for h in halves]
    spread = (
        jnp.sum(centers[0] * centers[0], axis=-1, keepdims=True)
        + jnp.sum(centers[1] * centers[1], axis=-1, keepdims=True)
    ) / 256.0
    inverse = lax.rsqrt(spread + EPS)
    at = pl.ds(row, 96)
    inverse_ref[at, :] = jnp.broadcast_to(inverse, (96, LANE))
    for half in range(2):
        lanes = slice(half * LANE, (half + 1) * LANE)
        normed = centers[half] * inverse
        normed_ref[at, lanes] = normed
        scaled_ref[at, lanes] = (normed * vectors_ref[2:3, lanes] + vectors_ref[3:4, lanes]).astype(BF16)


def mix_block(
    own_row, row, stem_ref, vectors_ref, w_up_ref, w_down_ref, head_ref,
    scaled_ref, slope_ref, active_ref, hidden_ref,
):
    b_up = jnp.concatenate([vectors_ref[6 + k : 7 + k, :] for k in range(4)], axis=1)
    at = pl.ds(row, 96)
    upward = dot(scaled_ref[at, :], w_up_ref[...]) + b_up
    square = upward * upward
    tanh_part = jnp.tanh(ROOT * (upward + CUBIC * square * upward))
    plus = 0.5 * (1.0 + tanh_part)
    slope = plus + 0.5 * upward * (1.0 - tanh_part * tanh_part) * (ROOT + (3.0 * CUBIC * ROOT) * square)
    slope_ref[at, :] = slope.astype(BF16)
    active = (upward * plus).astype(BF16)
    active_ref[at, :] = active
    own = [
        stem_ref[half, pl.ds(own_row, 4), 3 : 3 + SIDE, :].reshape(96, LANE) for half in range(2)
    ]
    own = jnp.concatenate(own, axis=1)
    hidden = (own + dot(active, w_down_ref[...]) + vectors_ref[4:5, :]).astype(BF16)
    hidden_ref[at, :] = hidden
    return dot(hidden, head_ref[...], 1, 1) + vectors_ref[5:6, 0:96]


def middle_forward_kernel(
    ready, seam_turns_ref, wide_ref, w_in_ref, w_depth_ref, w_up_ref, w_down_ref, head_ref,
    patches_out, stem_out, normed_out, inverse_out, scaled_out, slope_out, active_out, hidden_out,
    field_ref,
    patches_ref, stem_ref, normed_ref, inverse_ref, scaled_ref, slope_ref, active_ref, hidden_ref,
    stage_ref, w_in_wide_ref, sem,
):
    pairs = ((normed_ref, normed_out), (inverse_ref, inverse_out), (scaled_ref, scaled_out),
             (slope_ref, slope_out), (active_ref, active_out), (hidden_ref, hidden_out))
    sends = [pltpu.make_async_copy(a, b.at[96:480], sem.at[2 + k]) for k, (a, b) in enumerate(pairs)]
    send_patches = pltpu.make_async_copy(patches_ref, patches_out.at[96:864], sem.at[0])
    send_stem = pltpu.make_async_copy(stem_ref, stem_out.at[:, 3:27], sem.at[1])
    turn_at, _ = turn_reader(seam_turns_ref)
    vectors_ref = w_depth_ref.at[VECTORS : VECTORS + 16]
    ready()
    widen_stem_weight(w_in_ref, w_in_wide_ref)
    turns = (turn_at(0), None, (4 - turn_at(1)) & 3)
    pieces = [(turn, 0, 0, SIDE) + columns for turn, columns in zip(turns, BANDS)]
    gather_patches(pieces, wide_ref, stage_ref, patches_ref)
    send_patches.start()
    for part in range(4):
        stem = dot(patches_ref[part * 192 : (part + 1) * 192, :], w_in_wide_ref[...]) + vectors_ref[0:1, :]
        stem = stem.astype(BF16).astype(F32)
        for half in range(2):
            stem_ref[half, part * 6 : (part + 1) * 6] = stem[
                :, half * LANE : (half + 1) * LANE
            ].reshape(6, 32, LANE)
    send_stem.start()

    def normalise(block, carry):
        normalise_block(
            1 + 4 * block, pl.multiple_of(block * 96, 96), stem_ref, w_depth_ref, vectors_ref,
            normed_ref, inverse_ref, scaled_ref,
        )
        return carry

    lax.fori_loop(0, 4, normalise, 0)

    def mix(block, carry):
        row = pl.multiple_of(block * 96, 96)
        field_ref[pl.ds(row, 96), :] = mix_block(
            4 + 4 * block, row, stem_ref, vectors_ref, w_up_ref, w_down_ref, head_ref,
            scaled_ref, slope_ref, active_ref, hidden_ref,
        )
        return carry

    lax.fori_loop(0, 4, mix, 0)
    for send in sends:
        send.start()
    return sends + [send_patches, send_stem]


def rim_forward_kernel(
    ready, seam_turns_ref, wide_ref, w_in_ref, w_depth_ref, w_up_ref, w_down_ref,
    head_ref, middle_field_ref,
    patches_in, stem_in, normed_in, inverse_in, scaled_in, slope_in, active_in, hidden_in,
    patches_out, stem_out, normed_out, inverse_out, scaled_out, slope_out, active_out, hidden_out,
    field_ref, tight_ref, sent_ref,
    patches_ref, stem_ref, normed_ref, inverse_ref, scaled_ref, slope_ref, active_ref, hidden_ref,
    stage_ref, w_in_wide_ref, sem,
):
    fetches = [
        pltpu.make_async_copy(stem_in.at[:, 3:10], stem_ref.at[:, 3:10], sem.at[0, 0]),
        pltpu.make_async_copy(stem_in.at[:, 20:27], stem_ref.at[:, 10:17], sem.at[0, 1]),
    ]
    for fetch in fetches:
        fetch.start()
    pairs = ((normed_ref, normed_out), (inverse_ref, inverse_out), (scaled_ref, scaled_out),
             (slope_ref, slope_out), (active_ref, active_out), (hidden_ref, hidden_out))
    sends = []
    for k, (here, there) in enumerate(pairs):
        sends.append(pltpu.make_async_copy(here.at[0:96], there.at[0:96], sem.at[1, 2 + k]))
        sends.append(pltpu.make_async_copy(here.at[96:192], there.at[480:576], sem.at[2, 2 + k]))
    early_sends = [
        pltpu.make_async_copy(patches_ref.at[0:96], patches_out.at[0:96], sem.at[1, 0]),
        pltpu.make_async_copy(patches_ref.at[96:192], patches_out.at[864:960], sem.at[2, 0]),
        pltpu.make_async_copy(stem_ref.at[:, 0:3], stem_out.at[:, 0:3], sem.at[1, 1]),
        pltpu.make_async_copy(stem_ref.at[:, 17:20], stem_out.at[:, 27:30], sem.at[2, 1]),
    ]
    turn_at, across = turn_reader(seam_turns_ref)
    vectors_ref = w_depth_ref.at[VECTORS : VECTORS + 16]
    ready()
    widen_stem_weight(w_in_ref, w_in_wide_ref)
    north = (turn_at(-across), None, (4 - turn_at(1 - across)) & 3)
    south = (turn_at(across), None, (4 - turn_at(across + 1)) & 3)
    pieces = [(turn, 0, 0, 3) + columns for turn, columns in zip(north, BANDS)]
    pieces += [(turn, 3, 5, 3) + columns for turn, columns in zip(south, BANDS)]
    gather_patches(pieces, wide_ref, stage_ref, patches_ref)
    stem = dot(patches_ref[...], w_in_wide_ref[...]) + vectors_ref[0:1, :]
    stem = stem.astype(BF16).astype(F32)
    for half in range(2):
        lanes = slice(half * LANE, (half + 1) * LANE)
        stem_ref[half, 0:3] = stem[0:96, lanes].reshape(3, 32, LANE)
        stem_ref[half, 17:20] = stem[96:192, lanes].reshape(3, 32, LANE)
    for send in early_sends:
        send.start()
    for fetch in fetches:
        fetch.wait()

    def normalise(block, carry):
        normalise_block(
            10 * block, pl.multiple_of(block * 96, 96), stem_ref, w_depth_ref, vectors_ref,
            normed_ref, inverse_ref, scaled_ref,
        )
        return carry

    lax.fori_loop(0, 2, normalise, 0)
    field_ref[96:480, :] = middle_field_ref[...]

    def mix(block, carry):
        row = pl.multiple_of(block * 96, 96)
        field_ref[pl.ds(pl.multiple_of(block * 480, 96), 96), :] = mix_block(
            10 * block + 3, row, stem_ref, vectors_ref, w_up_ref, w_down_ref, head_ref,
            scaled_ref, slope_ref, active_ref, hidden_ref,
        )
        return carry

    lax.fori_loop(0, 2, mix, 0)
    for send in sends:
        send.start()
    for quarter in range(4):
        tight_ref[:, 96 * quarter : 96 * (quarter + 1)] = field_ref[
            144 * quarter : 144 * (quarter + 1), :
        ]
    sent = tight_ref[...].astype(BF16)
    for member in range(sent_ref.shape[0]):
        sent_ref[member] = sent
    return sends + early_sends


def mixer_backward_kernel(
    coefficient,
    ready,
    every_ref,
    own_ref,
    target_ref,
    hidden_ref,
    head_ref,
    pick_ref,
    active_in,
    slope_in,
    scaled_ref,
    w_down_in,
    w_up_in,
    early_ref,
    out_part_ref,
    hidden_grad_out,
    scaled_grad_out,
    small_ref,
    tight_ref,
    field_ref,
    low_ref,
    up_low_ref,
    up_sum_ref,
    down_ref,
    active_ref,
    slope_ref,
    w_down_ref,
    w_up_ref,
    hidden_grad_ref,
    scaled_grad_ref,
    in_sem,
    out_sem,
):
    fetch_active = pltpu.make_async_copy(active_in, active_ref, in_sem.at[0])
    fetch_slope = pltpu.make_async_copy(slope_in, slope_ref, in_sem.at[1])
    fetch_down = pltpu.make_async_copy(w_down_in, w_down_ref, in_sem.at[2])
    fetch_up = pltpu.make_async_copy(w_up_in, w_up_ref, in_sem.at[3])
    for fetch in (fetch_active, fetch_down, fetch_slope, fetch_up):
        fetch.start()
    send_hidden = pltpu.make_async_copy(hidden_grad_ref, hidden_grad_out, out_sem.at[0])
    send_scaled = pltpu.make_async_copy(scaled_grad_ref, scaled_grad_out, out_sem.at[1])
    ready()
    members = every_ref.shape[0]
    own = own_ref[...]
    own_sent = own.astype(BF16).astype(F32)
    pair_sum = soft_slope(own_sent - every_ref[0].astype(F32))
    for member in range(1, members):
        pair_sum = pair_sum + soft_slope(own_sent - every_ref[member].astype(F32))
    direct = soft_slope(own - target_ref[...].astype(F32))
    tight_ref[...] = (
        direct * (coefficient / members) - pair_sum * (coefficient / (members * (members - 1)))
    )
    field_ref[...] = jnp.zeros_like(field_ref)
    for quarter in range(4):
        field_ref[144 * quarter : 144 * (quarter + 1), 0:96] = tight_ref[
            :, 96 * quarter : 96 * (quarter + 1)
        ]
    grad_f = field_ref[...]
    grad_b_out = jnp.sum(grad_f, axis=0, keepdims=True)
    grad_f_low = grad_f.astype(BF16)
    picked = dot(grad_f_low, pick_ref[...]).astype(BF16)
    out_part_ref[...] = dot(picked, hidden_ref[...], 0, 0)
    grad_hidden = dot(grad_f_low[:, 0:96], head_ref[...])
    hidden_grad_ref[...] = grad_hidden
    send_hidden.start()
    low_ref[...] = grad_hidden.astype(BF16)
    grad_b_down = jnp.sum(grad_hidden, axis=0, keepdims=True)
    fetch_active.wait()
    down_ref[...] = dot(low_ref[...], active_ref[...], 0, 0)
    up_sum_ref[...] = jnp.zeros_like(up_sum_ref)
    fetch_down.wait()
    fetch_slope.wait()
    fetch_up.wait()

    def widen(part, carry):
        at = pl.ds(pl.multiple_of(part * 96, 96), 96)
        grad_up = dot(low_ref[at, :], w_down_ref[...], 1, 1) * slope_ref[at, :].astype(F32)
        up_sum_ref[...] += jnp.sum(grad_up.reshape(12, 8, 1024), axis=0)
        up_low = grad_up.astype(BF16)
        up_low_ref[at, :] = up_low
        scaled_grad_ref[at, :] = dot(up_low, w_up_ref[...], 1, 1)
        return carry

    lax.fori_loop(0, 6, widen, 0)
    send_scaled.start()
    for chunk in range(4):
        up = dot(up_low_ref[:, chunk * 256 : (chunk + 1) * 256], scaled_ref[...], 0, 0)
        up = up.reshape(8, 4, 8, 256)
        for row_tile in range(4):
            for lane_tile in range(2):
                part = 2 * row_tile + lane_tile
                upper = down_ref[
                    chunk * 64 : (chunk + 1) * 64, part * LANE : (part + 1) * LANE
                ].reshape(8, 8, LANE)
                lower = up[:, row_tile, :, lane_tile * LANE : (lane_tile + 1) * LANE]
                early_ref[part, chunk * 8 : (chunk + 1) * 8] = jnp.concatenate(
                    [upper, lower], axis=1
                ).astype(BF16)
    up_sum = jnp.sum(up_sum_ref[...], axis=0, keepdims=True)
    unit = lax.broadcasted_iota(jnp.int32, (8, 1024), 1)
    row = lax.broadcasted_iota(jnp.int32, (8, 1024), 0)
    spread = jnp.where((unit & 3) == row, jnp.broadcast_to(up_sum, (8, 1024)), 0.0)
    fold = (
        lax.broadcasted_iota(jnp.int32, (1024, 256), 0) >> 2
        == lax.broadcasted_iota(jnp.int32, (1024, 256), 1)
    ).astype(F32).astype(BF16)
    column = lax.broadcasted_iota(jnp.int32, (LANE, 256), 1)
    place = (
        (lax.broadcasted_iota(jnp.int32, (LANE, 256), 0) == 3 * (column >> 3) + (column & 7))
        & ((column & 7) < 3)
    ).astype(F32).astype(BF16)
    b_out = jnp.broadcast_to(grad_b_out, (8, LANE))

    def two_part(values, matrix):
        high = values.astype(BF16)
        rest = (values - high.astype(F32)).astype(BF16)
        return dot(high, matrix) + dot(rest, matrix)

    small_ref[...] = jnp.zeros_like(small_ref)
    small_ref[0:1, :] = grad_b_down
    small_ref[1:5, :] = two_part(spread, fold)[0:4]
    small_ref[5:6, :] = two_part(b_out, place)[0:1]
    return [send_hidden, send_scaled]


def depth_backward_kernel(
    ready,
    scaled_grad_ref,
    normed_ref,
    inverse_ref,
    hidden_grad_in,
    stem_in,
    w_depth_ref,
    patches_in,
    order_ref,
    early_small_ref,
    out_part_ref,
    late_ref,
    deep_ref,
    stem_grad_ref,
    small_ref,
    sums_ref,
    low_ref,
    tight_ref,
    hidden_grad_ref,
    stem_ref,
    patches_ref,
    in_sem,
):
    fetch_stem = pltpu.make_async_copy(stem_in, stem_ref, in_sem.at[0])
    fetch_hidden = pltpu.make_async_copy(hidden_grad_in, hidden_grad_ref, in_sem.at[1])
    fetch_patches = pltpu.make_async_copy(patches_in, patches_ref, in_sem.at[2])
    for fetch in (fetch_stem, fetch_hidden, fetch_patches):
        fetch.start()
    deep_ref[...] = jnp.zeros_like(deep_ref)
    small_ref[...] = jnp.zeros_like(small_ref)
    sums_ref[...] = jnp.zeros_like(sums_ref)
    vectors_ref = w_depth_ref.at[VECTORS : VECTORS + 16]
    ready()

    def unnormalise(block, carry):
        at = pl.ds(pl.multiple_of(block * 96, 96), 96)
        halves = []
        first = jnp.zeros((96, 1), F32)
        second = jnp.zeros((96, 1), F32)
        for half in range(2):
            lanes = slice(half * LANE, (half + 1) * LANE)
            grad = scaled_grad_ref[at, lanes]
            normed = normed_ref[at, lanes]
            sums_ref[0, :, lanes] += jnp.sum((grad * normed).reshape(12, 8, LANE), axis=0)
            sums_ref[1, :, lanes] += jnp.sum(grad.reshape(12, 8, LANE), axis=0)
            grad = grad * vectors_ref[2:3, lanes]
            first = first + jnp.sum(grad, axis=-1, keepdims=True)
            second = second + jnp.sum(grad * normed, axis=-1, keepdims=True)
            halves.append((grad, normed))
        first = first / 256.0
        second = second / 256.0
        inverse = inverse_ref[at, :]
        for half, (grad, normed) in enumerate(halves):
            lanes = slice(half * LANE, (half + 1) * LANE)
            deep = (grad - first - normed * second) * inverse
            sums_ref[2, :, lanes] += jnp.sum(deep.reshape(12, 8, LANE), axis=0)
            deep_ref[half, pl.ds(6 + block * 4, 4), 8 : 8 + SIDE, :] = deep.reshape(4, SIDE, LANE)
        return carry

    lax.fori_loop(0, 6, unnormalise, 0)
    fetch_stem.wait()
    fetch_hidden.wait()
    for half in range(2):
        lanes = slice(half * LANE, (half + 1) * LANE)

        def spread(block, carry):
            row = block * 3
            total = jnp.zeros((3, 32, LANE), F32)
            for col_off in range(7):
                slab = deep_ref[half, pl.ds(row, 9), 8 - col_off : 40 - col_off, :]
                for row_off in range(7):
                    tap = 7 * row_off + col_off
                    total = total + slab[6 - row_off : 9 - row_off] * w_depth_ref[tap : tap + 1, lanes][None]
            stem_grad_ref[half, pl.ds(row, 3)] = total
            return carry

        lax.fori_loop(0, 10, spread, 0)
        for col_off in range(7):

            def weigh(block, totals):
                row = block * 4
                deep = deep_ref[half, pl.ds(6 + row, 4), 8 : 8 + SIDE, :]
                slab = stem_ref[half, pl.ds(row, 10), col_off : col_off + SIDE, :]
                return tuple(
                    totals[row_off]
                    + jnp.sum((slab[row_off : row_off + 4] * deep).reshape(12, 8, LANE), axis=0)
                    for row_off in range(7)
                )

            totals = lax.fori_loop(0, 6, weigh, tuple(jnp.zeros((8, LANE), F32) for _ in range(7)))
            for row_off in range(7):
                tap = 7 * row_off + col_off
                small_ref[tap : tap + 1, lanes] = jnp.sum(totals[row_off], axis=0, keepdims=True)

        def add_direct(block, carry):
            at = pl.ds(pl.multiple_of(block * 96, 96), 96)
            stem_grad_ref[half, pl.ds(3 + block * 4, 4), 3 : 3 + SIDE, :] += hidden_grad_ref[
                at, lanes
            ].reshape(4, SIDE, LANE)
            return carry

        lax.fori_loop(0, 6, add_direct, 0)
        grad_stem = stem_grad_ref[half].reshape(960, LANE)
        small_ref[52:53, lanes] = jnp.sum(grad_stem, axis=0, keepdims=True)
        low_ref[:, lanes] = grad_stem.astype(BF16)
    small_ref[49:50, :] = jnp.sum(sums_ref[2], axis=0, keepdims=True)
    small_ref[50:51, :] = jnp.sum(sums_ref[0], axis=0, keepdims=True)
    small_ref[51:52, :] = jnp.sum(sums_ref[1], axis=0, keepdims=True)
    small_ref[53:59, :] = early_small_ref[0:6, :]
    fetch_patches.wait()
    order = order_ref[...]
    ordered = dot(low_ref[...], order).astype(BF16)
    wide = dot(ordered, patches_ref[...], 0, 0)
    tight_ref[...] = jnp.zeros_like(tight_ref)
    for offset in range(9):
        tight_ref[:, 96 * offset : 96 * (offset + 1)] = wide[:, LANE * offset : LANE * offset + 96]
    for part in range(8):
        rows = slice(32 * part, 32 * (part + 1))
        for row, at in enumerate((864, 1024, 1056)):
            tight_ref[rows, at : at + 32] = out_part_ref[32 * row : 32 * (row + 1), rows]
    small = small_ref[...]
    high = small.astype(BF16)
    rest = (small - high.astype(F32)).astype(BF16)
    both = jnp.concatenate([high, rest], axis=0)
    tight_ref[:, 896:1024] = dot(order, both, 0, 1)
    late_ref[...] = tight_ref[...].astype(BF16)


def combine_kernel(ready, early_ref, late_ref, share_ref, rows_ref):
    ready()
    members = early_ref.shape[0]
    early = early_ref[0].astype(F32)
    late = late_ref[0].astype(F32)
    for member in range(1, members):
        early = early + early_ref[member].astype(F32)
        late = late + late_ref[member].astype(F32)
    rows_ref[:, 0:16, :] = early
    for row in range(7):
        rows_ref[:, 16 + row : 17 + row, :] = late[:, row * LANE : (row + 1) * LANE][:, None, :]
    small = late[:, 896 : 896 + SMALL] + late[:, 960 : 960 + SMALL]
    last = jnp.concatenate([small, late[:, 1024:1088]], axis=1)
    rows_ref[:, 23:24, :] = last[:, None, :]
    share_ref[...] = rows_ref[...].astype(BF16)


def total_kernel(ready, share_ref, copies_ref):
    ready()
    total = share_ref[0].astype(F32)
    for tile in range(1, share_ref.shape[0]):
        total = total + share_ref[tile].astype(F32)
    for member in range(copies_ref.shape[0]):
        copies_ref[member] = total


def unpack_kernel(
    ready, whole_ref, w_in_ref, w_depth_ref, w_up_ref, w_down_ref, w_out_ref, small_ref, b_up_ref
):
    ready()
    parts = whole_ref.shape[0]
    for part in range(parts):
        for row in range(7):
            lanes = slice(row * LANE, min((row + 1) * LANE, 864))
            w_in_ref[part : part + 1, lanes] = whole_ref[part, 16 + row : 17 + row, 0 : lanes.stop - lanes.start]
        w_down_ref[:, part * LANE : (part + 1) * LANE] = whole_ref[part, 0:8, :]
        row_tile, lane_tile = divmod(part, 2)
        w_up_ref[8 * row_tile : 8 * row_tile + 8, lane_tile * LANE : (lane_tile + 1) * LANE] = whole_ref[
            part, 8:16, :
        ]
        w_depth_ref[part : part + 1, :] = whole_ref[part, 23:24, 0:49]
        lanes = slice(32 * part, 32 * (part + 1))
        w_out_ref[0:1, lanes] = whole_ref[part, 22:23, 96:128]
        w_out_ref[1:2, lanes] = whole_ref[part, 23:24, 64:96]
        w_out_ref[2:3, lanes] = whole_ref[part, 23:24, 96:128]
        b_up_ref[0:1, 4 * part : 4 * part + 4] = whole_ref[part, 23:24, 54:58]
    small = jnp.concatenate([whole_ref[part, 23:24, :] for part in range(parts)], axis=0)
    small_ref[...] = small.T[48:64, :]


def call(kernel, outs, scratch, *operands, spaces=None, vmem=VMEM_BYTES, flops=0, aliases=None):
    spaces = spaces or "v" * len(operands)
    count_in, count_out = len(operands), len(outs)
    copied_in = [k for k in range(count_in) if spaces[k] == "v"]
    copied_out = [k for k in range(count_out) if outs[k][2] == "v"]
    buffers = [pltpu.VMEM(operands[k].shape, operands[k].dtype) for k in copied_in]
    buffers += [pltpu.VMEM(outs[k][0], outs[k][1]) for k in copied_out]
    own = [x if not isinstance(x, tuple) else pltpu.VMEM(*x) for x in scratch]
    semaphores = pltpu.SemaphoreType.DMA((len(buffers),))

    def wrapped(*refs):
        ins, results = list(refs[:count_in]), list(refs[count_in : count_in + count_out])
        rest = refs[count_in + count_out :]
        held, sem, working = rest[: len(buffers)], rest[len(buffers)], rest[len(buffers) + 1 :]
        fetches, sends = [], []
        for place, k in enumerate(copied_in):
            fetches.append(pltpu.make_async_copy(ins[k], held[place], sem.at[place]))
            ins[k] = held[place]
        for place, k in enumerate(copied_out, len(copied_in)):
            sends.append(pltpu.make_async_copy(held[place], results[k], sem.at[place]))
            results[k] = held[place]
        for fetch in fetches:
            fetch.start()

        def ready():
            for fetch in fetches:
                fetch.wait()

        started = kernel(ready, *ins, *results, *working) or []
        for send in sends:
            send.start()
        for send in list(started) + sends:
            send.wait()

    place_of = {"s": pltpu.SMEM, "a": pl.ANY, "v": pl.ANY}
    return pl.pallas_call(
        wrapped,
        out_shape=[jax.ShapeDtypeStruct(shape, kind) for shape, kind, _ in outs],
        in_specs=[pl.BlockSpec(memory_space=place_of[letter]) for letter in spaces],
        out_specs=[pl.BlockSpec(memory_space=pl.ANY)] * count_out,
        scratch_shapes=buffers + [semaphores] + own,
        input_output_aliases=aliases or {},
        compiler_params=pltpu.CompilerParams(vmem_limit_bytes=vmem),
        cost_estimate=pl.CostEstimate(flops=flops, bytes_accessed=8_000_000, transcendentals=0),
    )(*operands)


VECTORS = 56


def stack_params(w_depth, b_in, b_depth, gain, shift, b_down, head_bias, b_up):
    rows = [b_in, b_depth, gain, shift, b_down, jnp.pad(head_bias, (0, 160)), b_up]
    vectors = jnp.concatenate(rows).reshape(10, 256)
    return jnp.concatenate(
        [jnp.pad(w_depth, ((0, VECTORS - 49), (0, 0))), jnp.pad(vectors, ((0, 6), (0, 0)))]
    ).astype(F32)


KEPT = (
    ((960, 1152), BF16),
    ((2, 30, 32, LANE), F32),
    ((CELLS, 256), F32),
    ((CELLS, LANE), F32),
    ((CELLS, 256), BF16),
    ((CELLS, 1024), BF16),
    ((CELLS, 1024), BF16),
    ((CELLS, 256), BF16),
)


def forward_scratch(patch_rows, stem_rows, cells, semaphores):
    return [
        ((patch_rows, 1152), BF16),
        ((2, stem_rows, 32, LANE), F32),
        ((cells, 256), F32),
        ((cells, LANE), F32),
        ((cells, 256), BF16),
        ((cells, 1024), BF16),
        ((cells, 1024), BF16),
        ((cells, 256), BF16),
        ((patch_rows // 32, 32, LANE), F32),
        ((1152, 256), BF16),
        pltpu.SemaphoreType.DMA(semaphores),
    ]


def widened(source):
    return jnp.pad(source, ((0, 0), (0, 4), (0, 32))).astype(F32)


def run_middle_forward(seam_turns, band, w_in, params, w_up, w_down, head):
    outs = call(
        middle_forward_kernel,
        [(shape, kind, "a") for shape, kind in KEPT]
        + [((384, 96), F32, "v")],
        forward_scratch(768, SIDE, 384, (8,)),
        seam_turns, widened(band), w_in, params, w_up, w_down, head,
        spaces="svvvvvv",
        flops=10_000_000_000,
    )
    return outs[:8], outs[8]


def run_rim_forward(
    seam_turns, north, south, w_in, params, w_up, w_down, head, middle_field, kept, members
):
    outs = call(
        rim_forward_kernel,
        [(shape, kind, "a") for shape, kind in KEPT]
        + [((CELLS, 96), F32, "v"), ((144, 384), F32, "v"), ((members, 144, 384), BF16, "v")],
        forward_scratch(192, 20, 192, (3, 8)),
        seam_turns, widened(jnp.concatenate([north, south])), w_in, params, w_up, w_down, head, middle_field, *kept,
        spaces="svvvvvvvaaaaaaaa",
        aliases={8 + k: k for k in range(8)},
        flops=5_000_000_000,
    )
    return outs[:8], outs[8], outs[9], outs[10]


def run_mixer_backward(every, tight, target, saved, head, w_down, w_up, coefficient):
    hidden, active, slope, scaled = saved
    column = jnp.arange(96)
    owner = 3 * (column % 32) + column // 32
    pick = (jnp.arange(LANE)[:, None] == owner[None, :]).astype(BF16)
    return call(
        functools.partial(mixer_backward_kernel, coefficient),
        [
            ((8, 32, 16, LANE), BF16, "v"),
            ((96, 256), F32, "v"),
            ((CELLS, 256), F32, "a"),
            ((CELLS, 256), F32, "a"),
            ((8, 256), F32, "v"),
        ],
        [
            ((144, 384), F32),
            ((CELLS, LANE), F32),
            ((CELLS, 256), BF16),
            ((CELLS, 1024), BF16),
            ((8, 1024), F32),
            ((256, 1024), F32),
            ((CELLS, 1024), BF16),
            ((CELLS, 1024), BF16),
            ((1024, 256), BF16),
            ((256, 1024), BF16),
            ((CELLS, 256), F32),
            ((CELLS, 256), F32),
            pltpu.SemaphoreType.DMA((4,)),
            pltpu.SemaphoreType.DMA((2,)),
        ],
        every,
        tight,
        target,
        hidden,
        head,
        pick,
        active,
        slope,
        scaled,
        w_down,
        w_up,
        spaces="vvvvvvaavaa",
        flops=12_000_000_000,
    )


def run_depth_backward(
    scaled_grad, normed, inverse, hidden_grad, stem, params, patches, early_small, out_part
):
    column = jnp.arange(256)
    order = (column[:, None] == (8 * (column % 32) + column // 32)[None, :]).astype(BF16)
    return call(
        depth_backward_kernel,
        [((256, 1152), BF16, "v")],
        [
            ((2, 36, 40, LANE), F32),
            ((2, 30, 32, LANE), F32),
            ((SMALL, 256), F32),
            ((3, 8, 256), F32),
            ((960, 256), BF16),
            ((256, 1152), F32),
            ((CELLS, 256), F32),
            ((2, 30, 32, LANE), F32),
            ((960, 1152), BF16),
            pltpu.SemaphoreType.DMA((3,)),
        ],
        scaled_grad,
        normed,
        inverse,
        hidden_grad,
        stem,
        params,
        patches,
        order,
        early_small,
        out_part,
        spaces="vvvaavavvv",
        flops=12_000_000_000,
    )[0]


def run_combine(early, late):
    return call(
        combine_kernel,
        [((32, 24, LANE), BF16, "v")],
        [((32, 24, LANE), F32)],
        early,
        late,
        vmem=SMALL_VMEM_BYTES,
    )[0]


def run_total(share, members):
    return call(total_kernel, [((members, 24, LANE), F32, "v")], [], share, vmem=SMALL_VMEM_BYTES)[0]


def run_unpack(whole):
    shapes = ((8, 864), (8, 49), (32, 256), (8, 1024), (3, 256), (16, 8), (1, 32))
    return call(
        unpack_kernel, [(shape, F32, "v") for shape in shapes], [], whole, vmem=SMALL_VMEM_BYTES
    )


def shifted(value, axis, by):
    peers = lax.axis_size(axis)
    return lax.ppermute(value, axis, [(i, (i + by) % peers) for i in range(peers)])


def turned_edge(tile, turns, width, east):
    size = tile.shape[0]

    def columns(x):
        return x[:, size - width :] if east else x[:, :width]

    sides = (
        columns(tile),
        columns(jnp.rot90(tile, 1)),
        columns(jnp.rot90(tile, 2)),
        columns(jnp.rot90(tile, 3)),
    )
    result = sides[0]
    for quarter in range(1, 4):
        result = jnp.where(turns == quarter, sides[quarter], result)
    return result


def seam_strips(tile, my_turn, next_turn, margin, row_tiles):
    came_west = shifted(turned_edge(tile, next_turn, margin, True), "space", 1)
    came_east = shifted(turned_edge(tile, (4 - my_turn) % 4, margin, False), "space", -1)
    widened = jnp.concatenate([came_west, tile, came_east], axis=1)
    came_north = shifted(widened[-margin:], "space", row_tiles)
    came_south = shifted(widened[:margin], "space", -row_tiles)
    return came_north, widened, came_south


def swap(value, axis):
    return lax.all_to_all(value, axis, 0, 0, tiled=True)


def body(
    initial_state,
    starting_field_nudges,
    verifying_analysis,
    seam_turns,
    w_in,
    b_in,
    w_depth,
    b_depth,
    norm_gain,
    norm_shift,
    w_up,
    b_up,
    w_down,
    b_down,
    head_weight,
    head_bias,
):
    spaces = lax.axis_size("space")
    members = lax.axis_size("ens")
    row_tiles = spaces // 4
    tile_index = lax.axis_index("space")

    def turn_at(offset):
        return lax.dynamic_index_in_dim(seam_turns, (tile_index + offset) % spaces, keepdims=False)

    my_turn = turn_at(0)
    next_turn = turn_at(1)
    source = (
        initial_state.astype(F32) + starting_field_nudges[0].astype(F32)
    ).astype(BF16).reshape(SIDE, SIDE, 96)
    near = jnp.concatenate(seam_strips(source, my_turn, next_turn, 1, row_tiles), axis=0)
    north, band, south = seam_strips(near, my_turn, next_turn, 5, row_tiles)
    params = stack_params(w_depth, b_in, b_depth, norm_gain, norm_shift, b_down, head_bias, b_up)
    head = head_weight.T
    kept, middle_field = run_middle_forward(seam_turns, band, w_in, params, w_up, w_down, head)
    kept, field, tight, sent = run_rim_forward(
        seam_turns, north, south, w_in, params, w_up, w_down, head, middle_field, kept, members
    )
    patches, stem, normed, inverse, scaled, slope, active, hidden = kept
    sent, verifying_analysis, field_again = lax.optimization_barrier((sent, verifying_analysis, field))
    every = swap(sent, "ens")
    predicted = field_again.reshape(1, SIDE, SIDE * 96)
    target = verifying_analysis.reshape(4, 144, 96).transpose(1, 0, 2).reshape(144, 384)
    coefficient = 1.0 / math.sqrt(spaces * CELLS * 96)
    early, out_part, hidden_grad, scaled_grad, early_small = run_mixer_backward(
        every, tight, target, (hidden, active, slope, scaled), head, w_down, w_up, coefficient
    )
    late = run_depth_backward(
        scaled_grad, normed, inverse, hidden_grad, stem, params, patches, early_small, out_part
    )
    early_parts, late = lax.optimization_barrier((swap(early, "ens"), late))
    late_parts = swap(late.reshape(8, 32, 1152), "ens")
    shares = swap(run_combine(early_parts, late_parts), "space")
    whole = swap(run_total(shares, members), "ens")
    grad_w_in, grad_w_depth, grad_w_up, grad_w_down, grad_w_out, small, grad_b_up = run_unpack(whole)
    return (
        predicted,
        grad_w_in.T,
        small[4],
        grad_w_depth.T,
        small[1],
        small[2],
        small[3],
        grad_w_up.T,
        grad_b_up[0],
        grad_w_down.T,
        small[5],
        grad_w_out.T,
        small[10, :3],
    )


def solution(mesh):
    return jax.shard_map(
        body,
        mesh=mesh,
        in_specs=(
            P("space", None),
            P("ens", "space", None),
            P("space", None),
            P(),
            P(),
            P(),
            P(),
            P(),
            P(),
            P(),
            P(),
            P(),
            P(),
            P(),
            P(),
            P(),
        ),
        out_specs=(
            P("ens", "space", None),
            P(None, "space"),
            P("space"),
            P(None, "space"),
            P("space"),
            P("space"),
            P("space"),
            P(None, "space"),
            P("space"),
            P(None, "space"),
            P("space"),
            P(None, "space"),
            P("space"),
        ),
        check_vma=False,
    )
```

```python
import functools
import math

import jax
import jax.numpy as jnp
from jax import lax
from jax.experimental import pallas as pl
from jax.experimental.pallas import tpu as pltpu
from jax.sharding import PartitionSpec as P

EPS = 1e-06
CUBIC = 0.044715
ROOT = math.sqrt(2.0 / math.pi)
SOFT_SQUARE = 0.01
F32 = jnp.float32
BF16 = jnp.bfloat16
SIDE = 24
CELLS = SIDE * SIDE
LANE = 128
SMALL = 64
DEEP_ROWS = 4
SPREAD_ROWS = 6
WEIGH_ROWS = 4
VMEM_BYTES = 56 * 1024 * 1024
SMALL_VMEM_BYTES = 16 * 1024 * 1024


def dot(left, right, left_dim=1, right_dim=0):
    return lax.dot_general(
        left, right, (((left_dim,), (right_dim,)), ((), ())), preferred_element_type=F32
    )


def soft_slope(values):
    return values * lax.rsqrt(values * values + SOFT_SQUARE)


def turned_offset(quarter, row_off, col_off):
    return (
        (row_off, col_off),
        (2 - col_off, row_off),
        (2 - row_off, 2 - col_off),
        (col_off, 2 - row_off),
    )[quarter]


BANDS = ((0, 0, 3), (3, 5, SIDE), (27, 31, 3))


def gather_patches(pieces, wide_ref, stage_ref, patches_ref):
    stage_ref[...] = jnp.zeros_like(stage_ref)
    cells = patches_ref.shape[0]
    for row_off in range(3):
        for col_off in range(3):
            for turn, row_to, row_from, row_len, col_to, col_from, col_len in pieces:

                def read(quarter):
                    row, col = turned_offset(quarter, row_off, col_off)
                    return wide_ref[
                        row_from + row : row_from + row + row_len,
                        col_from + col : col_from + col + col_len,
                        :,
                    ]

                piece = read(0)
                if turn is not None:
                    for quarter in range(1, 4):
                        piece = jnp.where(turn == quarter, read(quarter), piece)
                stage_ref[row_to : row_to + row_len, col_to : col_to + col_len, :] = piece
            at = (3 * row_off + col_off) * LANE
            patches_ref[:, at : at + LANE] = stage_ref[...].reshape(cells, LANE).astype(BF16)


def turn_reader(seam_turns_ref):
    tile = lax.axis_index("space")
    tiles = seam_turns_ref.shape[0]
    return lambda offset: seam_turns_ref[lax.rem(tile + (tiles + offset), tiles)], tiles // 4


def widen_stem_weight(w_in_ref, w_in_wide_ref):
    for offset in range(9):
        w_in_wide_ref[offset * LANE : offset * LANE + 96, :] = w_in_ref[offset * 96 : (offset + 1) * 96, :]
        w_in_wide_ref[offset * LANE + 96 : (offset + 1) * LANE, :] = jnp.zeros((32, 256), BF16)


def normalise_block(slab_row, row, stem_ref, w_depth_ref, vectors_ref, normed_ref, inverse_ref, scaled_ref):
    halves = []
    for half in range(2):
        lanes = slice(half * LANE, (half + 1) * LANE)
        parts = []
        for first in range(0, 4, DEEP_ROWS):
            total = jnp.zeros((DEEP_ROWS, SIDE, LANE), F32)
            for col_off in range(7):
                slab = stem_ref[half, pl.ds(slab_row + first, DEEP_ROWS + 6), col_off : col_off + SIDE, :]
                for row_off in range(7):
                    tap = 7 * row_off + col_off
                    total = total + slab[row_off : row_off + DEEP_ROWS] * w_depth_ref[tap : tap + 1, lanes][None]
            parts.append(total.reshape(DEEP_ROWS * SIDE, LANE))
        halves.append(jnp.concatenate(parts, axis=0) + vectors_ref[1:2, lanes])
    mean = (
        jnp.sum(halves[0], axis=-1, keepdims=True) + jnp.sum(halves[1], axis=-1, keepdims=True)
    ) / 256.0
    centers = [h - mean for h in halves]
    spread = (
        jnp.sum(centers[0] * centers[0], axis=-1, keepdims=True)
        + jnp.sum(centers[1] * centers[1], axis=-1, keepdims=True)
    ) / 256.0
    inverse = lax.rsqrt(spread + EPS)
    at = pl.ds(row, 96)
    inverse_ref[at, :] = jnp.broadcast_to(inverse, (96, LANE))
    for half in range(2):
        lanes = slice(half * LANE, (half + 1) * LANE)
        normed = centers[half] * inverse
        normed_ref[at, lanes] = normed
        scaled_ref[at, lanes] = (normed * vectors_ref[2:3, lanes] + vectors_ref[3:4, lanes]).astype(BF16)


def mix_block(
    own_row, row, stem_ref, vectors_ref, w_up_ref, w_down_ref, head_ref,
    scaled_ref, slope_ref, active_ref, hidden_ref,
):
    b_up = jnp.concatenate([vectors_ref[6 + k : 7 + k, :] for k in range(4)], axis=1)
    at = pl.ds(row, 96)
    upward = dot(scaled_ref[at, :], w_up_ref[...]) + b_up
    square = upward * upward
    tanh_part = jnp.tanh(ROOT * (upward + CUBIC * square * upward))
    plus = 0.5 * (1.0 + tanh_part)
    slope = plus + 0.5 * upward * (1.0 - tanh_part * tanh_part) * (ROOT + (3.0 * CUBIC * ROOT) * square)
    slope_ref[at, :] = slope.astype(BF16)
    active = (upward * plus).astype(BF16)
    active_ref[at, :] = active
    own = [
        stem_ref[half, pl.ds(own_row, 4), 3 : 3 + SIDE, :].reshape(96, LANE) for half in range(2)
    ]
    own = jnp.concatenate(own, axis=1)
    hidden = (own + dot(active, w_down_ref[...]) + vectors_ref[4:5, :]).astype(BF16)
    hidden_ref[at, :] = hidden
    return dot(hidden, head_ref[...], 1, 1) + vectors_ref[5:6, 0:96]


def middle_forward_kernel(
    seam_turns_ref, wide_ref, w_in_ref, w_depth_ref, w_up_ref, w_down_ref, head_ref,
    patches_out, stem_out, normed_out, inverse_out, scaled_out, slope_out, active_out, hidden_out,
    field_ref,
    patches_ref, stem_ref, normed_ref, inverse_ref, scaled_ref, slope_ref, active_ref, hidden_ref,
    stage_ref, w_in_wide_ref, sem,
):
    pairs = ((normed_ref, normed_out), (inverse_ref, inverse_out), (scaled_ref, scaled_out),
             (slope_ref, slope_out), (active_ref, active_out), (hidden_ref, hidden_out))
    sends = [pltpu.make_async_copy(a, b.at[96:480], sem.at[2 + k]) for k, (a, b) in enumerate(pairs)]
    send_patches = pltpu.make_async_copy(patches_ref, patches_out.at[96:864], sem.at[0])
    send_stem = pltpu.make_async_copy(stem_ref, stem_out.at[:, 3:27], sem.at[1])
    turn_at, _ = turn_reader(seam_turns_ref)
    vectors_ref = w_depth_ref.at[VECTORS : VECTORS + 16]
    widen_stem_weight(w_in_ref, w_in_wide_ref)
    turns = (turn_at(0), None, (4 - turn_at(1)) & 3)
    pieces = [(turn, 0, 0, SIDE) + columns for turn, columns in zip(turns, BANDS)]
    gather_patches(pieces, wide_ref, stage_ref, patches_ref)
    send_patches.start()
    for part in range(4):
        stem = dot(patches_ref[part * 192 : (part + 1) * 192, :], w_in_wide_ref[...]) + vectors_ref[0:1, :]
        stem = stem.astype(BF16).astype(F32)
        for half in range(2):
            stem_ref[half, part * 6 : (part + 1) * 6] = stem[
                :, half * LANE : (half + 1) * LANE
            ].reshape(6, 32, LANE)
    send_stem.start()

    def normalise(block, carry):
        normalise_block(
            1 + 4 * block, pl.multiple_of(block * 96, 96), stem_ref, w_depth_ref, vectors_ref,
            normed_ref, inverse_ref, scaled_ref,
        )
        return carry

    lax.fori_loop(0, 4, normalise, 0)
    for send in sends[:3]:
        send.start()

    def mix(block, carry):
        row = pl.multiple_of(block * 96, 96)
        field_ref[pl.ds(row, 96), :] = mix_block(
            4 + 4 * block, row, stem_ref, vectors_ref, w_up_ref, w_down_ref, head_ref,
            scaled_ref, slope_ref, active_ref, hidden_ref,
        )
        return carry

    lax.fori_loop(0, 4, mix, 0)
    for send in sends[3:]:
        send.start()
    return sends + [send_patches, send_stem]


def rim_forward_kernel(
    seam_turns_ref, wide_ref, w_in_ref, w_depth_ref, w_up_ref, w_down_ref,
    head_ref, middle_field_ref,
    patches_in, stem_in, normed_in, inverse_in, scaled_in, slope_in, active_in, hidden_in,
    patches_out, stem_out, normed_out, inverse_out, scaled_out, slope_out, active_out, hidden_out,
    field_ref, tight_ref, sent_ref,
    patches_ref, stem_ref, normed_ref, inverse_ref, scaled_ref, slope_ref, active_ref, hidden_ref,
    stage_ref, w_in_wide_ref, sem,
):
    fetches = [
        pltpu.make_async_copy(stem_in.at[:, 3:10], stem_ref.at[:, 3:10], sem.at[0, 0]),
        pltpu.make_async_copy(stem_in.at[:, 20:27], stem_ref.at[:, 10:17], sem.at[0, 1]),
    ]
    for fetch in fetches:
        fetch.start()
    pairs = ((normed_ref, normed_out), (inverse_ref, inverse_out), (scaled_ref, scaled_out),
             (slope_ref, slope_out), (active_ref, active_out), (hidden_ref, hidden_out))
    sends = []
    for k, (here, there) in enumerate(pairs):
        sends.append(pltpu.make_async_copy(here.at[0:96], there.at[0:96], sem.at[1, 2 + k]))
        sends.append(pltpu.make_async_copy(here.at[96:192], there.at[480:576], sem.at[2, 2 + k]))
    early_sends = [
        pltpu.make_async_copy(patches_ref.at[0:96], patches_out.at[0:96], sem.at[1, 0]),
        pltpu.make_async_copy(patches_ref.at[96:192], patches_out.at[864:960], sem.at[2, 0]),
        pltpu.make_async_copy(stem_ref.at[:, 0:3], stem_out.at[:, 0:3], sem.at[1, 1]),
        pltpu.make_async_copy(stem_ref.at[:, 17:20], stem_out.at[:, 27:30], sem.at[2, 1]),
    ]
    turn_at, across = turn_reader(seam_turns_ref)
    vectors_ref = w_depth_ref.at[VECTORS : VECTORS + 16]
    widen_stem_weight(w_in_ref, w_in_wide_ref)
    north = (turn_at(-across), None, (4 - turn_at(1 - across)) & 3)
    south = (turn_at(across), None, (4 - turn_at(across + 1)) & 3)
    pieces = [(turn, 0, 0, 3) + columns for turn, columns in zip(north, BANDS)]
    pieces += [(turn, 3, 5, 3) + columns for turn, columns in zip(south, BANDS)]
    gather_patches(pieces, wide_ref, stage_ref, patches_ref)
    stem = dot(patches_ref[...], w_in_wide_ref[...]) + vectors_ref[0:1, :]
    stem = stem.astype(BF16).astype(F32)
    for half in range(2):
        lanes = slice(half * LANE, (half + 1) * LANE)
        stem_ref[half, 0:3] = stem[0:96, lanes].reshape(3, 32, LANE)
        stem_ref[half, 17:20] = stem[96:192, lanes].reshape(3, 32, LANE)
    for send in early_sends:
        send.start()
    for fetch in fetches:
        fetch.wait()

    def normalise(block, carry):
        normalise_block(
            10 * block, pl.multiple_of(block * 96, 96), stem_ref, w_depth_ref, vectors_ref,
            normed_ref, inverse_ref, scaled_ref,
        )
        return carry

    lax.fori_loop(0, 2, normalise, 0)
    for send in sends[:6]:
        send.start()
    field_ref[96:480, :] = middle_field_ref[...]

    def mix(block, carry):
        row = pl.multiple_of(block * 96, 96)
        field_ref[pl.ds(pl.multiple_of(block * 480, 96), 96), :] = mix_block(
            10 * block + 3, row, stem_ref, vectors_ref, w_up_ref, w_down_ref, head_ref,
            scaled_ref, slope_ref, active_ref, hidden_ref,
        )
        return carry

    lax.fori_loop(0, 2, mix, 0)
    for send in sends[6:]:
        send.start()
    for quarter in range(4):
        tight_ref[:, 96 * quarter : 96 * (quarter + 1)] = field_ref[
            144 * quarter : 144 * (quarter + 1), :
        ]
    sent = tight_ref[...].astype(BF16)
    for member in range(sent_ref.shape[0]):
        sent_ref[member] = sent
    return sends + early_sends


def mixer_backward_kernel(
    coefficient,
    every_ref,
    own_ref,
    target_ref,
    hidden_ref,
    head_ref,
    pick_ref,
    active_in,
    slope_in,
    scaled_ref,
    w_down_in,
    w_up_in,
    early_ref,
    out_part_ref,
    hidden_grad_out,
    scaled_grad_out,
    small_ref,
    tight_ref,
    field_ref,
    low_ref,
    up_low_ref,
    up_sum_ref,
    down_ref,
    active_ref,
    slope_ref,
    w_down_ref,
    w_up_ref,
    hidden_grad_ref,
    scaled_grad_ref,
    in_sem,
    out_sem,
):
    fetch_active = pltpu.make_async_copy(active_in, active_ref, in_sem.at[0])
    fetch_slope = pltpu.make_async_copy(slope_in, slope_ref, in_sem.at[1])
    fetch_down = pltpu.make_async_copy(w_down_in, w_down_ref, in_sem.at[2])
    fetch_up = pltpu.make_async_copy(w_up_in, w_up_ref, in_sem.at[3])
    for fetch in (fetch_active, fetch_down, fetch_slope, fetch_up):
        fetch.start()
    send_hidden = pltpu.make_async_copy(hidden_grad_ref, hidden_grad_out, out_sem.at[0])
    send_scaled = pltpu.make_async_copy(scaled_grad_ref, scaled_grad_out, out_sem.at[1])
    members = every_ref.shape[0]
    own = own_ref[...]
    own_sent = own.astype(BF16).astype(F32)
    pair_sum = soft_slope(own_sent - every_ref[0].astype(F32))
    for member in range(1, members):
        pair_sum = pair_sum + soft_slope(own_sent - every_ref[member].astype(F32))
    direct = soft_slope(own - target_ref[...].astype(F32))
    tight_ref[...] = (
        direct * (coefficient / members) - pair_sum * (coefficient / (members * (members - 1)))
    )
    field_ref[...] = jnp.zeros_like(field_ref)
    for quarter in range(4):
        field_ref[144 * quarter : 144 * (quarter + 1), 0:96] = tight_ref[
            :, 96 * quarter : 96 * (quarter + 1)
        ]
    grad_f = field_ref[...]
    grad_b_out = jnp.sum(grad_f, axis=0, keepdims=True)
    grad_f_low = grad_f.astype(BF16)
    picked = dot(grad_f_low, pick_ref[...]).astype(BF16)
    out_part_ref[...] = dot(picked, hidden_ref[...], 0, 0)
    grad_hidden = dot(grad_f_low[:, 0:96], head_ref[...])
    hidden_grad_ref[...] = grad_hidden
    send_hidden.start()
    low_ref[...] = grad_hidden.astype(BF16)
    grad_b_down = jnp.sum(grad_hidden, axis=0, keepdims=True)
    fetch_active.wait()
    down_ref[...] = dot(low_ref[...], active_ref[...], 0, 0)
    up_sum_ref[...] = jnp.zeros_like(up_sum_ref)
    fetch_down.wait()
    fetch_slope.wait()
    fetch_up.wait()

    def widen(part, carry):
        at = pl.ds(pl.multiple_of(part * 96, 96), 96)
        grad_up = dot(low_ref[at, :], w_down_ref[...], 1, 1) * slope_ref[at, :].astype(F32)
        up_sum_ref[...] += jnp.sum(grad_up.reshape(12, 8, 1024), axis=0)
        up_low = grad_up.astype(BF16)
        up_low_ref[at, :] = up_low
        scaled_grad_ref[at, :] = dot(up_low, w_up_ref[...], 1, 1)
        return carry

    lax.fori_loop(0, 6, widen, 0)
    send_scaled.start()
    for chunk in range(4):
        up = dot(up_low_ref[:, chunk * 256 : (chunk + 1) * 256], scaled_ref[...], 0, 0)
        up = up.reshape(8, 4, 8, 256)
        for row_tile in range(4):
            for lane_tile in range(2):
                part = 2 * row_tile + lane_tile
                upper = down_ref[
                    chunk * 64 : (chunk + 1) * 64, part * LANE : (part + 1) * LANE
                ].reshape(8, 8, LANE)
                lower = up[:, row_tile, :, lane_tile * LANE : (lane_tile + 1) * LANE]
                early_ref[part, chunk * 8 : (chunk + 1) * 8] = jnp.concatenate(
                    [upper, lower], axis=1
                ).astype(BF16)
    up_sum = jnp.sum(up_sum_ref[...], axis=0, keepdims=True)
    unit = lax.broadcasted_iota(jnp.int32, (8, 1024), 1)
    row = lax.broadcasted_iota(jnp.int32, (8, 1024), 0)
    spread = jnp.where((unit & 3) == row, jnp.broadcast_to(up_sum, (8, 1024)), 0.0)
    fold = (
        lax.broadcasted_iota(jnp.int32, (1024, 256), 0) >> 2
        == lax.broadcasted_iota(jnp.int32, (1024, 256), 1)
    ).astype(F32).astype(BF16)
    column = lax.broadcasted_iota(jnp.int32, (LANE, 256), 1)
    place = (
        (lax.broadcasted_iota(jnp.int32, (LANE, 256), 0) == 3 * (column >> 3) + (column & 7))
        & ((column & 7) < 3)
    ).astype(F32).astype(BF16)
    b_out = jnp.broadcast_to(grad_b_out, (8, LANE))

    def two_part(values, matrix):
        high = values.astype(BF16)
        rest = (values - high.astype(F32)).astype(BF16)
        return dot(high, matrix) + dot(rest, matrix)

    small_ref[...] = jnp.zeros_like(small_ref)
    small_ref[0:1, :] = grad_b_down
    small_ref[1:5, :] = two_part(spread, fold)[0:4]
    small_ref[5:6, :] = two_part(b_out, place)[0:1]
    return [send_hidden, send_scaled]


def depth_backward_kernel(
    scaled_grad_ref,
    normed_ref,
    inverse_ref,
    hidden_grad_in,
    stem_in,
    w_depth_ref,
    patches_in,
    order_ref,
    early_small_ref,
    out_part_ref,
    late_ref,
    deep_ref,
    stem_grad_ref,
    small_ref,
    sums_ref,
    low_ref,
    tight_ref,
    hidden_grad_ref,
    stem_ref,
    patches_ref,
    in_sem,
):
    fetch_stem = pltpu.make_async_copy(stem_in, stem_ref, in_sem.at[0])
    fetch_hidden = pltpu.make_async_copy(hidden_grad_in, hidden_grad_ref, in_sem.at[1])
    fetch_patches = pltpu.make_async_copy(patches_in, patches_ref, in_sem.at[2])
    for fetch in (fetch_stem, fetch_hidden, fetch_patches):
        fetch.start()
    deep_ref[...] = jnp.zeros_like(deep_ref)
    small_ref[...] = jnp.zeros_like(small_ref)
    sums_ref[...] = jnp.zeros_like(sums_ref)
    vectors_ref = w_depth_ref.at[VECTORS : VECTORS + 16]

    def unnormalise(block, carry):
        at = pl.ds(pl.multiple_of(block * 96, 96), 96)
        halves = []
        first = jnp.zeros((96, 1), F32)
        second = jnp.zeros((96, 1), F32)
        for half in range(2):
            lanes = slice(half * LANE, (half + 1) * LANE)
            grad = scaled_grad_ref[at, lanes]
            normed = normed_ref[at, lanes]
            sums_ref[0, :, lanes] += jnp.sum((grad * normed).reshape(12, 8, LANE), axis=0)
            sums_ref[1, :, lanes] += jnp.sum(grad.reshape(12, 8, LANE), axis=0)
            grad = grad * vectors_ref[2:3, lanes]
            first = first + jnp.sum(grad, axis=-1, keepdims=True)
            second = second + jnp.sum(grad * normed, axis=-1, keepdims=True)
            halves.append((grad, normed))
        first = first / 256.0
        second = second / 256.0
        inverse = inverse_ref[at, :]
        for half, (grad, normed) in enumerate(halves):
            lanes = slice(half * LANE, (half + 1) * LANE)
            deep = (grad - first - normed * second) * inverse
            sums_ref[2, :, lanes] += jnp.sum(deep.reshape(12, 8, LANE), axis=0)
            deep_ref[half, pl.ds(6 + block * 4, 4), 8 : 8 + SIDE, :] = deep.reshape(4, SIDE, LANE)
        return carry

    lax.fori_loop(0, 6, unnormalise, 0)
    fetch_stem.wait()
    fetch_hidden.wait()
    for half in range(2):
        lanes = slice(half * LANE, (half + 1) * LANE)

        def spread(block, carry):
            row = block * SPREAD_ROWS
            total = jnp.zeros((SPREAD_ROWS, 32, LANE), F32)
            for col_off in range(7):
                slab = deep_ref[half, pl.ds(row, SPREAD_ROWS + 6), 8 - col_off : 40 - col_off, :]
                for row_off in range(7):
                    tap = 7 * row_off + col_off
                    total = total + slab[6 - row_off : 6 - row_off + SPREAD_ROWS] * w_depth_ref[tap : tap + 1, lanes][None]
            stem_grad_ref[half, pl.ds(row, SPREAD_ROWS)] = total
            return carry

        lax.fori_loop(0, 30 // SPREAD_ROWS, spread, 0)
        for col_off in range(7):

            def weigh(block, totals):
                row = block * WEIGH_ROWS
                deep = deep_ref[half, pl.ds(6 + row, WEIGH_ROWS), 8 : 8 + SIDE, :]
                slab = stem_ref[half, pl.ds(row, WEIGH_ROWS + 6), col_off : col_off + SIDE, :]
                return tuple(
                    totals[row_off]
                    + jnp.sum(
                        (slab[row_off : row_off + WEIGH_ROWS] * deep).reshape(3 * WEIGH_ROWS, 8, LANE), axis=0
                    )
                    for row_off in range(7)
                )

            totals = lax.fori_loop(0, SIDE // WEIGH_ROWS, weigh, tuple(jnp.zeros((8, LANE), F32) for _ in range(7)))
            for row_off in range(7):
                tap = 7 * row_off + col_off
                small_ref[tap : tap + 1, lanes] = jnp.sum(totals[row_off], axis=0, keepdims=True)

        def add_direct(block, carry):
            at = pl.ds(pl.multiple_of(block * 96, 96), 96)
            stem_grad_ref[half, pl.ds(3 + block * 4, 4), 3 : 3 + SIDE, :] += hidden_grad_ref[
                at, lanes
            ].reshape(4, SIDE, LANE)
            return carry

        lax.fori_loop(0, 6, add_direct, 0)
        grad_stem = stem_grad_ref[half].reshape(960, LANE)
        small_ref[52:53, lanes] = jnp.sum(grad_stem, axis=0, keepdims=True)
        low_ref[:, lanes] = grad_stem.astype(BF16)
    small_ref[49:50, :] = jnp.sum(sums_ref[2], axis=0, keepdims=True)
    small_ref[50:51, :] = jnp.sum(sums_ref[0], axis=0, keepdims=True)
    small_ref[51:52, :] = jnp.sum(sums_ref[1], axis=0, keepdims=True)
    small_ref[53:59, :] = early_small_ref[0:6, :]
    fetch_patches.wait()
    order = order_ref[...]
    ordered = dot(low_ref[...], order).astype(BF16)
    wide = dot(ordered, patches_ref[...], 0, 0)
    tight_ref[...] = jnp.zeros_like(tight_ref)
    for offset in range(9):
        tight_ref[:, 96 * offset : 96 * (offset + 1)] = wide[:, LANE * offset : LANE * offset + 96]
    for part in range(8):
        rows = slice(32 * part, 32 * (part + 1))
        for row, at in enumerate((864, 1024, 1056)):
            tight_ref[rows, at : at + 32] = out_part_ref[32 * row : 32 * (row + 1), rows]
    small = small_ref[...]
    high = small.astype(BF16)
    rest = (small - high.astype(F32)).astype(BF16)
    both = jnp.concatenate([high, rest], axis=0)
    tight_ref[:, 896:1024] = dot(order, both, 0, 1)
    late_ref[...] = tight_ref[...].astype(BF16)


def combine_kernel(early_ref, late_ref, share_ref, rows_ref):
    members = early_ref.shape[0]
    early = early_ref[0].astype(F32)
    late = late_ref[0].astype(F32)
    for member in range(1, members):
        early = early + early_ref[member].astype(F32)
        late = late + late_ref[member].astype(F32)
    rows_ref[:, 0:16, :] = early
    for row in range(7):
        rows_ref[:, 16 + row : 17 + row, :] = late[:, row * LANE : (row + 1) * LANE][:, None, :]
    small = late[:, 896 : 896 + SMALL] + late[:, 960 : 960 + SMALL]
    last = jnp.concatenate([small, late[:, 1024:1088]], axis=1)
    rows_ref[:, 23:24, :] = last[:, None, :]
    share_ref[...] = rows_ref[...].astype(BF16)


def total_kernel(share_ref, copies_ref):
    total = share_ref[0].astype(F32)
    for tile in range(1, share_ref.shape[0]):
        total = total + share_ref[tile].astype(F32)
    for member in range(copies_ref.shape[0]):
        copies_ref[member] = total


def unpack_kernel(
    whole_ref, w_in_ref, w_depth_ref, w_up_ref, w_down_ref, w_out_ref, small_ref, b_up_ref
):
    parts = whole_ref.shape[0]
    for part in range(parts):
        for row in range(7):
            lanes = slice(row * LANE, min((row + 1) * LANE, 864))
            w_in_ref[part : part + 1, lanes] = whole_ref[part, 16 + row : 17 + row, 0 : lanes.stop - lanes.start]
        w_down_ref[:, part * LANE : (part + 1) * LANE] = whole_ref[part, 0:8, :]
        row_tile, lane_tile = divmod(part, 2)
        w_up_ref[8 * row_tile : 8 * row_tile + 8, lane_tile * LANE : (lane_tile + 1) * LANE] = whole_ref[
            part, 8:16, :
        ]
        w_depth_ref[part : part + 1, :] = whole_ref[part, 23:24, 0:49]
        lanes = slice(32 * part, 32 * (part + 1))
        w_out_ref[0:1, lanes] = whole_ref[part, 22:23, 96:128]
        w_out_ref[1:2, lanes] = whole_ref[part, 23:24, 64:96]
        w_out_ref[2:3, lanes] = whole_ref[part, 23:24, 96:128]
        b_up_ref[0:1, 4 * part : 4 * part + 4] = whole_ref[part, 23:24, 54:58]
    small = jnp.concatenate([whole_ref[part, 23:24, :] for part in range(parts)], axis=0)
    small_ref[...] = small.T[48:64, :]


def call(kernel, outs, scratch, *operands, spaces=None, vmem=VMEM_BYTES, flops=0, aliases=None):
    kinds = {"v": pltpu.VMEM, "s": pltpu.SMEM, "a": pl.ANY}

    def wrapped(*refs):
        for send in kernel(*refs) or ():
            send.wait()

    return pl.pallas_call(
        wrapped,
        out_shape=[jax.ShapeDtypeStruct(shape, kind) for shape, kind, _ in outs],
        in_specs=[pl.BlockSpec(memory_space=kinds[k]) for k in spaces or "v" * len(operands)],
        out_specs=[pl.BlockSpec(memory_space=kinds[k]) for _, _, k in outs],
        scratch_shapes=[x if not isinstance(x, tuple) else pltpu.VMEM(*x) for x in scratch],
        input_output_aliases=aliases or {},
        compiler_params=pltpu.CompilerParams(vmem_limit_bytes=vmem),
        cost_estimate=pl.CostEstimate(flops=flops, bytes_accessed=8_000_000, transcendentals=0),
    )(*operands)


VECTORS = 56


def stack_params(w_depth, b_in, b_depth, gain, shift, b_down, head_bias, b_up):
    rows = [b_in, b_depth, gain, shift, b_down, jnp.pad(head_bias, (0, 160)), b_up]
    vectors = jnp.concatenate(rows).reshape(10, 256)
    return jnp.concatenate(
        [jnp.pad(w_depth, ((0, VECTORS - 49), (0, 0))), jnp.pad(vectors, ((0, 6), (0, 0)))]
    ).astype(F32)


KEPT = (
    ((960, 1152), BF16),
    ((2, 30, 32, LANE), F32),
    ((CELLS, 256), F32),
    ((CELLS, LANE), F32),
    ((CELLS, 256), BF16),
    ((CELLS, 1024), BF16),
    ((CELLS, 1024), BF16),
    ((CELLS, 256), BF16),
)


def forward_scratch(patch_rows, stem_rows, cells, semaphores):
    return [
        ((patch_rows, 1152), BF16),
        ((2, stem_rows, 32, LANE), F32),
        ((cells, 256), F32),
        ((cells, LANE), F32),
        ((cells, 256), BF16),
        ((cells, 1024), BF16),
        ((cells, 1024), BF16),
        ((cells, 256), BF16),
        ((patch_rows // 32, 32, LANE), F32),
        ((1152, 256), BF16),
        pltpu.SemaphoreType.DMA(semaphores),
    ]


def widened(source):
    return jnp.pad(source, ((0, 0), (0, 4), (0, 32))).astype(F32)


def run_middle_forward(seam_turns, band, w_in, params, w_up, w_down, head):
    outs = call(
        middle_forward_kernel,
        [(shape, kind, "a") for shape, kind in KEPT]
        + [((384, 96), F32, "v")],
        forward_scratch(768, SIDE, 384, (8,)),
        seam_turns, widened(band), w_in, params, w_up, w_down, head,
        spaces="svvvvvv",
        flops=10_000_000_000,
    )
    return outs[:8], outs[8]


def run_rim_forward(
    seam_turns, north, south, w_in, params, w_up, w_down, head, middle_field, kept, members
):
    outs = call(
        rim_forward_kernel,
        [(shape, kind, "a") for shape, kind in KEPT]
        + [((CELLS, 96), F32, "v"), ((144, 384), F32, "v"), ((members, 144, 384), BF16, "v")],
        forward_scratch(192, 20, 192, (3, 8)),
        seam_turns, widened(jnp.concatenate([north, south])), w_in, params, w_up, w_down, head, middle_field, *kept,
        spaces="svvvvvvvaaaaaaaa",
        aliases={8 + k: k for k in range(8)},
        flops=5_000_000_000,
    )
    return outs[:8], outs[8], outs[9], outs[10]


def run_mixer_backward(every, tight, target, saved, head, w_down, w_up, coefficient):
    hidden, active, slope, scaled = saved
    column = jnp.arange(96)
    owner = 3 * (column % 32) + column // 32
    pick = (jnp.arange(LANE)[:, None] == owner[None, :]).astype(BF16)
    return call(
        functools.partial(mixer_backward_kernel, coefficient),
        [
            ((8, 32, 16, LANE), BF16, "v"),
            ((96, 256), F32, "v"),
            ((CELLS, 256), F32, "a"),
            ((CELLS, 256), F32, "a"),
            ((8, 256), F32, "v"),
        ],
        [
            ((144, 384), F32),
            ((CELLS, LANE), F32),
            ((CELLS, 256), BF16),
            ((CELLS, 1024), BF16),
            ((8, 1024), F32),
            ((256, 1024), F32),
            ((CELLS, 1024), BF16),
            ((CELLS, 1024), BF16),
            ((1024, 256), BF16),
            ((256, 1024), BF16),
            ((CELLS, 256), F32),
            ((CELLS, 256), F32),
            pltpu.SemaphoreType.DMA((4,)),
            pltpu.SemaphoreType.DMA((2,)),
        ],
        every,
        tight,
        target,
        hidden,
        head,
        pick,
        active,
        slope,
        scaled,
        w_down,
        w_up,
        spaces="vvvvvvaavaa",
        flops=12_000_000_000,
    )


def run_depth_backward(
    scaled_grad, normed, inverse, hidden_grad, stem, params, patches, early_small, out_part
):
    column = jnp.arange(256)
    order = (column[:, None] == (8 * (column % 32) + column // 32)[None, :]).astype(BF16)
    return call(
        depth_backward_kernel,
        [((256, 1152), BF16, "v")],
        [
            ((2, 36, 40, LANE), F32),
            ((2, 30, 32, LANE), F32),
            ((SMALL, 256), F32),
            ((3, 8, 256), F32),
            ((960, 256), BF16),
            ((256, 1152), F32),
            ((CELLS, 256), F32),
            ((2, 30, 32, LANE), F32),
            ((960, 1152), BF16),
            pltpu.SemaphoreType.DMA((3,)),
        ],
        scaled_grad,
        normed,
        inverse,
        hidden_grad,
        stem,
        params,
        patches,
        order,
        early_small,
        out_part,
        spaces="vvvaavavvv",
        flops=12_000_000_000,
    )[0]


def run_combine(early, late):
    return call(
        combine_kernel,
        [((32, 24, LANE), BF16, "v")],
        [((32, 24, LANE), F32)],
        early,
        late,
        vmem=SMALL_VMEM_BYTES,
    )[0]


def run_total(share, members):
    return call(total_kernel, [((members, 24, LANE), F32, "v")], [], share, vmem=SMALL_VMEM_BYTES)[0]


def run_unpack(whole):
    shapes = ((8, 864), (8, 49), (32, 256), (8, 1024), (3, 256), (16, 8), (1, 32))
    return call(
        unpack_kernel, [(shape, F32, "v") for shape in shapes], [], whole, vmem=SMALL_VMEM_BYTES
    )


def shifted(value, axis, by):
    peers = lax.axis_size(axis)
    return lax.ppermute(value, axis, [(i, (i + by) % peers) for i in range(peers)])


def turned_edge(tile, turns, width, east):
    size = tile.shape[0]

    def columns(x):
        return x[:, size - width :] if east else x[:, :width]

    sides = (
        columns(tile),
        columns(jnp.rot90(tile, 1)),
        columns(jnp.rot90(tile, 2)),
        columns(jnp.rot90(tile, 3)),
    )
    result = sides[0]
    for quarter in range(1, 4):
        result = jnp.where(turns == quarter, sides[quarter], result)
    return result


def turned_side(rows, turns, east):
    size = rows.shape[0]
    width = rows.shape[1] // size
    west_side, east_side = rows[:, :width], rows[:, -width:]
    north_side, south_side = rows[0].reshape(size, width), rows[-1].reshape(size, width)
    if east:
        sides = (east_side, south_side[::-1], west_side[::-1], north_side)
    else:
        sides = (west_side, north_side[::-1], east_side[::-1], south_side)
    result = sides[0]
    for quarter in range(1, 4):
        result = jnp.where(turns == quarter, sides[quarter], result)
    return result[:, None]


def near_source(rows, my_turn, next_turn, row_tiles):
    tile = rows.reshape(SIDE, SIDE, -1)
    came_west = shifted(turned_side(rows, next_turn, True), "space", 1)
    came_east = shifted(turned_side(rows, (4 - my_turn) % 4, False), "space", -1)
    widened_rows = jnp.concatenate([came_west, tile, came_east], axis=1)
    came_north = shifted(widened_rows[-1:], "space", row_tiles)
    came_south = shifted(widened_rows[:1], "space", -row_tiles)
    return jnp.concatenate([came_north, widened_rows, came_south], axis=0)


def widened_band(near, my_turn, next_turn, margin):
    came_west = shifted(turned_edge(near, next_turn, margin, True), "space", 1)
    came_east = shifted(turned_edge(near, (4 - my_turn) % 4, margin, False), "space", -1)
    return jnp.concatenate([came_west, near, came_east], axis=1)


def exchange_rows(band, margin, tile_index, spaces):
    row_tiles = spaces // 4
    place = tile_index // row_tiles
    to_south = (jnp.arange(4) == (place + 1) % 4)[:, None, None, None]
    parts = jnp.where(to_south, band[None, -margin:], band[None, :margin])
    columns = [[column + row_tiles * k for k in range(4)] for column in range(row_tiles)]
    came = lax.all_to_all(parts, "space", 0, 0, axis_index_groups=columns, tiled=True)
    north = lax.dynamic_index_in_dim(came, (place + 3) % 4, keepdims=False)
    south = lax.dynamic_index_in_dim(came, (place + 1) % 4, keepdims=False)
    return north, south


def swap(value, axis):
    return lax.all_to_all(value, axis, 0, 0, tiled=True)


def body(
    initial_state,
    starting_field_nudges,
    verifying_analysis,
    seam_turns,
    w_in,
    b_in,
    w_depth,
    b_depth,
    norm_gain,
    norm_shift,
    w_up,
    b_up,
    w_down,
    b_down,
    head_weight,
    head_bias,
):
    spaces = lax.axis_size("space")
    members = lax.axis_size("ens")
    row_tiles = spaces // 4
    tile_index = lax.axis_index("space")

    def turn_at(offset):
        return lax.dynamic_index_in_dim(seam_turns, (tile_index + offset) % spaces, keepdims=False)

    my_turn = turn_at(0)
    next_turn = turn_at(1)
    source = (initial_state.astype(F32) + starting_field_nudges[0].astype(F32)).astype(BF16)
    near = near_source(source, my_turn, next_turn, row_tiles)
    band = widened_band(near, my_turn, next_turn, 5)
    north, south = exchange_rows(band, 5, tile_index, spaces)
    params = stack_params(w_depth, b_in, b_depth, norm_gain, norm_shift, b_down, head_bias, b_up)
    head = head_weight.T
    kept, middle_field = run_middle_forward(seam_turns, band, w_in, params, w_up, w_down, head)
    kept, field, tight, sent = run_rim_forward(
        seam_turns, north, south, w_in, params, w_up, w_down, head, middle_field, kept, members
    )
    patches, stem, normed, inverse, scaled, slope, active, hidden = kept
    sent, verifying_analysis, field_again = lax.optimization_barrier((sent, verifying_analysis, field))
    every = swap(sent, "ens")
    predicted = field_again.reshape(1, SIDE, SIDE * 96)
    target = verifying_analysis.reshape(4, 144, 96).transpose(1, 0, 2).reshape(144, 384)
    coefficient = 1.0 / math.sqrt(spaces * CELLS * 96)
    early, out_part, hidden_grad, scaled_grad, early_small = run_mixer_backward(
        every, tight, target, (hidden, active, slope, scaled), head, w_down, w_up, coefficient
    )
    late = run_depth_backward(
        scaled_grad, normed, inverse, hidden_grad, stem, params, patches, early_small, out_part
    )
    early_parts, late = lax.optimization_barrier((swap(early, "ens"), late))
    late_parts = swap(late.reshape(8, 32, 1152), "ens")
    shares = swap(run_combine(early_parts, late_parts), "space")
    whole = swap(run_total(shares, members), "ens")
    grad_w_in, grad_w_depth, grad_w_up, grad_w_down, grad_w_out, small, grad_b_up = run_unpack(whole)
    return (
        predicted,
        grad_w_in.T,
        small[4],
        grad_w_depth.T,
        small[1],
        small[2],
        small[3],
        grad_w_up.T,
        grad_b_up[0],
        grad_w_down.T,
        small[5],
        grad_w_out.T,
        small[10, :3],
    )


def solution(mesh):
    return jax.shard_map(
        body,
        mesh=mesh,
        in_specs=(
            P("space", None),
            P("ens", "space", None),
            P("space", None),
            P(),
            P(),
            P(),
            P(),
            P(),
            P(),
            P(),
            P(),
            P(),
            P(),
            P(),
            P(),
            P(),
        ),
        out_specs=(
            P("ens", "space", None),
            P(None, "space"),
            P("space"),
            P(None, "space"),
            P("space"),
            P("space"),
            P("space"),
            P(None, "space"),
            P("space"),
            P(None, "space"),
            P("space"),
            P(None, "space"),
            P("space"),
        ),
        check_vma=False,
    )
```

```python
import functools
import math

import jax
import jax.numpy as jnp
from jax import lax
from jax.experimental import pallas as pl
from jax.experimental.pallas import tpu as pltpu
from jax.sharding import PartitionSpec as P

EPS = 1e-06
CUBIC = 0.044715
ROOT = math.sqrt(2.0 / math.pi)
SOFT_SQUARE = 0.01
F32 = jnp.float32
BF16 = jnp.bfloat16
SIDE = 24
CELLS = SIDE * SIDE
LANE = 128
SMALL = 64
VMEM_BYTES = 56 * 1024 * 1024
SMALL_VMEM_BYTES = 16 * 1024 * 1024


def dot(left, right, left_dim=1, right_dim=0):
    return lax.dot_general(
        left, right, (((left_dim,), (right_dim,)), ((), ())), preferred_element_type=F32
    )


def soft_slope(values):
    return values * lax.rsqrt(values * values + SOFT_SQUARE)


def turned_offset(quarter, row_off, col_off):
    return (
        (row_off, col_off),
        (2 - col_off, row_off),
        (2 - row_off, 2 - col_off),
        (col_off, 2 - row_off),
    )[quarter]


def gather_patches(turns, wide_ref, stage_ref, patches_ref):
    bands = ((0, 0, 3), (3, 5, SIDE), (27, 31, 3))
    turn_of = {(1, 0): 0, (1, 2): 1, (0, 0): 2, (0, 2): 3, (2, 0): 4, (2, 2): 5}
    stage_ref[...] = jnp.zeros_like(stage_ref)
    for row_off in range(3):
        for col_off in range(3):
            for row_band, (row_to, row_from, row_len) in enumerate(bands):
                for col_band, (col_to, col_from, col_len) in enumerate(bands):

                    def read(quarter):
                        row, col = turned_offset(quarter, row_off, col_off)
                        return wide_ref[
                            row_from + row : row_from + row + row_len,
                            col_from + col : col_from + col + col_len,
                            :,
                        ]

                    piece = read(0)
                    if (row_band, col_band) in turn_of:
                        turn = turns[turn_of[row_band, col_band]]
                        for quarter in range(1, 4):
                            piece = jnp.where(turn == quarter, read(quarter), piece)
                    stage_ref[row_to : row_to + row_len, col_to : col_to + col_len, :] = piece
            at = (3 * row_off + col_off) * LANE
            patches_ref[:, at : at + LANE] = stage_ref[...].reshape(960, LANE).astype(BF16)


def forward_kernel(
    seam_turns_ref,
    source_ref,
    w_in_ref,
    w_depth_low_ref,
    vectors_ref,
    w_up_ref,
    w_down_ref,
    head_ref,
    patches_out,
    stem_out,
    normed_ref,
    inverse_ref,
    scaled_ref,
    slope_out,
    active_out,
    hidden_ref,
    field_ref,
    tight_ref,
    sent_ref,
    w_depth_ref,
    patches_ref,
    stem_ref,
    slope_ref,
    active_ref,
    wide_ref,
    stage_ref,
    w_in_wide_ref,
    whole_sem,
    part_sem,
):
    def send_part(part, row):
        at = pl.ds(row, 96)
        return (
            pltpu.make_async_copy(slope_ref.at[at], slope_out.at[at], part_sem.at[0, part]),
            pltpu.make_async_copy(active_ref.at[at], active_out.at[at], part_sem.at[1, part]),
        )

    send_patches = pltpu.make_async_copy(patches_ref, patches_out, whole_sem.at[0])
    send_stem = pltpu.make_async_copy(stem_ref, stem_out, whole_sem.at[1])
    tile = lax.axis_index("space")
    tiles = seam_turns_ref.shape[0]
    across = tiles // 4

    def turn_at(offset):
        return seam_turns_ref[lax.rem(tile + (tiles + offset), tiles)]

    turns = (
        turn_at(0),
        (4 - turn_at(1)) & 3,
        turn_at(-across),
        (4 - turn_at(1 - across)) & 3,
        turn_at(across),
        (4 - turn_at(across + 1)) & 3,
    )
    b_in, b_depth, gain, shift, b_down = (vectors_ref[k : k + 1, :] for k in range(5))
    head_bias = vectors_ref[5:6, 0:96]
    b_up = jnp.concatenate([vectors_ref[6 + k : 7 + k, :] for k in range(4)], axis=1)
    w_depth_ref[...] = w_depth_low_ref[...].astype(F32)
    for offset in range(9):
        w_in_wide_ref[offset * LANE : offset * LANE + 96, :] = w_in_ref[offset * 96 : (offset + 1) * 96, :]
        w_in_wide_ref[offset * LANE + 96 : (offset + 1) * LANE, :] = jnp.zeros((32, 256), BF16)
    wide_ref[...] = jnp.zeros_like(wide_ref)
    wide_ref[:, 0:36, 0:96] = source_ref[...].astype(F32)
    gather_patches(turns, wide_ref, stage_ref, patches_ref)
    send_patches.start()
    for part in range(5):
        rows = slice(part * 192, (part + 1) * 192)
        stem = dot(patches_ref[rows, :], w_in_wide_ref[...]) + b_in
        stem = stem.astype(BF16).astype(F32)
        for half in range(2):
            stem_ref[half, part * 6 : (part + 1) * 6] = stem[
                :, half * LANE : (half + 1) * LANE
            ].reshape(6, 32, LANE)

    send_stem.start()

    def normalise(block, carry):
        row = block * 4
        halves = []
        for half in range(2):
            lanes = slice(half * LANE, (half + 1) * LANE)
            total = jnp.zeros((4, SIDE, LANE), F32)
            for col_off in range(7):
                slab = stem_ref[half, pl.ds(row, 10), col_off : col_off + SIDE, :]
                for row_off in range(7):
                    tap = 7 * row_off + col_off
                    total = total + slab[row_off : row_off + 4] * w_depth_ref[tap : tap + 1, lanes][None]
            halves.append(total.reshape(4 * SIDE, LANE) + b_depth[:, lanes])
        mean = (
            jnp.sum(halves[0], axis=-1, keepdims=True) + jnp.sum(halves[1], axis=-1, keepdims=True)
        ) / 256.0
        centers = [h - mean for h in halves]
        spread = (
            jnp.sum(centers[0] * centers[0], axis=-1, keepdims=True)
            + jnp.sum(centers[1] * centers[1], axis=-1, keepdims=True)
        ) / 256.0
        inverse = lax.rsqrt(spread + EPS)
        at = pl.ds(pl.multiple_of(block * 96, 96), 96)
        inverse_ref[at, :] = jnp.broadcast_to(inverse, (96, LANE))
        for half in range(2):
            lanes = slice(half * LANE, (half + 1) * LANE)
            normed = centers[half] * inverse
            normed_ref[at, lanes] = normed
            scaled_ref[at, lanes] = (normed * gain[:, lanes] + shift[:, lanes]).astype(BF16)
        return carry

    lax.fori_loop(0, 6, normalise, 0)

    def mix(part, carry):
        row = pl.multiple_of(part * 96, 96)
        at = pl.ds(row, 96)
        upward = dot(scaled_ref[at, :], w_up_ref[...]) + b_up
        square = upward * upward
        tanh_part = jnp.tanh(ROOT * (upward + CUBIC * square * upward))
        plus = 0.5 * (1.0 + tanh_part)
        slope = plus + 0.5 * upward * (1.0 - tanh_part * tanh_part) * (
            ROOT + (3.0 * CUBIC * ROOT) * square
        )
        slope_ref[at, :] = slope.astype(BF16)
        active = (upward * plus).astype(BF16)
        active_ref[at, :] = active
        for send in send_part(part, row):
            send.start()
        own = [
            stem_ref[half, pl.ds(3 + 4 * part, 4), 3 : 3 + SIDE, :].reshape(96, LANE)
            for half in range(2)
        ]
        own = jnp.concatenate(own, axis=1)
        hidden = (own + dot(active, w_down_ref[...]) + b_down).astype(BF16)
        hidden_ref[at, :] = hidden
        field_ref[at, :] = dot(hidden, head_ref[...], 1, 1) + head_bias
        return carry

    lax.fori_loop(0, 6, mix, 0)
    for quarter in range(4):
        tight_ref[:, 96 * quarter : 96 * (quarter + 1)] = field_ref[
            144 * quarter : 144 * (quarter + 1), :
        ]
    sent = tight_ref[...].astype(BF16)
    for member in range(sent_ref.shape[0]):
        sent_ref[member] = sent
    send_patches.wait()
    send_stem.wait()
    for part in range(6):
        for send in send_part(part, 96 * part):
            send.wait()


def mixer_backward_kernel(
    coefficient,
    every_ref,
    own_ref,
    target_ref,
    hidden_ref,
    head_ref,
    pick_ref,
    active_in,
    slope_in,
    scaled_ref,
    w_down_in,
    w_up_in,
    early_ref,
    out_part_ref,
    hidden_grad_out,
    scaled_grad_out,
    small_ref,
    tight_ref,
    field_ref,
    low_ref,
    up_low_ref,
    up_sum_ref,
    down_ref,
    active_ref,
    slope_ref,
    w_down_ref,
    w_up_ref,
    hidden_grad_ref,
    scaled_grad_ref,
    in_sem,
    out_sem,
):
    fetch_active = pltpu.make_async_copy(active_in, active_ref, in_sem.at[0])
    fetch_slope = pltpu.make_async_copy(slope_in, slope_ref, in_sem.at[1])
    fetch_down = pltpu.make_async_copy(w_down_in, w_down_ref, in_sem.at[2])
    fetch_up = pltpu.make_async_copy(w_up_in, w_up_ref, in_sem.at[3])
    for fetch in (fetch_active, fetch_down, fetch_slope, fetch_up):
        fetch.start()
    send_hidden = pltpu.make_async_copy(hidden_grad_ref, hidden_grad_out, out_sem.at[0])
    send_scaled = pltpu.make_async_copy(scaled_grad_ref, scaled_grad_out, out_sem.at[1])
    members = every_ref.shape[0]
    own = own_ref[...]
    own_sent = own.astype(BF16).astype(F32)
    pair_sum = soft_slope(own_sent - every_ref[0].astype(F32))
    for member in range(1, members):
        pair_sum = pair_sum + soft_slope(own_sent - every_ref[member].astype(F32))
    direct = soft_slope(own - target_ref[...].astype(F32))
    tight_ref[...] = (
        direct * (coefficient / members) - pair_sum * (coefficient / (members * (members - 1)))
    )
    field_ref[...] = jnp.zeros_like(field_ref)
    for quarter in range(4):
        field_ref[144 * quarter : 144 * (quarter + 1), 0:96] = tight_ref[
            :, 96 * quarter : 96 * (quarter + 1)
        ]
    grad_f = field_ref[...]
    grad_b_out = jnp.sum(grad_f, axis=0, keepdims=True)
    grad_f_low = grad_f.astype(BF16)
    picked = dot(grad_f_low, pick_ref[...]).astype(BF16)
    out_part_ref[...] = dot(picked, hidden_ref[...], 0, 0)
    grad_hidden = dot(grad_f_low[:, 0:96], head_ref[...])
    hidden_grad_ref[...] = grad_hidden
    send_hidden.start()
    low_ref[...] = grad_hidden.astype(BF16)
    grad_b_down = jnp.sum(grad_hidden, axis=0, keepdims=True)
    fetch_active.wait()
    down_ref[...] = dot(low_ref[...], active_ref[...], 0, 0)
    up_sum_ref[...] = jnp.zeros_like(up_sum_ref)
    fetch_down.wait()
    fetch_slope.wait()
    fetch_up.wait()

    def widen(part, carry):
        at = pl.ds(pl.multiple_of(part * 96, 96), 96)
        grad_up = dot(low_ref[at, :], w_down_ref[...], 1, 1) * slope_ref[at, :].astype(F32)
        up_sum_ref[...] += jnp.sum(grad_up.reshape(12, 8, 1024), axis=0)
        up_low = grad_up.astype(BF16)
        up_low_ref[at, :] = up_low
        scaled_grad_ref[at, :] = dot(up_low, w_up_ref[...], 1, 1)
        return carry

    lax.fori_loop(0, 6, widen, 0)
    send_scaled.start()
    for chunk in range(4):
        up = dot(up_low_ref[:, chunk * 256 : (chunk + 1) * 256], scaled_ref[...], 0, 0)
        up = up.reshape(8, 4, 8, 256)
        for row_tile in range(4):
            for lane_tile in range(2):
                part = 2 * row_tile + lane_tile
                upper = down_ref[
                    chunk * 64 : (chunk + 1) * 64, part * LANE : (part + 1) * LANE
                ].reshape(8, 8, LANE)
                lower = up[:, row_tile, :, lane_tile * LANE : (lane_tile + 1) * LANE]
                early_ref[part, chunk * 8 : (chunk + 1) * 8] = jnp.concatenate(
                    [upper, lower], axis=1
                ).astype(BF16)
    up_sum = jnp.sum(up_sum_ref[...], axis=0, keepdims=True)
    unit = lax.broadcasted_iota(jnp.int32, (8, 1024), 1)
    row = lax.broadcasted_iota(jnp.int32, (8, 1024), 0)
    spread = jnp.where((unit & 3) == row, jnp.broadcast_to(up_sum, (8, 1024)), 0.0)
    fold = (
        lax.broadcasted_iota(jnp.int32, (1024, 256), 0) >> 2
        == lax.broadcasted_iota(jnp.int32, (1024, 256), 1)
    ).astype(F32).astype(BF16)
    column = lax.broadcasted_iota(jnp.int32, (LANE, 256), 1)
    place = (
        (lax.broadcasted_iota(jnp.int32, (LANE, 256), 0) == 3 * (column >> 3) + (column & 7))
        & ((column & 7) < 3)
    ).astype(F32).astype(BF16)
    b_out = jnp.broadcast_to(grad_b_out, (8, LANE))

    def two_part(values, matrix):
        high = values.astype(BF16)
        rest = (values - high.astype(F32)).astype(BF16)
        return dot(high, matrix) + dot(rest, matrix)

    small_ref[...] = jnp.zeros_like(small_ref)
    small_ref[0:1, :] = grad_b_down
    small_ref[1:5, :] = two_part(spread, fold)[0:4]
    small_ref[5:6, :] = two_part(b_out, place)[0:1]
    send_hidden.wait()
    send_scaled.wait()


def depth_backward_kernel(
    scaled_grad_ref,
    normed_ref,
    inverse_ref,
    vectors_ref,
    hidden_grad_in,
    stem_in,
    w_depth_ref,
    patches_in,
    order_ref,
    early_small_ref,
    out_part_ref,
    late_ref,
    deep_ref,
    stem_grad_ref,
    small_ref,
    sums_ref,
    low_ref,
    tight_ref,
    hidden_grad_ref,
    stem_ref,
    patches_ref,
    in_sem,
):
    fetch_stem = pltpu.make_async_copy(stem_in, stem_ref, in_sem.at[0])
    fetch_hidden = pltpu.make_async_copy(hidden_grad_in, hidden_grad_ref, in_sem.at[1])
    fetch_patches = pltpu.make_async_copy(patches_in, patches_ref, in_sem.at[2])
    for fetch in (fetch_stem, fetch_hidden, fetch_patches):
        fetch.start()
    deep_ref[...] = jnp.zeros_like(deep_ref)
    small_ref[...] = jnp.zeros_like(small_ref)
    sums_ref[...] = jnp.zeros_like(sums_ref)

    def unnormalise(block, carry):
        at = pl.ds(pl.multiple_of(block * 96, 96), 96)
        halves = []
        first = jnp.zeros((96, 1), F32)
        second = jnp.zeros((96, 1), F32)
        for half in range(2):
            lanes = slice(half * LANE, (half + 1) * LANE)
            grad = scaled_grad_ref[at, lanes]
            normed = normed_ref[at, lanes]
            sums_ref[0, :, lanes] += jnp.sum((grad * normed).reshape(12, 8, LANE), axis=0)
            sums_ref[1, :, lanes] += jnp.sum(grad.reshape(12, 8, LANE), axis=0)
            grad = grad * vectors_ref[2:3, lanes]
            first = first + jnp.sum(grad, axis=-1, keepdims=True)
            second = second + jnp.sum(grad * normed, axis=-1, keepdims=True)
            halves.append((grad, normed))
        first = first / 256.0
        second = second / 256.0
        inverse = inverse_ref[at, :]
        for half, (grad, normed) in enumerate(halves):
            lanes = slice(half * LANE, (half + 1) * LANE)
            deep = (grad - first - normed * second) * inverse
            sums_ref[2, :, lanes] += jnp.sum(deep.reshape(12, 8, LANE), axis=0)
            deep_ref[half, pl.ds(6 + block * 4, 4), 8 : 8 + SIDE, :] = deep.reshape(4, SIDE, LANE)
        return carry

    lax.fori_loop(0, 6, unnormalise, 0)
    fetch_stem.wait()
    fetch_hidden.wait()
    for half in range(2):
        lanes = slice(half * LANE, (half + 1) * LANE)

        def spread(block, carry):
            row = block * 6
            total = jnp.zeros((6, 32, LANE), F32)
            for col_off in range(7):
                slab = deep_ref[half, pl.ds(row, 12), 8 - col_off : 40 - col_off, :]
                for row_off in range(7):
                    tap = 7 * row_off + col_off
                    total = total + slab[6 - row_off : 12 - row_off] * w_depth_ref[tap : tap + 1, lanes][None]
            stem_grad_ref[half, pl.ds(row, 6)] = total
            return carry

        lax.fori_loop(0, 5, spread, 0)
        for col_off in range(7):

            def weigh(block, totals):
                row = block * 4
                deep = deep_ref[half, pl.ds(6 + row, 4), 8 : 8 + SIDE, :]
                slab = stem_ref[half, pl.ds(row, 10), col_off : col_off + SIDE, :]
                return tuple(
                    totals[row_off]
                    + jnp.sum((slab[row_off : row_off + 4] * deep).reshape(12, 8, LANE), axis=0)
                    for row_off in range(7)
                )

            totals = lax.fori_loop(0, 6, weigh, tuple(jnp.zeros((8, LANE), F32) for _ in range(7)))
            for row_off in range(7):
                tap = 7 * row_off + col_off
                small_ref[tap : tap + 1, lanes] = jnp.sum(totals[row_off], axis=0, keepdims=True)

        def add_direct(block, carry):
            at = pl.ds(pl.multiple_of(block * 96, 96), 96)
            stem_grad_ref[half, pl.ds(3 + block * 4, 4), 3 : 3 + SIDE, :] += hidden_grad_ref[
                at, lanes
            ].reshape(4, SIDE, LANE)
            return carry

        lax.fori_loop(0, 6, add_direct, 0)
        grad_stem = stem_grad_ref[half].reshape(960, LANE)
        small_ref[52:53, lanes] = jnp.sum(grad_stem, axis=0, keepdims=True)
        low_ref[:, lanes] = grad_stem.astype(BF16)
    small_ref[49:50, :] = jnp.sum(sums_ref[2], axis=0, keepdims=True)
    small_ref[50:51, :] = jnp.sum(sums_ref[0], axis=0, keepdims=True)
    small_ref[51:52, :] = jnp.sum(sums_ref[1], axis=0, keepdims=True)
    small_ref[53:59, :] = early_small_ref[0:6, :]
    fetch_patches.wait()
    order = order_ref[...]
    ordered = dot(low_ref[...], order).astype(BF16)
    wide = dot(ordered, patches_ref[...], 0, 0)
    tight_ref[...] = jnp.zeros_like(tight_ref)
    for offset in range(9):
        tight_ref[:, 96 * offset : 96 * (offset + 1)] = wide[:, LANE * offset : LANE * offset + 96]
    for part in range(8):
        rows = slice(32 * part, 32 * (part + 1))
        for row, at in enumerate((864, 1024, 1056)):
            tight_ref[rows, at : at + 32] = out_part_ref[32 * row : 32 * (row + 1), rows]
    small = small_ref[...]
    high = small.astype(BF16)
    rest = (small - high.astype(F32)).astype(BF16)
    both = jnp.concatenate([high, rest], axis=0)
    tight_ref[:, 896:1024] = dot(order, both, 0, 1)
    late_ref[...] = tight_ref[...].astype(BF16)


def combine_kernel(early_ref, late_ref, share_ref, rows_ref):
    members = early_ref.shape[0]
    early = early_ref[0].astype(F32)
    late = late_ref[0].astype(F32)
    for member in range(1, members):
        early = early + early_ref[member].astype(F32)
        late = late + late_ref[member].astype(F32)
    rows_ref[:, 0:16, :] = early
    for row in range(7):
        rows_ref[:, 16 + row : 17 + row, :] = late[:, row * LANE : (row + 1) * LANE][:, None, :]
    small = late[:, 896 : 896 + SMALL] + late[:, 960 : 960 + SMALL]
    last = jnp.concatenate([small, late[:, 1024:1088]], axis=1)
    rows_ref[:, 23:24, :] = last[:, None, :]
    share_ref[...] = rows_ref[...].astype(BF16)


def total_kernel(share_ref, copies_ref):
    total = share_ref[0].astype(F32)
    for tile in range(1, share_ref.shape[0]):
        total = total + share_ref[tile].astype(F32)
    for member in range(copies_ref.shape[0]):
        copies_ref[member] = total


def unpack_kernel(
    whole_ref,
    w_in_ref,
    w_depth_ref,
    w_up_ref,
    w_down_ref,
    w_out_ref,
    b_up_ref,
    b_depth_ref,
    gain_ref,
    shift_ref,
    b_in_ref,
    b_down_ref,
    b_out_ref,
):
    parts = whole_ref.shape[0]
    for part in range(parts):
        for row in range(7):
            lanes = slice(row * LANE, min((row + 1) * LANE, 864))
            w_in_ref[part : part + 1, lanes] = whole_ref[part, 16 + row : 17 + row, 0 : lanes.stop - lanes.start]
        w_down_ref[:, part * LANE : (part + 1) * LANE] = whole_ref[part, 0:8, :]
        row_tile, lane_tile = divmod(part, 2)
        w_up_ref[8 * row_tile : 8 * row_tile + 8, lane_tile * LANE : (lane_tile + 1) * LANE] = whole_ref[
            part, 8:16, :
        ]
        w_depth_ref[part : part + 1, :] = whole_ref[part, 23:24, 0:49]
        lanes = slice(32 * part, 32 * (part + 1))
        w_out_ref[0:1, lanes] = whole_ref[part, 22:23, 96:128]
        w_out_ref[1:2, lanes] = whole_ref[part, 23:24, 64:96]
        w_out_ref[2:3, lanes] = whole_ref[part, 23:24, 96:128]
        b_up_ref[0:1, 4 * part : 4 * part + 4] = whole_ref[part, 23:24, 54:58]
    small = jnp.concatenate([whole_ref[part, 23:24, :] for part in range(parts)], axis=0)
    by_row = small.T
    for row, out_ref in enumerate((b_depth_ref, gain_ref, shift_ref, b_in_ref, b_down_ref), 49):
        out_ref[...] = by_row[row : row + 1, :]
    b_out_ref[...] = by_row[58:59, 0:3]


def call(kernel, outs, scratch, *operands, spaces=None, vmem=VMEM_BYTES, flops=0):
    kinds = {"v": pltpu.VMEM, "s": pltpu.SMEM, "a": pl.ANY}
    spaces = spaces or "v" * len(operands)
    return pl.pallas_call(
        kernel,
        out_shape=[jax.ShapeDtypeStruct(shape, kind) for shape, kind, _ in outs],
        in_specs=[pl.BlockSpec(memory_space=kinds[letter]) for letter in spaces],
        out_specs=[pl.BlockSpec(memory_space=kinds[letter]) for _, _, letter in outs],
        scratch_shapes=[x if not isinstance(x, tuple) else pltpu.VMEM(*x) for x in scratch],
        compiler_params=pltpu.CompilerParams(vmem_limit_bytes=vmem),
        cost_estimate=pl.CostEstimate(flops=flops, bytes_accessed=8_000_000, transcendentals=0),
    )(*operands)


def stack_vectors(b_in, b_depth, gain, shift, b_down, head_bias, b_up):
    rows = [b_in, b_depth, gain, shift, b_down, jnp.pad(head_bias, (0, 160)), b_up]
    return jnp.concatenate(rows).astype(F32).reshape(10, 256)


def run_forward(seam_turns, source, w_in, w_depth, vectors, w_up, w_down, head, members):
    return call(
        forward_kernel,
        [
            ((960, 1152), BF16, "a"),
            ((2, 30, 32, LANE), F32, "a"),
            ((CELLS, 256), F32, "v"),
            ((CELLS, LANE), F32, "v"),
            ((CELLS, 256), BF16, "v"),
            ((CELLS, 1024), BF16, "a"),
            ((CELLS, 1024), BF16, "a"),
            ((CELLS, 256), BF16, "v"),
            ((CELLS, 96), F32, "v"),
            ((144, 384), F32, "v"),
            ((members, 144, 384), BF16, "v"),
            ((49, 256), F32, "v"),
        ],
        [
            ((960, 1152), BF16),
            ((2, 30, 32, LANE), F32),
            ((CELLS, 1024), BF16),
            ((CELLS, 1024), BF16),
            ((36, 40, LANE), F32),
            ((30, 32, LANE), F32),
            ((1152, 256), BF16),
            pltpu.SemaphoreType.DMA((2,)),
            pltpu.SemaphoreType.DMA((2, 6)),
        ],
        seam_turns,
        source,
        w_in,
        w_depth,
        vectors,
        w_up,
        w_down,
        head,
        spaces="svvvvvvv",
        flops=10_000_000_000,
    )


def run_mixer_backward(every, tight, target, saved, head, w_down, w_up, coefficient):
    hidden, active, slope, scaled = saved
    column = jnp.arange(96)
    owner = 3 * (column % 32) + column // 32
    pick = (jnp.arange(LANE)[:, None] == owner[None, :]).astype(BF16)
    return call(
        functools.partial(mixer_backward_kernel, coefficient),
        [
            ((8, 32, 16, LANE), BF16, "v"),
            ((96, 256), F32, "v"),
            ((CELLS, 256), F32, "a"),
            ((CELLS, 256), F32, "a"),
            ((8, 256), F32, "v"),
        ],
        [
            ((144, 384), F32),
            ((CELLS, LANE), F32),
            ((CELLS, 256), BF16),
            ((CELLS, 1024), BF16),
            ((8, 1024), F32),
            ((256, 1024), F32),
            ((CELLS, 1024), BF16),
            ((CELLS, 1024), BF16),
            ((1024, 256), BF16),
            ((256, 1024), BF16),
            ((CELLS, 256), F32),
            ((CELLS, 256), F32),
            pltpu.SemaphoreType.DMA((4,)),
            pltpu.SemaphoreType.DMA((2,)),
        ],
        every,
        tight,
        target,
        hidden,
        head,
        pick,
        active,
        slope,
        scaled,
        w_down,
        w_up,
        spaces="vvvvvvaavaa",
        flops=12_000_000_000,
    )


def run_depth_backward(
    scaled_grad, normed, inverse, vectors, hidden_grad, stem, w_depth, patches, early_small, out_part
):
    column = jnp.arange(256)
    order = (column[:, None] == (8 * (column % 32) + column // 32)[None, :]).astype(BF16)
    return call(
        depth_backward_kernel,
        [((256, 1152), BF16, "v")],
        [
            ((2, 36, 40, LANE), F32),
            ((2, 30, 32, LANE), F32),
            ((SMALL, 256), F32),
            ((3, 8, 256), F32),
            ((960, 256), BF16),
            ((256, 1152), F32),
            ((CELLS, 256), F32),
            ((2, 30, 32, LANE), F32),
            ((960, 1152), BF16),
            pltpu.SemaphoreType.DMA((3,)),
        ],
        scaled_grad,
        normed,
        inverse,
        vectors,
        hidden_grad,
        stem,
        w_depth,
        patches,
        order,
        early_small,
        out_part,
        spaces="vvvvaavavvv",
        flops=12_000_000_000,
    )[0]


def run_combine(early, late):
    return call(
        combine_kernel,
        [((32, 24, LANE), BF16, "v")],
        [((32, 24, LANE), F32)],
        early,
        late,
        vmem=SMALL_VMEM_BYTES,
    )[0]


def run_total(share, members):
    return call(total_kernel, [((members, 24, LANE), F32, "v")], [], share, vmem=SMALL_VMEM_BYTES)[0]


def run_unpack(whole):
    shapes = ((8, 864), (8, 49), (32, 256), (8, 1024), (3, 256), (1, 32)) + ((1, 8),) * 5 + ((1, 3),)
    return call(
        unpack_kernel, [(shape, F32, "v") for shape in shapes], [], whole, vmem=SMALL_VMEM_BYTES
    )


def shifted(value, axis, by):
    peers = lax.axis_size(axis)
    return lax.ppermute(value, axis, [(i, (i + by) % peers) for i in range(peers)])


def turned_edge(tile, turns, width, east):
    size = tile.shape[0]

    def columns(x):
        return x[:, size - width :] if east else x[:, :width]

    sides = (
        columns(tile),
        columns(jnp.rot90(tile, 1)),
        columns(jnp.rot90(tile, 2)),
        columns(jnp.rot90(tile, 3)),
    )
    result = sides[0]
    for quarter in range(1, 4):
        result = jnp.where(turns == quarter, sides[quarter], result)
    return result


def seam_pad(tile, my_turn, next_turn, margin, row_tiles):
    came_west = shifted(turned_edge(tile, next_turn, margin, True), "space", 1)
    came_east = shifted(turned_edge(tile, (4 - my_turn) % 4, margin, False), "space", -1)
    widened = jnp.concatenate([came_west, tile, came_east], axis=1)
    came_north = shifted(widened[-margin:], "space", row_tiles)
    came_south = shifted(widened[:margin], "space", -row_tiles)
    return jnp.concatenate([came_north, widened, came_south], axis=0)


def swap(value, axis):
    return lax.all_to_all(value, axis, 0, 0, tiled=True)


def body(
    initial_state,
    starting_field_nudges,
    verifying_analysis,
    seam_turns,
    w_in,
    b_in,
    w_depth,
    b_depth,
    norm_gain,
    norm_shift,
    w_up,
    b_up,
    w_down,
    b_down,
    head_weight,
    head_bias,
):
    spaces = lax.axis_size("space")
    members = lax.axis_size("ens")
    row_tiles = spaces // 4
    tile_index = lax.axis_index("space")

    def turn_at(offset):
        return lax.dynamic_index_in_dim(seam_turns, (tile_index + offset) % spaces, keepdims=False)

    my_turn = turn_at(0)
    next_turn = turn_at(1)
    source = (
        initial_state.astype(F32) + starting_field_nudges[0].astype(F32)
    ).astype(BF16).reshape(SIDE, SIDE, 96)
    near = seam_pad(source, my_turn, next_turn, 1, row_tiles)
    wide_source = seam_pad(near, my_turn, next_turn, 5, row_tiles)
    vectors = stack_vectors(b_in, b_depth, norm_gain, norm_shift, b_down, head_bias, b_up)
    head = head_weight.T
    saved = run_forward(seam_turns, wide_source, w_in, w_depth, vectors, w_up, w_down, head, members)
    patches, stem, normed, inverse, scaled, slope, active, hidden, field, tight, sent, w_depth_wide = saved
    sent, verifying_analysis, field_again = lax.optimization_barrier((sent, verifying_analysis, field))
    every = swap(sent, "ens")
    predicted = field_again.reshape(1, SIDE, SIDE * 96)
    target = verifying_analysis.reshape(4, 144, 96).transpose(1, 0, 2).reshape(144, 384)
    coefficient = 1.0 / math.sqrt(spaces * CELLS * 96)
    early, out_part, hidden_grad, scaled_grad, early_small = run_mixer_backward(
        every, tight, target, (hidden, active, slope, scaled), head, w_down, w_up, coefficient
    )
    late = run_depth_backward(
        scaled_grad, normed, inverse, vectors, hidden_grad, stem, w_depth_wide, patches, early_small, out_part
    )
    early_parts, late = lax.optimization_barrier((swap(early, "ens"), late))
    late_parts = swap(late.reshape(8, 32, 1152), "ens")
    shares = swap(run_combine(early_parts, late_parts), "space")
    whole = swap(run_total(shares, members), "ens")
    (
        grad_w_in, grad_w_depth, grad_w_up, grad_w_down, grad_w_out,
        grad_b_up, grad_b_depth, grad_gain, grad_shift, grad_b_in, grad_b_down, grad_b_out,
    ) = run_unpack(whole)
    return (
        predicted,
        grad_w_in.T,
        grad_b_in[0],
        grad_w_depth.T,
        grad_b_depth[0],
        grad_gain[0],
        grad_shift[0],
        grad_w_up.T,
        grad_b_up[0],
        grad_w_down.T,
        grad_b_down[0],
        grad_w_out.T,
        grad_b_out[0],
    )


def solution(mesh):
    return jax.shard_map(
        body,
        mesh=mesh,
        in_specs=(
            P("space", None),
            P("ens", "space", None),
            P("space", None),
            P(),
            P(),
            P(),
            P(),
            P(),
            P(),
            P(),
            P(),
            P(),
            P(),
            P(),
            P(),
            P(),
        ),
        out_specs=(
            P("ens", "space", None),
            P(None, "space"),
            P("space"),
            P(None, "space"),
            P("space"),
            P("space"),
            P("space"),
            P(None, "space"),
            P("space"),
            P(None, "space"),
            P("space"),
            P(None, "space"),
            P("space"),
        ),
        check_vma=False,
    )
```

```python
import functools
import math

import jax
import jax.numpy as jnp
from jax import lax
from jax.experimental import pallas as pl
from jax.experimental.pallas import tpu as pltpu
from jax.sharding import PartitionSpec as P

EPS = 1e-06
CUBIC = 0.044715
ROOT = math.sqrt(2.0 / math.pi)
SOFT_SQUARE = 0.01
F32 = jnp.float32
BF16 = jnp.bfloat16
SIDE = 24
CELLS = SIDE * SIDE
LANE = 128
SMALL = 64
VMEM_BYTES = 56 * 1024 * 1024
SMALL_VMEM_BYTES = 16 * 1024 * 1024


def dot(left, right, left_dim=1, right_dim=0):
    return lax.dot_general(
        left, right, (((left_dim,), (right_dim,)), ((), ())), preferred_element_type=F32
    )


def soft_slope(values):
    return values * lax.rsqrt(values * values + SOFT_SQUARE)


def turned_offset(quarter, row_off, col_off):
    return (
        (row_off, col_off),
        (2 - col_off, row_off),
        (2 - row_off, 2 - col_off),
        (col_off, 2 - row_off),
    )[quarter]


def gather_patches(turns, wide_ref, stage_ref, patches_ref):
    bands = ((0, 0, 3), (3, 5, SIDE), (27, 31, 3))
    turn_of = {(1, 0): 0, (1, 2): 1, (0, 0): 2, (0, 2): 3, (2, 0): 4, (2, 2): 5}
    stage_ref[...] = jnp.zeros_like(stage_ref)
    for row_off in range(3):
        for col_off in range(3):
            for row_band, (row_to, row_from, row_len) in enumerate(bands):
                for col_band, (col_to, col_from, col_len) in enumerate(bands):

                    def read(quarter):
                        row, col = turned_offset(quarter, row_off, col_off)
                        return wide_ref[
                            row_from + row : row_from + row + row_len,
                            col_from + col : col_from + col + col_len,
                            :,
                        ]

                    piece = read(0)
                    if (row_band, col_band) in turn_of:
                        turn = turns[turn_of[row_band, col_band]]
                        for quarter in range(1, 4):
                            piece = jnp.where(turn == quarter, read(quarter), piece)
                    stage_ref[row_to : row_to + row_len, col_to : col_to + col_len, :] = piece
            at = (3 * row_off + col_off) * LANE
            patches_ref[:, at : at + LANE] = stage_ref[...].reshape(960, LANE).astype(BF16)


def forward_kernel(
    seam_turns_ref,
    source_ref,
    w_in_ref,
    w_depth_low_ref,
    vectors_ref,
    w_up_ref,
    w_down_ref,
    head_ref,
    patches_out,
    stem_out,
    normed_out,
    inverse_out,
    scaled_out,
    slope_out,
    active_out,
    hidden_ref,
    field_ref,
    tight_ref,
    sent_ref,
    w_depth_ref,
    patches_ref,
    stem_ref,
    slope_ref,
    active_ref,
    normed_ref,
    inverse_ref,
    scaled_ref,
    wide_ref,
    stage_ref,
    w_in_wide_ref,
    whole_sem,
    part_sem,
):
    def send_part(part, row):
        at = pl.ds(row, 96)
        return (
            pltpu.make_async_copy(slope_ref.at[at], slope_out.at[at], part_sem.at[0, part]),
            pltpu.make_async_copy(active_ref.at[at], active_out.at[at], part_sem.at[1, part]),
        )

    send_patches = pltpu.make_async_copy(patches_ref, patches_out, whole_sem.at[0])
    send_stem = pltpu.make_async_copy(stem_ref, stem_out, whole_sem.at[1])
    send_norms = [
        pltpu.make_async_copy(normed_ref, normed_out, whole_sem.at[2]),
        pltpu.make_async_copy(inverse_ref, inverse_out, whole_sem.at[3]),
        pltpu.make_async_copy(scaled_ref, scaled_out, whole_sem.at[4]),
    ]
    tile = lax.axis_index("space")
    tiles = seam_turns_ref.shape[0]
    across = tiles // 4

    def turn_at(offset):
        return seam_turns_ref[lax.rem(tile + (tiles + offset), tiles)]

    turns = (
        turn_at(0),
        (4 - turn_at(1)) & 3,
        turn_at(-across),
        (4 - turn_at(1 - across)) & 3,
        turn_at(across),
        (4 - turn_at(across + 1)) & 3,
    )
    b_in, b_depth, gain, shift, b_down = (vectors_ref[k : k + 1, :] for k in range(5))
    head_bias = vectors_ref[5:6, 0:96]
    b_up = jnp.concatenate([vectors_ref[6 + k : 7 + k, :] for k in range(4)], axis=1)
    w_depth_ref[...] = w_depth_low_ref[...].astype(F32)
    for offset in range(9):
        w_in_wide_ref[offset * LANE : offset * LANE + 96, :] = w_in_ref[offset * 96 : (offset + 1) * 96, :]
        w_in_wide_ref[offset * LANE + 96 : (offset + 1) * LANE, :] = jnp.zeros((32, 256), BF16)
    wide_ref[...] = jnp.zeros_like(wide_ref)
    wide_ref[:, 0:36, 0:96] = source_ref[...].astype(F32)
    gather_patches(turns, wide_ref, stage_ref, patches_ref)
    send_patches.start()
    for part in range(5):
        rows = slice(part * 192, (part + 1) * 192)
        stem = dot(patches_ref[rows, :], w_in_wide_ref[...]) + b_in
        stem = stem.astype(BF16).astype(F32)
        for half in range(2):
            stem_ref[half, part * 6 : (part + 1) * 6] = stem[
                :, half * LANE : (half + 1) * LANE
            ].reshape(6, 32, LANE)

    send_stem.start()

    def normalise(block, carry):
        row = block * 4
        halves = []
        for half in range(2):
            lanes = slice(half * LANE, (half + 1) * LANE)
            total = jnp.zeros((4, SIDE, LANE), F32)
            for col_off in range(7):
                slab = stem_ref[half, pl.ds(row, 10), col_off : col_off + SIDE, :]
                for row_off in range(7):
                    tap = 7 * row_off + col_off
                    total = total + slab[row_off : row_off + 4] * w_depth_ref[tap : tap + 1, lanes][None]
            halves.append(total.reshape(4 * SIDE, LANE) + b_depth[:, lanes])
        mean = (
            jnp.sum(halves[0], axis=-1, keepdims=True) + jnp.sum(halves[1], axis=-1, keepdims=True)
        ) / 256.0
        centers = [h - mean for h in halves]
        spread = (
            jnp.sum(centers[0] * centers[0], axis=-1, keepdims=True)
            + jnp.sum(centers[1] * centers[1], axis=-1, keepdims=True)
        ) / 256.0
        inverse = lax.rsqrt(spread + EPS)
        at = pl.ds(pl.multiple_of(block * 96, 96), 96)
        inverse_ref[at, :] = jnp.broadcast_to(inverse, (96, LANE))
        for half in range(2):
            lanes = slice(half * LANE, (half + 1) * LANE)
            normed = centers[half] * inverse
            normed_ref[at, lanes] = normed
            scaled_ref[at, lanes] = (normed * gain[:, lanes] + shift[:, lanes]).astype(BF16)
        return carry

    lax.fori_loop(0, 6, normalise, 0)
    for send in send_norms:
        send.start()

    def mix(part, carry):
        row = pl.multiple_of(part * 96, 96)
        at = pl.ds(row, 96)
        upward = dot(scaled_ref[at, :], w_up_ref[...]) + b_up
        square = upward * upward
        tanh_part = jnp.tanh(ROOT * (upward + CUBIC * square * upward))
        plus = 0.5 * (1.0 + tanh_part)
        slope = plus + 0.5 * upward * (1.0 - tanh_part * tanh_part) * (
            ROOT + (3.0 * CUBIC * ROOT) * square
        )
        slope_ref[at, :] = slope.astype(BF16)
        active = (upward * plus).astype(BF16)
        active_ref[at, :] = active
        for send in send_part(part, row):
            send.start()
        own = [
            stem_ref[half, pl.ds(3 + 4 * part, 4), 3 : 3 + SIDE, :].reshape(96, LANE)
            for half in range(2)
        ]
        own = jnp.concatenate(own, axis=1)
        hidden = (own + dot(active, w_down_ref[...]) + b_down).astype(BF16)
        hidden_ref[at, :] = hidden
        field_ref[at, :] = dot(hidden, head_ref[...], 1, 1) + head_bias
        return carry

    lax.fori_loop(0, 6, mix, 0)
    for quarter in range(4):
        tight_ref[:, 96 * quarter : 96 * (quarter + 1)] = field_ref[
            144 * quarter : 144 * (quarter + 1), :
        ]
    sent = tight_ref[...].astype(BF16)
    for member in range(sent_ref.shape[0]):
        sent_ref[member] = sent
    send_patches.wait()
    send_stem.wait()
    for send in send_norms:
        send.wait()
    for part in range(6):
        for send in send_part(part, 96 * part):
            send.wait()


def mixer_backward_kernel(
    coefficient,
    every_ref,
    own_ref,
    target_ref,
    hidden_ref,
    head_ref,
    pick_ref,
    active_in,
    slope_in,
    scaled_ref,
    w_down_in,
    w_up_in,
    early_ref,
    out_part_ref,
    hidden_grad_out,
    scaled_grad_out,
    small_ref,
    tight_ref,
    field_ref,
    low_ref,
    up_low_ref,
    up_sum_ref,
    down_ref,
    active_ref,
    slope_ref,
    w_down_ref,
    w_up_ref,
    hidden_grad_ref,
    scaled_grad_ref,
    in_sem,
    out_sem,
):
    fetch_active = pltpu.make_async_copy(active_in, active_ref, in_sem.at[0])
    fetch_slope = pltpu.make_async_copy(slope_in, slope_ref, in_sem.at[1])
    fetch_down = pltpu.make_async_copy(w_down_in, w_down_ref, in_sem.at[2])
    fetch_up = pltpu.make_async_copy(w_up_in, w_up_ref, in_sem.at[3])
    for fetch in (fetch_active, fetch_down, fetch_slope, fetch_up):
        fetch.start()
    send_hidden = pltpu.make_async_copy(hidden_grad_ref, hidden_grad_out, out_sem.at[0])
    send_scaled = pltpu.make_async_copy(scaled_grad_ref, scaled_grad_out, out_sem.at[1])
    members = every_ref.shape[0]
    own = own_ref[...]
    own_sent = own.astype(BF16).astype(F32)
    pair_sum = soft_slope(own_sent - every_ref[0].astype(F32))
    for member in range(1, members):
        pair_sum = pair_sum + soft_slope(own_sent - every_ref[member].astype(F32))
    direct = soft_slope(own - target_ref[...].astype(F32))
    tight_ref[...] = (
        direct * (coefficient / members) - pair_sum * (coefficient / (members * (members - 1)))
    )
    field_ref[...] = jnp.zeros_like(field_ref)
    for quarter in range(4):
        field_ref[144 * quarter : 144 * (quarter + 1), 0:96] = tight_ref[
            :, 96 * quarter : 96 * (quarter + 1)
        ]
    grad_f = field_ref[...]
    grad_b_out = jnp.sum(grad_f, axis=0, keepdims=True)
    grad_f_low = grad_f.astype(BF16)
    picked = dot(grad_f_low, pick_ref[...]).astype(BF16)
    out_part_ref[...] = dot(picked, hidden_ref[...], 0, 0)
    grad_hidden = dot(grad_f_low[:, 0:96], head_ref[...])
    hidden_grad_ref[...] = grad_hidden
    send_hidden.start()
    low_ref[...] = grad_hidden.astype(BF16)
    grad_b_down = jnp.sum(grad_hidden, axis=0, keepdims=True)
    fetch_active.wait()
    down_ref[...] = dot(low_ref[...], active_ref[...], 0, 0)
    up_sum_ref[...] = jnp.zeros_like(up_sum_ref)
    fetch_down.wait()
    fetch_slope.wait()
    fetch_up.wait()

    def widen(part, carry):
        at = pl.ds(pl.multiple_of(part * 96, 96), 96)
        grad_up = dot(low_ref[at, :], w_down_ref[...], 1, 1) * slope_ref[at, :].astype(F32)
        up_sum_ref[...] += jnp.sum(grad_up.reshape(12, 8, 1024), axis=0)
        up_low = grad_up.astype(BF16)
        up_low_ref[at, :] = up_low
        scaled_grad_ref[at, :] = dot(up_low, w_up_ref[...], 1, 1)
        return carry

    lax.fori_loop(0, 6, widen, 0)
    send_scaled.start()
    for chunk in range(4):
        up = dot(up_low_ref[:, chunk * 256 : (chunk + 1) * 256], scaled_ref[...], 0, 0)
        up = up.reshape(8, 4, 8, 256)
        for row_tile in range(4):
            for lane_tile in range(2):
                part = 2 * row_tile + lane_tile
                upper = down_ref[
                    chunk * 64 : (chunk + 1) * 64, part * LANE : (part + 1) * LANE
                ].reshape(8, 8, LANE)
                lower = up[:, row_tile, :, lane_tile * LANE : (lane_tile + 1) * LANE]
                early_ref[part, chunk * 8 : (chunk + 1) * 8] = jnp.concatenate(
                    [upper, lower], axis=1
                ).astype(BF16)
    up_sum = jnp.sum(up_sum_ref[...], axis=0, keepdims=True)
    unit = lax.broadcasted_iota(jnp.int32, (8, 1024), 1)
    row = lax.broadcasted_iota(jnp.int32, (8, 1024), 0)
    spread = jnp.where((unit & 3) == row, jnp.broadcast_to(up_sum, (8, 1024)), 0.0)
    fold = (
        lax.broadcasted_iota(jnp.int32, (1024, 256), 0) >> 2
        == lax.broadcasted_iota(jnp.int32, (1024, 256), 1)
    ).astype(F32).astype(BF16)
    column = lax.broadcasted_iota(jnp.int32, (LANE, 256), 1)
    place = (
        (lax.broadcasted_iota(jnp.int32, (LANE, 256), 0) == 3 * (column >> 3) + (column & 7))
        & ((column & 7) < 3)
    ).astype(F32).astype(BF16)
    b_out = jnp.broadcast_to(grad_b_out, (8, LANE))

    def two_part(values, matrix):
        high = values.astype(BF16)
        rest = (values - high.astype(F32)).astype(BF16)
        return dot(high, matrix) + dot(rest, matrix)

    small_ref[...] = jnp.zeros_like(small_ref)
    small_ref[0:1, :] = grad_b_down
    small_ref[1:5, :] = two_part(spread, fold)[0:4]
    small_ref[5:6, :] = two_part(b_out, place)[0:1]
    send_hidden.wait()
    send_scaled.wait()


def depth_backward_kernel(
    scaled_grad_ref,
    normed_ref,
    inverse_ref,
    vectors_ref,
    hidden_grad_in,
    stem_in,
    w_depth_ref,
    patches_in,
    order_ref,
    early_small_ref,
    out_part_ref,
    late_ref,
    deep_ref,
    stem_grad_ref,
    small_ref,
    sums_ref,
    low_ref,
    tight_ref,
    hidden_grad_ref,
    stem_ref,
    patches_ref,
    in_sem,
):
    fetch_stem = pltpu.make_async_copy(stem_in, stem_ref, in_sem.at[0])
    fetch_hidden = pltpu.make_async_copy(hidden_grad_in, hidden_grad_ref, in_sem.at[1])
    fetch_patches = pltpu.make_async_copy(patches_in, patches_ref, in_sem.at[2])
    for fetch in (fetch_stem, fetch_hidden, fetch_patches):
        fetch.start()
    deep_ref[...] = jnp.zeros_like(deep_ref)
    small_ref[...] = jnp.zeros_like(small_ref)
    sums_ref[...] = jnp.zeros_like(sums_ref)

    def unnormalise(block, carry):
        at = pl.ds(pl.multiple_of(block * 96, 96), 96)
        halves = []
        first = jnp.zeros((96, 1), F32)
        second = jnp.zeros((96, 1), F32)
        for half in range(2):
            lanes = slice(half * LANE, (half + 1) * LANE)
            grad = scaled_grad_ref[at, lanes]
            normed = normed_ref[at, lanes]
            sums_ref[0, :, lanes] += jnp.sum((grad * normed).reshape(12, 8, LANE), axis=0)
            sums_ref[1, :, lanes] += jnp.sum(grad.reshape(12, 8, LANE), axis=0)
            grad = grad * vectors_ref[2:3, lanes]
            first = first + jnp.sum(grad, axis=-1, keepdims=True)
            second = second + jnp.sum(grad * normed, axis=-1, keepdims=True)
            halves.append((grad, normed))
        first = first / 256.0
        second = second / 256.0
        inverse = inverse_ref[at, :]
        for half, (grad, normed) in enumerate(halves):
            lanes = slice(half * LANE, (half + 1) * LANE)
            deep = (grad - first - normed * second) * inverse
            sums_ref[2, :, lanes] += jnp.sum(deep.reshape(12, 8, LANE), axis=0)
            deep_ref[half, pl.ds(6 + block * 4, 4), 8 : 8 + SIDE, :] = deep.reshape(4, SIDE, LANE)
        return carry

    lax.fori_loop(0, 6, unnormalise, 0)
    fetch_stem.wait()
    fetch_hidden.wait()
    for half in range(2):
        lanes = slice(half * LANE, (half + 1) * LANE)

        def spread(block, carry):
            row = block * 6
            total = jnp.zeros((6, 32, LANE), F32)
            for col_off in range(7):
                slab = deep_ref[half, pl.ds(row, 12), 8 - col_off : 40 - col_off, :]
                for row_off in range(7):
                    tap = 7 * row_off + col_off
                    total = total + slab[6 - row_off : 12 - row_off] * w_depth_ref[tap : tap + 1, lanes][None]
            stem_grad_ref[half, pl.ds(row, 6)] = total
            return carry

        lax.fori_loop(0, 5, spread, 0)
        for col_off in range(7):

            def weigh(block, totals):
                row = block * 4
                deep = deep_ref[half, pl.ds(6 + row, 4), 8 : 8 + SIDE, :]
                slab = stem_ref[half, pl.ds(row, 10), col_off : col_off + SIDE, :]
                return tuple(
                    totals[row_off]
                    + jnp.sum((slab[row_off : row_off + 4] * deep).reshape(12, 8, LANE), axis=0)
                    for row_off in range(7)
                )

            totals = lax.fori_loop(0, 6, weigh, tuple(jnp.zeros((8, LANE), F32) for _ in range(7)))
            for row_off in range(7):
                tap = 7 * row_off + col_off
                small_ref[tap : tap + 1, lanes] = jnp.sum(totals[row_off], axis=0, keepdims=True)

        def add_direct(block, carry):
            at = pl.ds(pl.multiple_of(block * 96, 96), 96)
            stem_grad_ref[half, pl.ds(3 + block * 4, 4), 3 : 3 + SIDE, :] += hidden_grad_ref[
                at, lanes
            ].reshape(4, SIDE, LANE)
            return carry

        lax.fori_loop(0, 6, add_direct, 0)
        grad_stem = stem_grad_ref[half].reshape(960, LANE)
        small_ref[52:53, lanes] = jnp.sum(grad_stem, axis=0, keepdims=True)
        low_ref[:, lanes] = grad_stem.astype(BF16)
    small_ref[49:50, :] = jnp.sum(sums_ref[2], axis=0, keepdims=True)
    small_ref[50:51, :] = jnp.sum(sums_ref[0], axis=0, keepdims=True)
    small_ref[51:52, :] = jnp.sum(sums_ref[1], axis=0, keepdims=True)
    small_ref[53:59, :] = early_small_ref[0:6, :]
    fetch_patches.wait()
    order = order_ref[...]
    ordered = dot(low_ref[...], order).astype(BF16)
    wide = dot(ordered, patches_ref[...], 0, 0)
    tight_ref[...] = jnp.zeros_like(tight_ref)
    for offset in range(9):
        tight_ref[:, 96 * offset : 96 * (offset + 1)] = wide[:, LANE * offset : LANE * offset + 96]
    for part in range(8):
        rows = slice(32 * part, 32 * (part + 1))
        for row, at in enumerate((864, 1024, 1056)):
            tight_ref[rows, at : at + 32] = out_part_ref[32 * row : 32 * (row + 1), rows]
    small = small_ref[...]
    high = small.astype(BF16)
    rest = (small - high.astype(F32)).astype(BF16)
    both = jnp.concatenate([high, rest], axis=0)
    tight_ref[:, 896:1024] = dot(order, both, 0, 1)
    late_ref[...] = tight_ref[...].astype(BF16)


def combine_kernel(early_ref, late_ref, share_ref, rows_ref):
    members = early_ref.shape[0]
    early = early_ref[0].astype(F32)
    late = late_ref[0].astype(F32)
    for member in range(1, members):
        early = early + early_ref[member].astype(F32)
        late = late + late_ref[member].astype(F32)
    rows_ref[:, 0:16, :] = early
    for row in range(7):
        rows_ref[:, 16 + row : 17 + row, :] = late[:, row * LANE : (row + 1) * LANE][:, None, :]
    small = late[:, 896 : 896 + SMALL] + late[:, 960 : 960 + SMALL]
    last = jnp.concatenate([small, late[:, 1024:1088]], axis=1)
    rows_ref[:, 23:24, :] = last[:, None, :]
    share_ref[...] = rows_ref[...].astype(BF16)


def total_kernel(share_ref, copies_ref):
    total = share_ref[0].astype(F32)
    for tile in range(1, share_ref.shape[0]):
        total = total + share_ref[tile].astype(F32)
    for member in range(copies_ref.shape[0]):
        copies_ref[member] = total


def unpack_kernel(
    whole_ref,
    w_in_ref,
    w_depth_ref,
    w_up_ref,
    w_down_ref,
    w_out_ref,
    b_up_ref,
    b_depth_ref,
    gain_ref,
    shift_ref,
    b_in_ref,
    b_down_ref,
    b_out_ref,
):
    parts = whole_ref.shape[0]
    for part in range(parts):
        for row in range(7):
            lanes = slice(row * LANE, min((row + 1) * LANE, 864))
            w_in_ref[part : part + 1, lanes] = whole_ref[part, 16 + row : 17 + row, 0 : lanes.stop - lanes.start]
        w_down_ref[:, part * LANE : (part + 1) * LANE] = whole_ref[part, 0:8, :]
        row_tile, lane_tile = divmod(part, 2)
        w_up_ref[8 * row_tile : 8 * row_tile + 8, lane_tile * LANE : (lane_tile + 1) * LANE] = whole_ref[
            part, 8:16, :
        ]
        w_depth_ref[part : part + 1, :] = whole_ref[part, 23:24, 0:49]
        lanes = slice(32 * part, 32 * (part + 1))
        w_out_ref[0:1, lanes] = whole_ref[part, 22:23, 96:128]
        w_out_ref[1:2, lanes] = whole_ref[part, 23:24, 64:96]
        w_out_ref[2:3, lanes] = whole_ref[part, 23:24, 96:128]
        b_up_ref[0:1, 4 * part : 4 * part + 4] = whole_ref[part, 23:24, 54:58]
    small = jnp.concatenate([whole_ref[part, 23:24, :] for part in range(parts)], axis=0)
    by_row = small.T
    for row, out_ref in enumerate((b_depth_ref, gain_ref, shift_ref, b_in_ref, b_down_ref), 49):
        out_ref[...] = by_row[row : row + 1, :]
    b_out_ref[...] = by_row[58:59, 0:3]


def call(kernel, outs, scratch, *operands, spaces=None, vmem=VMEM_BYTES, flops=0):
    kinds = {"v": pltpu.VMEM, "s": pltpu.SMEM, "a": pl.ANY}
    spaces = spaces or "v" * len(operands)
    return pl.pallas_call(
        kernel,
        out_shape=[jax.ShapeDtypeStruct(shape, kind) for shape, kind, _ in outs],
        in_specs=[pl.BlockSpec(memory_space=kinds[letter]) for letter in spaces],
        out_specs=[pl.BlockSpec(memory_space=kinds[letter]) for _, _, letter in outs],
        scratch_shapes=[x if not isinstance(x, tuple) else pltpu.VMEM(*x) for x in scratch],
        compiler_params=pltpu.CompilerParams(vmem_limit_bytes=vmem),
        cost_estimate=pl.CostEstimate(flops=flops, bytes_accessed=8_000_000, transcendentals=0),
    )(*operands)


def stack_vectors(b_in, b_depth, gain, shift, b_down, head_bias, b_up):
    rows = [b_in, b_depth, gain, shift, b_down, jnp.pad(head_bias, (0, 160)), b_up]
    return jnp.concatenate(rows).astype(F32).reshape(10, 256)


def run_forward(seam_turns, source, w_in, w_depth, vectors, w_up, w_down, head, members):
    return call(
        forward_kernel,
        [
            ((960, 1152), BF16, "a"),
            ((2, 30, 32, LANE), F32, "a"),
            ((CELLS, 256), F32, "a"),
            ((CELLS, LANE), F32, "a"),
            ((CELLS, 256), BF16, "a"),
            ((CELLS, 1024), BF16, "a"),
            ((CELLS, 1024), BF16, "a"),
            ((CELLS, 256), BF16, "v"),
            ((CELLS, 96), F32, "v"),
            ((144, 384), F32, "v"),
            ((members, 144, 384), BF16, "v"),
            ((49, 256), F32, "v"),
        ],
        [
            ((960, 1152), BF16),
            ((2, 30, 32, LANE), F32),
            ((CELLS, 1024), BF16),
            ((CELLS, 1024), BF16),
            ((CELLS, 256), F32),
            ((CELLS, LANE), F32),
            ((CELLS, 256), BF16),
            ((36, 40, LANE), F32),
            ((30, 32, LANE), F32),
            ((1152, 256), BF16),
            pltpu.SemaphoreType.DMA((5,)),
            pltpu.SemaphoreType.DMA((2, 6)),
        ],
        seam_turns,
        source,
        w_in,
        w_depth,
        vectors,
        w_up,
        w_down,
        head,
        spaces="svvvvvvv",
        flops=10_000_000_000,
    )


def run_mixer_backward(every, tight, target, saved, head, w_down, w_up, coefficient):
    hidden, active, slope, scaled = saved
    column = jnp.arange(96)
    owner = 3 * (column % 32) + column // 32
    pick = (jnp.arange(LANE)[:, None] == owner[None, :]).astype(BF16)
    return call(
        functools.partial(mixer_backward_kernel, coefficient),
        [
            ((8, 32, 16, LANE), BF16, "v"),
            ((96, 256), F32, "v"),
            ((CELLS, 256), F32, "a"),
            ((CELLS, 256), F32, "a"),
            ((8, 256), F32, "v"),
        ],
        [
            ((144, 384), F32),
            ((CELLS, LANE), F32),
            ((CELLS, 256), BF16),
            ((CELLS, 1024), BF16),
            ((8, 1024), F32),
            ((256, 1024), F32),
            ((CELLS, 1024), BF16),
            ((CELLS, 1024), BF16),
            ((1024, 256), BF16),
            ((256, 1024), BF16),
            ((CELLS, 256), F32),
            ((CELLS, 256), F32),
            pltpu.SemaphoreType.DMA((4,)),
            pltpu.SemaphoreType.DMA((2,)),
        ],
        every,
        tight,
        target,
        hidden,
        head,
        pick,
        active,
        slope,
        scaled,
        w_down,
        w_up,
        spaces="vvvvvvaavaa",
        flops=12_000_000_000,
    )


def run_depth_backward(
    scaled_grad, normed, inverse, vectors, hidden_grad, stem, w_depth, patches, early_small, out_part
):
    column = jnp.arange(256)
    order = (column[:, None] == (8 * (column % 32) + column // 32)[None, :]).astype(BF16)
    return call(
        depth_backward_kernel,
        [((256, 1152), BF16, "v")],
        [
            ((2, 36, 40, LANE), F32),
            ((2, 30, 32, LANE), F32),
            ((SMALL, 256), F32),
            ((3, 8, 256), F32),
            ((960, 256), BF16),
            ((256, 1152), F32),
            ((CELLS, 256), F32),
            ((2, 30, 32, LANE), F32),
            ((960, 1152), BF16),
            pltpu.SemaphoreType.DMA((3,)),
        ],
        scaled_grad,
        normed,
        inverse,
        vectors,
        hidden_grad,
        stem,
        w_depth,
        patches,
        order,
        early_small,
        out_part,
        spaces="vvvvaavavvv",
        flops=12_000_000_000,
    )[0]


def run_combine(early, late):
    return call(
        combine_kernel,
        [((32, 24, LANE), BF16, "v")],
        [((32, 24, LANE), F32)],
        early,
        late,
        vmem=SMALL_VMEM_BYTES,
    )[0]


def run_total(share, members):
    return call(total_kernel, [((members, 24, LANE), F32, "v")], [], share, vmem=SMALL_VMEM_BYTES)[0]


def run_unpack(whole):
    shapes = ((8, 864), (8, 49), (32, 256), (8, 1024), (3, 256), (1, 32)) + ((1, 8),) * 5 + ((1, 3),)
    return call(
        unpack_kernel, [(shape, F32, "v") for shape in shapes], [], whole, vmem=SMALL_VMEM_BYTES
    )


def shifted(value, axis, by):
    peers = lax.axis_size(axis)
    return lax.ppermute(value, axis, [(i, (i + by) % peers) for i in range(peers)])


def turned_edge(tile, turns, width, east):
    size = tile.shape[0]

    def columns(x):
        return x[:, size - width :] if east else x[:, :width]

    sides = (
        columns(tile),
        columns(jnp.rot90(tile, 1)),
        columns(jnp.rot90(tile, 2)),
        columns(jnp.rot90(tile, 3)),
    )
    result = sides[0]
    for quarter in range(1, 4):
        result = jnp.where(turns == quarter, sides[quarter], result)
    return result


def seam_pad(tile, my_turn, next_turn, margin, row_tiles):
    came_west = shifted(turned_edge(tile, next_turn, margin, True), "space", 1)
    came_east = shifted(turned_edge(tile, (4 - my_turn) % 4, margin, False), "space", -1)
    widened = jnp.concatenate([came_west, tile, came_east], axis=1)
    came_north = shifted(widened[-margin:], "space", row_tiles)
    came_south = shifted(widened[:margin], "space", -row_tiles)
    return jnp.concatenate([came_north, widened, came_south], axis=0)


def swap(value, axis):
    return lax.all_to_all(value, axis, 0, 0, tiled=True)


def body(
    initial_state,
    starting_field_nudges,
    verifying_analysis,
    seam_turns,
    w_in,
    b_in,
    w_depth,
    b_depth,
    norm_gain,
    norm_shift,
    w_up,
    b_up,
    w_down,
    b_down,
    head_weight,
    head_bias,
):
    spaces = lax.axis_size("space")
    members = lax.axis_size("ens")
    row_tiles = spaces // 4
    tile_index = lax.axis_index("space")

    def turn_at(offset):
        return lax.dynamic_index_in_dim(seam_turns, (tile_index + offset) % spaces, keepdims=False)

    my_turn = turn_at(0)
    next_turn = turn_at(1)
    source = (
        initial_state.astype(F32) + starting_field_nudges[0].astype(F32)
    ).astype(BF16).reshape(SIDE, SIDE, 96)
    near = seam_pad(source, my_turn, next_turn, 1, row_tiles)
    wide_source = seam_pad(near, my_turn, next_turn, 5, row_tiles)
    vectors = stack_vectors(b_in, b_depth, norm_gain, norm_shift, b_down, head_bias, b_up)
    head = head_weight.T
    saved = run_forward(seam_turns, wide_source, w_in, w_depth, vectors, w_up, w_down, head, members)
    patches, stem, normed, inverse, scaled, slope, active, hidden, field, tight, sent, w_depth_wide = saved
    sent, verifying_analysis, field_again = lax.optimization_barrier((sent, verifying_analysis, field))
    every = swap(sent, "ens")
    predicted = field_again.reshape(1, SIDE, SIDE * 96)
    target = verifying_analysis.reshape(4, 144, 96).transpose(1, 0, 2).reshape(144, 384)
    coefficient = 1.0 / math.sqrt(spaces * CELLS * 96)
    early, out_part, hidden_grad, scaled_grad, early_small = run_mixer_backward(
        every, tight, target, (hidden, active, slope, scaled), head, w_down, w_up, coefficient
    )
    late = run_depth_backward(
        scaled_grad, normed, inverse, vectors, hidden_grad, stem, w_depth_wide, patches, early_small, out_part
    )
    early_parts, late = lax.optimization_barrier((swap(early, "ens"), late))
    late_parts = swap(late.reshape(8, 32, 1152), "ens")
    shares = swap(run_combine(early_parts, late_parts), "space")
    whole = swap(run_total(shares, members), "ens")
    (
        grad_w_in, grad_w_depth, grad_w_up, grad_w_down, grad_w_out,
        grad_b_up, grad_b_depth, grad_gain, grad_shift, grad_b_in, grad_b_down, grad_b_out,
    ) = run_unpack(whole)
    return (
        predicted,
        grad_w_in.T,
        grad_b_in[0],
        grad_w_depth.T,
        grad_b_depth[0],
        grad_gain[0],
        grad_shift[0],
        grad_w_up.T,
        grad_b_up[0],
        grad_w_down.T,
        grad_b_down[0],
        grad_w_out.T,
        grad_b_out[0],
    )


def solution(mesh):
    return jax.shard_map(
        body,
        mesh=mesh,
        in_specs=(
            P("space", None),
            P("ens", "space", None),
            P("space", None),
            P(),
            P(),
            P(),
            P(),
            P(),
            P(),
            P(),
            P(),
            P(),
            P(),
            P(),
            P(),
            P(),
        ),
        out_specs=(
            P("ens", "space", None),
            P(None, "space"),
            P("space"),
            P(None, "space"),
            P("space"),
            P("space"),
            P("space"),
            P(None, "space"),
            P("space"),
            P(None, "space"),
            P("space"),
            P(None, "space"),
            P("space"),
        ),
        check_vma=False,
    )
```
